32 devices in a mesh: slab: 4 (over y, x), energy: 4 (over z), mom: 2 (over core).
Axes of the slice: x: 2, y: 2, z: 4, core: 2. Of those that a mesh axis runs over, the one named last changes fastest.
Arguments:
- onsite: float32 [2, 4, 256], P('mom', 'slab'), may hold values from -0.5 to 0.5
- hop: float32 [2, 4, 2, 256, 256], P('mom', 'slab'), may hold values from -0.0234375 to 0.0234375
- couple: float32 [2, 4, 2, 256, 256], P('mom', 'slab'), may hold values from -2 to 2
- sigma_in: float32 [8, 4, 2, 256, 256], P('energy', 'slab'), may hold values from -0.03125 to 0.03125
- shifts: int32 [4], replicated, may hold values from 1 to 7
- mode_weight: float32 [2, 4], replicated, may hold values from 0.2 to 1
Outputs:
- sigma_out: float32 [8, 4, 2, 256, 256], P(None, 'slab', None, 'energy')
The draws below stay inside these ranges and needn't reach their ends.
Inputs may be any that keep to these rules, and one draw needn't show every extreme that they name: `shifts`: energy-index offsets of the phonon modes.
All inputs are finite; a program needn't handle non-finite values.
Results may differ from the reference program's by a relative error of at most 0.00025.
Values sent between devices are 32-bit elements; how exact they have to be, the bound alone decides.
No kernel may reach another device: no remote copies, remote signals or barrier semaphores. Data moves between devices by JAX's collectives and lax.ppermute only.
A program may use at most 128 MiB of HBM per device.

```python
import math
import jax
import jax.numpy as jnp
from jax import lax

O = 256
NMODE = 4
NE = 8
NS = 4
NK = 2


def draw_couple(key, part):
    key_size = jax.random.fold_in(key, 11)
    key_phase = jax.random.fold_in(key, 12)
    key_noise = jax.random.fold_in(key, 13)
    magnitude = jnp.exp(jax.random.uniform(key_size, (NK, NS, O), jnp.float32, math.log(1.6), math.log(2.0)))
    phase = jax.random.uniform(key_phase, (NK, NS, O), jnp.float32, -math.pi, math.pi)
    noise = jnp.clip(jax.random.normal(key_noise, (NK, NS, 2, O, O), jnp.float32), -4.0, 4.0)
    noise = noise * (0.03 / math.sqrt(O))
    identity = jnp.eye(O, dtype=jnp.float32)
    outside = 1.0 - identity
    real_part = noise[:, :, 0] * outside + identity * (magnitude * jnp.cos(phase))[..., None, :]
    imag_part = noise[:, :, 1] * outside + identity * (magnitude * jnp.sin(phase))[..., None, :]
    return jnp.stack([real_part, imag_part], axis=2).astype(jnp.float32)


def touch_ends(array, key, least, high):
    longest = array.shape.index(max(array.shape))
    spots = []
    for shift in (0, 1):
        where = [jax.random.randint(jax.random.fold_in(key, axis), (), 0, length) for axis, length in enumerate(array.shape)]
        where[longest] = (where[longest] + shift) % array.shape[longest]
        spots.append(tuple(where))
    return array.at[spots[0]].set(least).at[spots[1]].set(high)


def block_scale(own_key, shape, pieces, least, top_value):
    gain, own = 1.0, jax.random.fold_in(own_key, 6)
    for position, shards_of in pieces:
        draws = jnp.exp(jax.random.uniform(jax.random.fold_in(own, position), (shards_of,), jnp.float32, least / len(pieces), top_value / len(pieces)))
        gain = gain * jnp.repeat(draws, shape[position] // shards_of).reshape([-1 if axis == position else 1 for axis in range(len(shape))])
    return gain


def normal_values(own_key, extent, width, reach, shards=(), kind=jnp.bfloat16):
    values = width * jax.random.normal(own_key, extent, jnp.float32)
    if shards:
        values = values * block_scale(own_key, extent, shards, -0.22, 0.18)
    return jnp.clip(values, -reach, reach).astype(kind)


def setup_inputs(seed: int = 0) -> dict:
    key_list = jax.random.split(jax.random.key(seed), 7)
    onsite = jnp.clip(jax.random.uniform(key_list[0], (NK, NS, O), jnp.float32, -0.5, 0.5) * block_scale(key_list[0], (NK, NS, O), ((0, 2), (1, 4)), -0.4, 0.0), -0.5, 0.5)
    hop = normal_values(key_list[1], (NK, NS, 2, O, O), (256 * O) ** -0.5, 0.0234375, ((0, 2), (1, 4)), jnp.float32)
    couple = draw_couple(jax.random.fold_in(key_list[6], 71), 0)
    sigma_in = normal_values(key_list[3], (NE, NS, 2, O, O), (128 * O) ** -0.5, 0.03125, ((0, 4), (1, 4)), jnp.float32)
    shifts = touch_ends(jax.random.randint(key_list[4], (NMODE,), 1, NE), jax.random.fold_in(key_list[4], 1), 1, NE - 1).astype(jnp.int32)
    mode_weight = jnp.clip(jnp.exp(jax.random.uniform(key_list[5], (2, NMODE), jnp.float32, math.log(0.2), math.log(1.0))), 0.2, 1.0)
    return dict(onsite=onsite, hop=hop, couple=couple, sigma_in=sigma_in, shifts=shifts, mode_weight=mode_weight)


ETA = 0.5
HIGH = lax.Precision.HIGHEST


def complex_mul(form, left, right):
    def product(first, second):
        return jnp.einsum(form, first, second, precision=HIGH)
    return (product(left[0], right[0]) - product(left[1], right[1]),
            product(left[0], right[1]) + product(left[1], right[0]))


def newton_inverse(mat_real, mat_imag, form, identity):
    diag_real = jnp.diagonal(mat_real, axis1=-2, axis2=-1)
    diag_imag = jnp.diagonal(mat_imag, axis1=-2, axis2=-1)
    denom = diag_real * diag_real + diag_imag * diag_imag
    x_real = diag_real / denom
    x_imag = -diag_imag / denom
    rows_real = x_real[..., :, None] * mat_real - x_imag[..., :, None] * mat_imag
    rows_imag = x_real[..., :, None] * mat_imag + x_imag[..., :, None] * mat_real
    both_real = rows_real * x_real[..., None, :] - rows_imag * x_imag[..., None, :]
    both_imag = rows_real * x_imag[..., None, :] + rows_imag * x_real[..., None, :]
    first = (2.0 * identity * x_real[..., None, :] - both_real, 2.0 * identity * x_imag[..., None, :] - both_imag)
    resid = complex_mul(form, (mat_real, mat_imag), first)
    second = complex_mul(form, first, resid)
    return (2.0 * first[0] - second[0], 2.0 * first[1] - second[1])


def phonon_matrix(shifts, mode_weight, count):
    rows = jnp.arange(count)[:, None, None]
    cols = jnp.arange(count)[None, :, None]
    offset = shifts[None, None, :]
    upper = (cols == rows + offset).astype(jnp.float32)
    lower = (cols == rows - offset).astype(jnp.float32)
    return jnp.sum(upper * mode_weight[0] + lower * mode_weight[1], axis=2)


def reference(onsite, hop, couple, sigma_in, shifts, mode_weight):
    identity = jnp.eye(O, dtype=jnp.float32)
    energy = -0.5 + (jnp.arange(NE).astype(jnp.float32) + 0.5) / NE
    greens = []
    previous = None
    for slab_no in range(NS):
        coupling = (couple[:, slab_no, 0], couple[:, slab_no, 1])
        adjoint = (jnp.swapaxes(coupling[0], -1, -2), -jnp.swapaxes(coupling[1], -1, -2))
        if previous is None:
            left_real = jnp.zeros((NK, NE, O, O), jnp.float32)
            left_imag = jnp.zeros((NK, NE, O, O), jnp.float32)
        else:
            temp = complex_mul('kij,kejl->keil', coupling, previous)
            left_real, left_imag = complex_mul('keij,kjl->keil', temp, adjoint)
        z_real = energy[None, :, None] - onsite[:, slab_no][:, None, :]
        mat_real = identity * z_real[..., None, :] - hop[:, slab_no, 0][:, None] - sigma_in[:, slab_no, 0][None] - left_real
        mat_imag = identity * ETA - hop[:, slab_no, 1][:, None] - sigma_in[:, slab_no, 1][None] - left_imag
        green = newton_inverse(mat_real, mat_imag, 'keij,kejl->keil', identity)
        greens.append(green)
        previous = green
    phonon = phonon_matrix(shifts, mode_weight, NE)
    outputs = [None] * NS
    coupled = None
    for slab_no in range(NS - 1, -1, -1):
        green = greens[slab_no]
        if coupled is None:
            full = green
        else:
            temp = complex_mul('keij,kejl->keil', green, coupled)
            extra = complex_mul('keij,kejl->keil', temp, green)
            full = (green[0] + extra[0], green[1] + extra[1])
        stacked = jnp.stack(full, axis=2)
        outputs[slab_no] = jnp.einsum('ef,kfsjl->esjl', phonon, stacked, precision=HIGH) / NK
        coupling = (couple[:, slab_no, 0], couple[:, slab_no, 1])
        adjoint = (jnp.swapaxes(coupling[0], -1, -2), -jnp.swapaxes(coupling[1], -1, -2))
        temp = complex_mul('kij,kejl->keil', adjoint, full)
        coupled = complex_mul('keij,kjl->keil', temp, coupling)
    return jnp.stack(outputs, axis=1)
```

```python
import functools

import jax
import jax.numpy as jnp
from jax import lax
from jax.experimental import pallas as pl
from jax.experimental.pallas import tpu as pltpu
from jax.sharding import PartitionSpec as P

ETA = 0.5
HIGH = lax.Precision.HIGHEST


def shifted(shard, axis, by):
    length = lax.axis_size(axis)
    pairs = [(i, i + by) for i in range(length) if 0 <= i + by < length]
    return lax.ppermute(shard, axis, pairs)


def complex_mul(form, left, right):

    def product(first, second):
        return jnp.einsum(form, first, second, precision=HIGH)

    return (
        product(left[0], right[0]) - product(left[1], right[1]),
        product(left[0], right[1]) + product(left[1], right[0]),
    )


def newton_inverse(mat_real, mat_imag, form, identity):
    diag_real = jnp.diagonal(mat_real, axis1=-2, axis2=-1)
    diag_imag = jnp.diagonal(mat_imag, axis1=-2, axis2=-1)
    denom = diag_real * diag_real + diag_imag * diag_imag
    x_real = diag_real / denom
    x_imag = -diag_imag / denom
    rows_real = x_real[..., :, None] * mat_real - x_imag[..., :, None] * mat_imag
    rows_imag = x_real[..., :, None] * mat_imag + x_imag[..., :, None] * mat_real
    both_real = rows_real * x_real[..., None, :] - rows_imag * x_imag[..., None, :]
    both_imag = rows_real * x_imag[..., None, :] + rows_imag * x_real[..., None, :]
    first = (
        2.0 * identity * x_real[..., None, :] - both_real,
        2.0 * identity * x_imag[..., None, :] - both_imag,
    )
    resid = complex_mul(form, (mat_real, mat_imag), first)
    second = complex_mul(form, first, resid)
    return (2.0 * first[0] - second[0], 2.0 * first[1] - second[1])


def phonon_matrix(shifts, mode_weight, count):
    rows = jnp.arange(count)[:, None, None]
    cols = jnp.arange(count)[None, :, None]
    offset = shifts[None, None, :]
    upper = (cols == rows + offset).astype(jnp.float32)
    lower = (cols == rows - offset).astype(jnp.float32)
    return jnp.sum(upper * mode_weight[0] + lower * mode_weight[1], axis=2)


def chain_body(onsite, hop, couple, sigma_in, shifts, mode_weight):
    e_local = sigma_in.shape[0]
    width = onsite.shape[-1]
    slab_count = lax.axis_size("slab")
    slab_index = lax.axis_index("slab")
    energy_count = lax.axis_size("energy")
    mom_count = lax.axis_size("mom")
    total = e_local * energy_count
    identity = jnp.eye(width, dtype=jnp.float32)
    global_index = lax.axis_index("energy") * e_local + jnp.arange(e_local)
    energy = -0.5 + (global_index.astype(jnp.float32) + 0.5) / total
    coupling = (couple[0, 0, 0], couple[0, 0, 1])
    adjoint = (coupling[0].T, -coupling[1].T)
    hopping = (hop[0, 0, 0], hop[0, 0, 1])
    level = onsite[0, 0]
    sigma = sigma_in[:, 0]

    def forward(received, energies, sig):
        temp = complex_mul("ij,ejl->eil", coupling, (received[:, 0], received[:, 1]))
        left = complex_mul("eij,jl->eil", temp, adjoint)
        z_real = energies[:, None] - level[None, :]
        mat_real = identity * z_real[:, None, :] - hopping[0] - sig[:, 0] - left[0]
        mat_imag = identity * ETA - hopping[1] - sig[:, 1] - left[1]
        green = newton_inverse(mat_real, mat_imag, "eij,ejl->eil", identity)
        return jnp.stack(green, axis=1)

    def backward(green, received):
        pair = (green[:, 0], green[:, 1])
        temp = complex_mul("eij,ejl->eil", pair, (received[:, 0], received[:, 1]))
        extra = complex_mul("eij,ejl->eil", temp, pair)
        full = (pair[0] + extra[0], pair[1] + extra[1])
        temp = complex_mul("ij,ejl->eil", adjoint, full)
        coupled = complex_mul("eij,jl->eil", temp, coupling)
        return (jnp.stack(full, axis=1), jnp.stack(coupled, axis=1))

    empty = jnp.zeros((e_local, 2, width, width), jnp.float32)

    def forward_step(step, green_all):
        received = shifted(green_all, "slab", 1)
        return lax.cond(
            slab_index == step, lambda: forward(received, energy, sigma), lambda: green_all
        )

    green_all = lax.fori_loop(0, slab_count, forward_step, empty)

    def backward_step(step, carry):
        received = shifted(carry[1], "slab", -1)
        return lax.cond(
            slab_index == slab_count - 1 - step,
            lambda: backward(green_all, received),
            lambda: carry,
        )

    full_all, coupled_all = lax.fori_loop(0, slab_count, backward_step, (empty, empty))
    phonon = phonon_matrix(shifts, mode_weight, total)
    blocks = full_all[:, None]
    mixed = jnp.einsum(
        "ef,fsrjl->esrjl",
        phonon,
        lax.all_to_all(blocks, "energy", split_axis=3, concat_axis=0, tiled=True),
        precision=HIGH,
    )
    result = lax.psum(mixed, "mom") / mom_count
    return result


VMEM_BYTES = 48 * 1024 * 1024


def halves(value):
    high = value.astype(jnp.bfloat16)
    low = (value - high.astype(jnp.float32)).astype(jnp.bfloat16)
    return high, low


def form(pair):
    return halves(pair[0]), halves(pair[1]), halves(pair[0] + pair[1])


def real_dot(left, right, flip):
    lhs = jnp.concatenate([left[0], left[1], left[0]], axis=1)
    axis = 1 if flip else 0
    rhs = jnp.concatenate([right[0], right[0], right[1]], axis=axis)
    return lax.dot_general(
        lhs, rhs, (((1,), (axis,)), ((), ())), preferred_element_type=jnp.float32
    )


def mul(left, right):
    first = real_dot(left[0], right[0], False)
    second = real_dot(left[1], right[1], False)
    third = real_dot(left[2], right[2], False)
    return first - second, third - first - second


def mul_adjoint(left, right, difference):
    first = real_dot(left[0], right[0], True)
    second = real_dot(left[1], right[1], True)
    third = real_dot(left[2], difference, True)
    return first + second, third - first + second


def adjoint_form(pair):
    real = pair[0].T
    imag = -pair[1].T
    return form((real, imag))


def add(left, right):
    return left[0] + right[0], left[1] + right[1]


def read(ref):
    return ref[0], ref[1]


def write(ref, pair):
    ref[0] = pair[0]
    ref[1] = pair[1]


def choose(cond, left, right):
    return jnp.where(cond, left[0], right[0]), jnp.where(cond, left[1], right[1])


def inverse(mat):
    width = mat[0].shape[0]
    eye = lax.broadcasted_iota(jnp.int32, (width, width), 0) == lax.broadcasted_iota(
        jnp.int32, (width, width), 1
    )
    on_r = jnp.where(eye, mat[0], 0.0)
    on_i = jnp.where(eye, mat[1], 0.0)
    row_r = jnp.sum(on_r, axis=0, keepdims=True)
    row_i = jnp.sum(on_i, axis=0, keepdims=True)
    col_r = jnp.sum(on_r, axis=1, keepdims=True)
    col_i = jnp.sum(on_i, axis=1, keepdims=True)

    def invert(real, imag):
        denom = real * real + imag * imag
        return real / denom, -imag / denom

    xr, xi = invert(row_r, row_i)
    yr, yi = invert(col_r, col_i)
    off_r = jnp.where(eye, 0.0, mat[0])
    off_i = jnp.where(eye, 0.0, mat[1])
    e_r = off_r * xr - off_i * xi
    e_i = off_r * xi + off_i * xr
    e_form = form((e_r, e_i))
    sq = mul(e_form, e_form)
    cube = mul(e_form, form(sq))
    t_r = jnp.where(eye, 1.0, 0.0) - e_r + sq[0] - cube[0]
    t_i = sq[1] - e_i - cube[1]
    return yr * t_r - yi * t_i, yr * t_i + yi * t_r


def pick_block(y, x, slab, own, x_side, y_side, far):
    same_y = y == slab // 2
    same_x = x == slab % 2
    near = choose(same_x, read(own), read(x_side))
    away = choose(same_x, read(y_side), read(far))
    return choose(same_y, near, away)


def left_term(coupling, green_form):
    c_form = form(coupling)
    inner = mul_adjoint(green_form, c_form, halves(coupling[0] - coupling[1]))
    return mul(c_form, form(inner))


def minus(left, right):
    return left[0] - right[0], left[1] - right[1]


def forward_kernel(
    place, b_own, b_x, b_y, b_far, c_own, c_x, c_third,
    g0_ref, g1_ref, p1_ref, q1_ref, k1_ref, g2_ref, p2_ref, q2_ref, k2_ref,
):
    y, x = place[0], place[1]
    blocks = (b_own, b_x, b_y, b_far)
    green = inverse(pick_block(y, x, 0, *blocks))
    write(g0_ref, green)
    couplings = (
        choose(y == 0, choose(x == 1, read(c_own), read(c_x)), read(c_third)),
        choose(y == 1, choose(x == 0, read(c_own), read(c_x)), read(c_third)),
    )
    outs = ((g1_ref, p1_ref, q1_ref, k1_ref), (g2_ref, p2_ref, q2_ref, k2_ref))
    for slab in (1, 2):
        coupling = couplings[slab - 1]
        mat = minus(pick_block(y, x, slab, *blocks), left_term(coupling, form(green)))
        green = inverse(mat)
        g_form = form(green)
        adjoint = adjoint_form(coupling)
        right = mul(g_form, form(coupling))
        g_ref, p_ref, q_ref, k_ref = outs[slab - 1]
        write(g_ref, green)
        write(p_ref, right)
        write(q_ref, mul(adjoint, g_form))
        write(k_ref, mul(adjoint, form(right)))


def upper_kernel(
    place, b_own, b_x, b_y, b_far, c_own, c_x, c_last, g2_ref, p2_ref, q2_ref, k2_ref,
    keep_ref, send_ref, y2_ref,
):
    y, x = place[0], place[1]
    coupling = choose(y == 0, read(c_last), choose(x == 1, read(c_own), read(c_x)))
    green2 = read(g2_ref)
    form2 = form(green2)
    mat = minus(pick_block(y, x, 3, b_own, b_x, b_y, b_far), left_term(coupling, form2))
    green3 = inverse(mat)
    inner = mul(form(green3), form(coupling))
    y3_form = form(mul(adjoint_form(coupling), form(inner)))
    y2 = add(read(k2_ref), mul(form(read(q2_ref)), form(mul(y3_form, form(read(p2_ref))))))
    write(y2_ref, y2)
    full2 = add(green2, mul(form2, form(mul(y3_form, form2))))
    write(keep_ref, choose(x == 0, full2, green3))
    write(send_ref, choose(x == 0, green3, full2))


def lower_kernel(place, y2_ref, g1_ref, p1_ref, q1_ref, k1_ref, g0_ref, keep_ref, send_ref):
    x = place[1]
    green1 = read(g1_ref)
    form1 = form(green1)
    y2_form = form(read(y2_ref))
    y1 = add(read(k1_ref), mul(form(read(q1_ref)), form(mul(y2_form, form(read(p1_ref))))))
    full1 = add(green1, mul(form1, form(mul(y2_form, form1))))
    green0 = read(g0_ref)
    form0 = form(green0)
    full0 = add(green0, mul(form0, form(mul(form(y1), form0))))
    write(keep_ref, choose(x == 0, full0, full1))
    write(send_ref, choose(x == 0, full1, full0))


def mix_kernel(weight, *refs):
    *parts, out_ref = refs
    rows = parts[0].shape[1]
    step = 8
    for part in range(2):
        for row in range(0, rows, step):
            values = [ref[part, row : row + step, :] for ref in parts]
            for energy in range(out_ref.shape[0]):
                total = weight[energy, 0] * values[0]
                for slot in range(1, len(values)):
                    total = total + weight[energy, slot] * values[slot]
                out_ref[energy, part, row : row + step, :] = total


def call(kernel, place, arrays, count, products):
    shape = jax.ShapeDtypeStruct(arrays[0].shape, jnp.float32)
    width = arrays[0].shape[-1]
    vmem = pl.BlockSpec(memory_space=pltpu.VMEM)
    return pl.pallas_call(
        kernel,
        out_shape=[shape] * count,
        in_specs=[pl.BlockSpec(memory_space=pltpu.SMEM)] + [vmem] * len(arrays),
        out_specs=[vmem] * count,
        compiler_params=pltpu.CompilerParams(vmem_limit_bytes=VMEM_BYTES),
        cost_estimate=pl.CostEstimate(
            flops=products * 9 * 2 * width**3,
            bytes_accessed=(len(arrays) + count) * 2 * width * width * 4,
            transcendentals=0,
        ),
    )(place, *arrays)


def owner_body(onsite, hop, couple, sigma_in, shifts, mode_weight):
    e_local = sigma_in.shape[0]
    width = onsite.shape[-1]
    energy_count = lax.axis_size("energy")
    mom_count = lax.axis_size("mom")
    total = e_local * energy_count
    axes = ("slab", "energy", "mom")
    slab = lax.axis_index("slab")
    z = lax.axis_index("energy")
    k = lax.axis_index("mom")
    y, x = slab // 2, slab % 2
    place = jnp.stack([y, x]).astype(jnp.int32)
    active = k == x

    def device(yy, xx, zz, kk):
        return ((2 * yy + xx) * energy_count + zz) * mom_count + kk

    chips = [(yy, xx, zz) for yy in range(2) for xx in range(2) for zz in range(energy_count)]
    x_feed = [(device(a, b, c, 1 - b), device(a, 1 - b, c, 1 - b)) for a, b, c in chips]
    x_feed_c = [(device(a, b, c, 1 - b), device(a, 1 - b, c, 1 - b)) for a, b, c in chips if a + b > 0]
    y_pass = [(device(a, b, c, b), device(1 - a, b, c, b)) for a, b, c in chips]
    y_down = [(device(a, b, c, b), device(1 - a, b, c, b)) for a, b, c in chips if a == 1]
    x_swap = [(device(a, b, c, b), device(a, 1 - b, c, 1 - b)) for a, b, c in chips]
    core = [(device(a, b, c, b), device(a, b, c, 1 - b)) for a, b, c in chips]

    def send(value, pairs):
        return lax.ppermute(value, axes, pairs)

    eye = jnp.eye(width, dtype=bool)

    def block(local):
        index = (z * e_local + local).astype(jnp.float32)
        energy = -0.5 + (index + 0.5) / total
        sigma = lax.dynamic_index_in_dim(sigma_in[:, 0], local, 0, keepdims=False)
        real = jnp.where(eye, (energy - onsite[0, 0])[None, :], 0.0) - hop[0, 0, 0] - sigma[0]
        imag = jnp.where(eye, ETA, 0.0) - hop[0, 0, 1] - sigma[1]
        return jnp.stack([real, imag])

    coupling = couple[0, 0]
    b_other = block(1 - y)
    b_own = block(y)
    b_far_sent = send(b_other, x_feed)
    b_y = send(b_other, y_pass)
    c_x = send(coupling, x_feed_c)
    b_far = send(b_far_sent, y_pass)
    b_x = send(b_own, x_feed)
    c_third = send(jnp.where(x != y, coupling, c_x), y_pass)
    c_last = send(jnp.where(x == 1, coupling, c_x), y_down)

    blocks = (b_own, b_x, b_y, b_far)
    g0, g1, p1, q1, k1, g2, p2, q2, k2 = call(
        forward_kernel, place, (*blocks, coupling, c_x, c_third), 9, 16
    )
    keep_up, send_up, y2 = call(
        upper_kernel, place, (*blocks, coupling, c_x, c_last, g2, p2, q2, k2), 3, 10
    )
    up = keep_up + send(send_up, x_swap)
    keep_low, send_low = call(lower_kernel, place, (y2, g1, p1, q1, k1, g0), 2, 6)
    low = keep_low + send(send_low, x_swap)

    sum_own = jnp.where(y == 0, low, up)
    sum_other = send(jnp.where(y == 0, up, low), y_pass)

    rows = width // energy_count
    phonon = phonon_matrix(shifts, mode_weight, total) / mom_count
    parts, columns = [], []
    for source, local in ((sum_own, y), (sum_other, 1 - y)):
        for flip in range(energy_count):
            peer = z ^ flip
            piece = lax.dynamic_slice_in_dim(source, peer * rows, rows, axis=1)
            if flip:
                pairs = [(device(a, b, c, b), device(a, b, c ^ flip, b)) for a, b, c in chips]
                piece = send(piece, pairs)
            parts.append(piece)
            columns.append(
                lax.dynamic_index_in_dim(phonon, peer * e_local + local, 1, keepdims=False)
            )
    weight = jnp.stack(columns, axis=1)
    vmem = pl.BlockSpec(memory_space=pltpu.VMEM)
    mixed = pl.pallas_call(
        mix_kernel,
        out_shape=jax.ShapeDtypeStruct((total, 2, rows, width), jnp.float32),
        in_specs=[pl.BlockSpec(memory_space=pltpu.SMEM)] + [vmem] * len(parts),
        out_specs=vmem,
        compiler_params=pltpu.CompilerParams(vmem_limit_bytes=VMEM_BYTES),
    )(weight, *parts)
    result = jnp.where(active, mixed, send(mixed, core))
    return result[:, None]


def solution(mesh):
    in_specs = (
        P("mom", "slab", None),
        P("mom", "slab", None, None, None),
        P("mom", "slab", None, None, None),
        P("energy", "slab", None, None, None),
        P(),
        P(),
    )
    out_specs = P(None, "slab", None, "energy", None)
    count = mesh.shape["energy"]

    def run(onsite, hop, couple, sigma_in, shifts, mode_weight):
        owned = (
            mesh.shape["slab"] == 4
            and mesh.shape["mom"] == 2
            and couple.shape[:2] == (2, 4)
            and sigma_in.shape[0] == 2 * count
            and count & (count - 1) == 0
        )
        inner = owner_body if owned else chain_body
        sharded = jax.shard_map(
            inner, mesh=mesh, in_specs=in_specs, out_specs=out_specs, check_vma=False
        )
        return sharded(onsite, hop, couple, sigma_in, shifts, mode_weight)

    return run
```

```python
import functools

import jax
import jax.numpy as jnp
from jax import lax
from jax.experimental import pallas as pl
from jax.experimental.pallas import tpu as pltpu
from jax.sharding import PartitionSpec as P

ETA = 0.5
HIGH = lax.Precision.HIGHEST


def shifted(shard, axis, by):
    length = lax.axis_size(axis)
    pairs = [(i, i + by) for i in range(length) if 0 <= i + by < length]
    return lax.ppermute(shard, axis, pairs)


def complex_mul(form, left, right):

    def product(first, second):
        return jnp.einsum(form, first, second, precision=HIGH)

    return (
        product(left[0], right[0]) - product(left[1], right[1]),
        product(left[0], right[1]) + product(left[1], right[0]),
    )


def newton_inverse(mat_real, mat_imag, form, identity):
    diag_real = jnp.diagonal(mat_real, axis1=-2, axis2=-1)
    diag_imag = jnp.diagonal(mat_imag, axis1=-2, axis2=-1)
    denom = diag_real * diag_real + diag_imag * diag_imag
    x_real = diag_real / denom
    x_imag = -diag_imag / denom
    rows_real = x_real[..., :, None] * mat_real - x_imag[..., :, None] * mat_imag
    rows_imag = x_real[..., :, None] * mat_imag + x_imag[..., :, None] * mat_real
    both_real = rows_real * x_real[..., None, :] - rows_imag * x_imag[..., None, :]
    both_imag = rows_real * x_imag[..., None, :] + rows_imag * x_real[..., None, :]
    first = (
        2.0 * identity * x_real[..., None, :] - both_real,
        2.0 * identity * x_imag[..., None, :] - both_imag,
    )
    resid = complex_mul(form, (mat_real, mat_imag), first)
    second = complex_mul(form, first, resid)
    return (2.0 * first[0] - second[0], 2.0 * first[1] - second[1])


def phonon_matrix(shifts, mode_weight, count):
    rows = jnp.arange(count)[:, None, None]
    cols = jnp.arange(count)[None, :, None]
    offset = shifts[None, None, :]
    upper = (cols == rows + offset).astype(jnp.float32)
    lower = (cols == rows - offset).astype(jnp.float32)
    return jnp.sum(upper * mode_weight[0] + lower * mode_weight[1], axis=2)


def chain_body(onsite, hop, couple, sigma_in, shifts, mode_weight):
    e_local = sigma_in.shape[0]
    width = onsite.shape[-1]
    slab_count = lax.axis_size("slab")
    slab_index = lax.axis_index("slab")
    energy_count = lax.axis_size("energy")
    mom_count = lax.axis_size("mom")
    total = e_local * energy_count
    identity = jnp.eye(width, dtype=jnp.float32)
    global_index = lax.axis_index("energy") * e_local + jnp.arange(e_local)
    energy = -0.5 + (global_index.astype(jnp.float32) + 0.5) / total
    coupling = (couple[0, 0, 0], couple[0, 0, 1])
    adjoint = (coupling[0].T, -coupling[1].T)
    hopping = (hop[0, 0, 0], hop[0, 0, 1])
    level = onsite[0, 0]
    sigma = sigma_in[:, 0]

    def forward(received, energies, sig):
        temp = complex_mul("ij,ejl->eil", coupling, (received[:, 0], received[:, 1]))
        left = complex_mul("eij,jl->eil", temp, adjoint)
        z_real = energies[:, None] - level[None, :]
        mat_real = identity * z_real[:, None, :] - hopping[0] - sig[:, 0] - left[0]
        mat_imag = identity * ETA - hopping[1] - sig[:, 1] - left[1]
        green = newton_inverse(mat_real, mat_imag, "eij,ejl->eil", identity)
        return jnp.stack(green, axis=1)

    def backward(green, received):
        pair = (green[:, 0], green[:, 1])
        temp = complex_mul("eij,ejl->eil", pair, (received[:, 0], received[:, 1]))
        extra = complex_mul("eij,ejl->eil", temp, pair)
        full = (pair[0] + extra[0], pair[1] + extra[1])
        temp = complex_mul("ij,ejl->eil", adjoint, full)
        coupled = complex_mul("eij,jl->eil", temp, coupling)
        return (jnp.stack(full, axis=1), jnp.stack(coupled, axis=1))

    empty = jnp.zeros((e_local, 2, width, width), jnp.float32)

    def forward_step(step, green_all):
        received = shifted(green_all, "slab", 1)
        return lax.cond(
            slab_index == step, lambda: forward(received, energy, sigma), lambda: green_all
        )

    green_all = lax.fori_loop(0, slab_count, forward_step, empty)

    def backward_step(step, carry):
        received = shifted(carry[1], "slab", -1)
        return lax.cond(
            slab_index == slab_count - 1 - step,
            lambda: backward(green_all, received),
            lambda: carry,
        )

    full_all, coupled_all = lax.fori_loop(0, slab_count, backward_step, (empty, empty))
    phonon = phonon_matrix(shifts, mode_weight, total)
    blocks = full_all[:, None]
    mixed = jnp.einsum(
        "ef,fsrjl->esrjl",
        phonon,
        lax.all_to_all(blocks, "energy", split_axis=3, concat_axis=0, tiled=True),
        precision=HIGH,
    )
    result = lax.psum(mixed, "mom") / mom_count
    return result


VMEM_BYTES = 24 * 1024 * 1024


def halves(value):
    high = value.astype(jnp.bfloat16)
    low = (value - high.astype(jnp.float32)).astype(jnp.bfloat16)
    return high, low


def form(pair):
    return halves(pair[0]), halves(pair[1])


def left_side(operand):
    (rh, rl), (ih, il) = operand
    return jnp.concatenate([rh, ih, rl, il, rh, ih], axis=1)


def mul(left, right):
    (rh, rl), (ih, il) = right
    high_r, low_r = jnp.concatenate([rh, -ih], axis=0), jnp.concatenate([rl, -il], axis=0)
    high_i, low_i = jnp.concatenate([ih, rh], axis=0), jnp.concatenate([il, rl], axis=0)
    rhs = jnp.concatenate(
        [
            jnp.concatenate([high_r, high_r, low_r], axis=0),
            jnp.concatenate([high_i, high_i, low_i], axis=0),
        ],
        axis=1,
    )
    out = jnp.dot(left_side(left), rhs, preferred_element_type=jnp.float32)
    width = rh.shape[0]
    return out[:, :width], out[:, width:]


def mul_adjoint(left, right):
    (rh, rl), (ih, il) = right
    rhs = jnp.concatenate(
        [
            jnp.concatenate([rh, ih, rh, ih, rl, il], axis=1),
            jnp.concatenate([-ih, rh, -ih, rh, -il, rl], axis=1),
        ],
        axis=0,
    )
    out = lax.dot_general(
        left_side(left), rhs, (((1,), (1,)), ((), ())), preferred_element_type=jnp.float32
    )
    width = rh.shape[0]
    return out[:, :width], out[:, width:]


def adjoint_form(pair):
    real = pair[0].T
    imag = -pair[1].T
    return form((real, imag))


def add(left, right):
    return left[0] + right[0], left[1] + right[1]


def read(ref):
    return ref[0], ref[1]


def write(ref, pair):
    ref[0] = pair[0]
    ref[1] = pair[1]


def choose(cond, left, right):
    return jnp.where(cond, left[0], right[0]), jnp.where(cond, left[1], right[1])


def inverse(mat):
    width = mat[0].shape[0]
    eye = lax.broadcasted_iota(jnp.int32, (width, width), 0) == lax.broadcasted_iota(
        jnp.int32, (width, width), 1
    )
    on_r = jnp.where(eye, mat[0], 0.0)
    on_i = jnp.where(eye, mat[1], 0.0)
    row_r = jnp.sum(on_r, axis=0, keepdims=True)
    row_i = jnp.sum(on_i, axis=0, keepdims=True)
    col_r = jnp.sum(on_r, axis=1, keepdims=True)
    col_i = jnp.sum(on_i, axis=1, keepdims=True)

    def invert(real, imag):
        denom = real * real + imag * imag
        return real / denom, -imag / denom

    xr, xi = invert(row_r, row_i)
    yr, yi = invert(col_r, col_i)
    off_r = jnp.where(eye, 0.0, mat[0])
    off_i = jnp.where(eye, 0.0, mat[1])
    e_r = off_r * xr - off_i * xi
    e_i = off_r * xi + off_i * xr
    e_form = form((e_r, e_i))
    sq = mul(e_form, e_form)
    cube = mul(e_form, form(sq))
    t_r = jnp.where(eye, 1.0, 0.0) - e_r + sq[0] - cube[0]
    t_i = sq[1] - e_i - cube[1]
    return yr * t_r - yi * t_i, yr * t_i + yi * t_r


def pick_block(y, x, slab, own, x_side, y_side, far):
    same_y = y == slab // 2
    same_x = x == slab % 2
    near = choose(same_x, read(own), read(x_side))
    away = choose(same_x, read(y_side), read(far))
    return choose(same_y, near, away)


def left_term(coupling, green_form):
    c_form = form(coupling)
    inner = mul_adjoint(green_form, c_form)
    return mul(c_form, form(inner))


def minus(left, right):
    return left[0] - right[0], left[1] - right[1]


def forward_kernel(
    place, b_own, b_x, b_y, b_far, c_own, c_x, c_third,
    g0_ref, g1_ref, p1_ref, q1_ref, k1_ref, g2_ref, p2_ref, q2_ref, k2_ref,
):
    y, x = place[0], place[1]
    blocks = (b_own, b_x, b_y, b_far)
    green = inverse(pick_block(y, x, 0, *blocks))
    write(g0_ref, green)
    couplings = (
        choose(y == 0, choose(x == 1, read(c_own), read(c_x)), read(c_third)),
        choose(y == 1, choose(x == 0, read(c_own), read(c_x)), read(c_third)),
    )
    outs = ((g1_ref, p1_ref, q1_ref, k1_ref), (g2_ref, p2_ref, q2_ref, k2_ref))
    for slab in (1, 2):
        coupling = couplings[slab - 1]
        mat = minus(pick_block(y, x, slab, *blocks), left_term(coupling, form(green)))
        green = inverse(mat)
        g_form = form(green)
        adjoint = adjoint_form(coupling)
        right = mul(g_form, form(coupling))
        g_ref, p_ref, q_ref, k_ref = outs[slab - 1]
        write(g_ref, green)
        write(p_ref, right)
        write(q_ref, mul(adjoint, g_form))
        write(k_ref, mul(adjoint, form(right)))


def upper_kernel(
    place, b_own, b_x, b_y, b_far, c_own, c_x, c_last, g2_ref, p2_ref, q2_ref, k2_ref,
    keep_ref, send_ref, y2_ref,
):
    y, x = place[0], place[1]
    coupling = choose(y == 0, read(c_last), choose(x == 1, read(c_own), read(c_x)))
    green2 = read(g2_ref)
    form2 = form(green2)
    mat = minus(pick_block(y, x, 3, b_own, b_x, b_y, b_far), left_term(coupling, form2))
    green3 = inverse(mat)
    inner = mul(form(green3), form(coupling))
    y3_form = form(mul(adjoint_form(coupling), form(inner)))
    y2 = add(read(k2_ref), mul(form(read(q2_ref)), form(mul(y3_form, form(read(p2_ref))))))
    write(y2_ref, y2)
    full2 = add(green2, mul(form2, form(mul(y3_form, form2))))
    write(keep_ref, choose(x == 0, full2, green3))
    write(send_ref, choose(x == 0, green3, full2))


def lower_kernel(place, y2_ref, g1_ref, p1_ref, q1_ref, k1_ref, g0_ref, keep_ref, send_ref):
    x = place[1]
    green1 = read(g1_ref)
    form1 = form(green1)
    y2_form = form(read(y2_ref))
    y1 = add(read(k1_ref), mul(form(read(q1_ref)), form(mul(y2_form, form(read(p1_ref))))))
    full1 = add(green1, mul(form1, form(mul(y2_form, form1))))
    green0 = read(g0_ref)
    form0 = form(green0)
    full0 = add(green0, mul(form0, form(mul(form(y1), form0))))
    write(keep_ref, choose(x == 0, full0, full1))
    write(send_ref, choose(x == 0, full1, full0))


def mix_kernel(place, weight, *refs):
    *parts, other_ref, out_ref = refs
    slots = len(parts) // 2
    rows = parts[0].shape[1]
    upper = place[0] == 1
    step = 8
    for part in range(2):
        for row in range(0, rows, step):
            here = (part, slice(row, row + step), slice(None))
            values = [jnp.where(upper, parts[i][here], parts[slots + i][here]) for i in range(slots)]
            values += [other_ref[(i, *here)] for i in range(slots)]
            for energy in range(out_ref.shape[0]):
                total = weight[energy, 0] * values[0]
                for slot in range(1, len(values)):
                    total = total + weight[energy, slot] * values[slot]
                out_ref[energy, part, row : row + step, :] = total


def prepare_kernel(place, scale, onsite_ref, hop_ref, sigma_ref, own_ref, other_ref):
    width = hop_ref.shape[-1]
    eye = lax.broadcasted_iota(jnp.int32, (width, width), 0) == lax.broadcasted_iota(
        jnp.int32, (width, width), 1
    )
    for ref, local, energy in ((other_ref, 1 - place[0], scale[1]), (own_ref, place[0], scale[0])):
        level = energy - onsite_ref[...]
        ref[0] = jnp.where(eye, level, 0.0) - hop_ref[0] - sigma_ref[local, 0]
        ref[1] = jnp.where(eye, ETA, 0.0) - hop_ref[1] - sigma_ref[local, 1]


def call(kernel, place, arrays, count, products):
    shape = jax.ShapeDtypeStruct(arrays[0].shape, jnp.float32)
    width = arrays[0].shape[-1]
    vmem = pl.BlockSpec(memory_space=pltpu.VMEM)
    return pl.pallas_call(
        kernel,
        out_shape=[shape] * count,
        in_specs=[pl.BlockSpec(memory_space=pltpu.SMEM)] + [vmem] * len(arrays),
        out_specs=[vmem] * count,
        compiler_params=pltpu.CompilerParams(vmem_limit_bytes=VMEM_BYTES),
        cost_estimate=pl.CostEstimate(
            flops=products * 9 * 2 * width**3,
            bytes_accessed=(len(arrays) + count) * 2 * width * width * 4,
            transcendentals=0,
        ),
    )(place, *arrays)


def owner_body(onsite, hop, couple, sigma_in, shifts, mode_weight):
    e_local = sigma_in.shape[0]
    width = onsite.shape[-1]
    energy_count = lax.axis_size("energy")
    mom_count = lax.axis_size("mom")
    total = e_local * energy_count
    axes = ("slab", "energy", "mom")
    slab = lax.axis_index("slab")
    z = lax.axis_index("energy")
    k = lax.axis_index("mom")
    y, x = slab // 2, slab % 2
    place = jnp.stack([y, x]).astype(jnp.int32)
    active = k == x

    def device(yy, xx, zz, kk):
        return ((2 * yy + xx) * energy_count + zz) * mom_count + kk

    chips = [(yy, xx, zz) for yy in range(2) for xx in range(2) for zz in range(energy_count)]
    x_feed = [(device(a, b, c, 1 - b), device(a, 1 - b, c, 1 - b)) for a, b, c in chips]
    x_feed_c = [(device(a, b, c, 1 - b), device(a, 1 - b, c, 1 - b)) for a, b, c in chips if a + b > 0]
    y_pass = [(device(a, b, c, b), device(1 - a, b, c, b)) for a, b, c in chips]
    y_down = [(device(a, b, c, b), device(1 - a, b, c, b)) for a, b, c in chips if a == 1]
    x_swap = [(device(a, b, c, b), device(a, 1 - b, c, 1 - b)) for a, b, c in chips]
    core = [(device(a, b, c, b), device(a, b, c, 1 - b)) for a, b, c in chips]

    def send(value, pairs):
        return lax.ppermute(value, axes, pairs)

    def after(value, earlier):
        return lax.optimization_barrier((value, earlier))[0]

    locals_ = jnp.stack([y, 1 - y])
    energies = -0.5 + ((z * e_local + locals_).astype(jnp.float32) + 0.5) / total
    smem = pl.BlockSpec(memory_space=pltpu.SMEM)
    vmem = pl.BlockSpec(memory_space=pltpu.VMEM)
    block_shape = jax.ShapeDtypeStruct((2, width, width), jnp.float32)
    b_own, b_other = pl.pallas_call(
        prepare_kernel,
        out_shape=[block_shape] * 2,
        in_specs=[smem, smem, vmem, vmem, vmem],
        out_specs=[vmem] * 2,
        compiler_params=pltpu.CompilerParams(vmem_limit_bytes=VMEM_BYTES),
    )(place, energies, onsite[0], hop[0, 0], sigma_in[:, 0])

    coupling = couple[0, 0]
    b_far_sent = send(b_other, x_feed)
    b_y = send(b_other, y_pass)
    c_x = send(after(coupling, b_far_sent), x_feed_c)
    b_far = send(after(b_far_sent, b_y), y_pass)
    b_x = send(after(b_own, c_x), x_feed)
    c_third = send(after(jnp.where(x != y, coupling, c_x), b_far), y_pass)
    c_last = send(after(jnp.where(x == 1, coupling, c_x), c_third), y_down)

    blocks = (b_own, b_x, b_y, b_far)
    g0, g1, p1, q1, k1, g2, p2, q2, k2 = call(
        forward_kernel, place, (*blocks, coupling, c_x, c_third), 9, 16
    )
    keep_up, send_up, y2 = call(
        upper_kernel, place, (*blocks, coupling, c_x, c_last, g2, p2, q2, k2), 3, 10
    )
    got_up = send(send_up, x_swap)
    keep_low, send_low = call(lower_kernel, place, (y2, g1, p1, q1, k1, g0), 2, 6)
    got_low = send(after(send_low, got_up), x_swap)

    rows = width // energy_count

    def over_planes(value):
        parts = []
        for flip in range(energy_count):
            piece = lax.dynamic_slice_in_dim(value, (z ^ flip) * rows, rows, axis=1)
            if flip:
                pairs = [(device(a, b, c, b), device(a, b, c ^ flip, b)) for a, b, c in chips]
                piece = send(piece, pairs)
            parts.append(piece)
        return parts

    up = over_planes(keep_up + got_up)
    low = over_planes(keep_low + got_low)
    other = send(jnp.where(y == 0, jnp.stack(up), jnp.stack(low)), y_pass)

    phonon = phonon_matrix(shifts, mode_weight, total) / mom_count
    columns = [
        lax.dynamic_index_in_dim(phonon, (z ^ flip) * e_local + local, 1, keepdims=False)
        for local in (y, 1 - y)
        for flip in range(energy_count)
    ]
    weight = jnp.stack(columns, axis=1)
    mixed = pl.pallas_call(
        mix_kernel,
        out_shape=jax.ShapeDtypeStruct((total, 2, rows, width), jnp.float32),
        in_specs=[smem, smem] + [vmem] * (2 * energy_count + 1),
        out_specs=vmem,
        compiler_params=pltpu.CompilerParams(vmem_limit_bytes=VMEM_BYTES),
    )(place, weight, *up, *low, other)
    result = jnp.where(active, mixed, send(mixed, core))
    return result[:, None]


def solution(mesh):
    in_specs = (
        P("mom", "slab", None),
        P("mom", "slab", None, None, None),
        P("mom", "slab", None, None, None),
        P("energy", "slab", None, None, None),
        P(),
        P(),
    )
    out_specs = P(None, "slab", None, "energy", None)
    count = mesh.shape["energy"]

    def run(onsite, hop, couple, sigma_in, shifts, mode_weight):
        owned = (
            mesh.shape["slab"] == 4
            and mesh.shape["mom"] == 2
            and couple.shape[:2] == (2, 4)
            and sigma_in.shape[0] == 2 * count
            and count & (count - 1) == 0
        )
        inner = owner_body if owned else chain_body
        sharded = jax.shard_map(
            inner, mesh=mesh, in_specs=in_specs, out_specs=out_specs, check_vma=False
        )
        return sharded(onsite, hop, couple, sigma_in, shifts, mode_weight)

    return run
```

```python
import functools

import jax
import jax.numpy as jnp
from jax import lax
from jax.experimental import pallas as pl
from jax.experimental.pallas import tpu as pltpu
from jax.sharding import PartitionSpec as P

ETA = 0.5
HIGH = lax.Precision.HIGHEST


def shifted(shard, axis, by):
    length = lax.axis_size(axis)
    pairs = [(i, i + by) for i in range(length) if 0 <= i + by < length]
    return lax.ppermute(shard, axis, pairs)


def complex_mul(form, left, right):

    def product(first, second):
        return jnp.einsum(form, first, second, precision=HIGH)

    return (
        product(left[0], right[0]) - product(left[1], right[1]),
        product(left[0], right[1]) + product(left[1], right[0]),
    )


def newton_inverse(mat_real, mat_imag, form, identity):
    diag_real = jnp.diagonal(mat_real, axis1=-2, axis2=-1)
    diag_imag = jnp.diagonal(mat_imag, axis1=-2, axis2=-1)
    denom = diag_real * diag_real + diag_imag * diag_imag
    x_real = diag_real / denom
    x_imag = -diag_imag / denom
    rows_real = x_real[..., :, None] * mat_real - x_imag[..., :, None] * mat_imag
    rows_imag = x_real[..., :, None] * mat_imag + x_imag[..., :, None] * mat_real
    both_real = rows_real * x_real[..., None, :] - rows_imag * x_imag[..., None, :]
    both_imag = rows_real * x_imag[..., None, :] + rows_imag * x_real[..., None, :]
    first = (
        2.0 * identity * x_real[..., None, :] - both_real,
        2.0 * identity * x_imag[..., None, :] - both_imag,
    )
    resid = complex_mul(form, (mat_real, mat_imag), first)
    second = complex_mul(form, first, resid)
    return (2.0 * first[0] - second[0], 2.0 * first[1] - second[1])


def phonon_matrix(shifts, mode_weight, count):
    rows = jnp.arange(count)[:, None, None]
    cols = jnp.arange(count)[None, :, None]
    offset = shifts[None, None, :]
    upper = (cols == rows + offset).astype(jnp.float32)
    lower = (cols == rows - offset).astype(jnp.float32)
    return jnp.sum(upper * mode_weight[0] + lower * mode_weight[1], axis=2)


def chain_body(onsite, hop, couple, sigma_in, shifts, mode_weight):
    e_local = sigma_in.shape[0]
    width = onsite.shape[-1]
    slab_count = lax.axis_size("slab")
    slab_index = lax.axis_index("slab")
    energy_count = lax.axis_size("energy")
    mom_count = lax.axis_size("mom")
    total = e_local * energy_count
    identity = jnp.eye(width, dtype=jnp.float32)
    global_index = lax.axis_index("energy") * e_local + jnp.arange(e_local)
    energy = -0.5 + (global_index.astype(jnp.float32) + 0.5) / total
    coupling = (couple[0, 0, 0], couple[0, 0, 1])
    adjoint = (coupling[0].T, -coupling[1].T)
    hopping = (hop[0, 0, 0], hop[0, 0, 1])
    level = onsite[0, 0]
    sigma = sigma_in[:, 0]

    def forward(received, energies, sig):
        temp = complex_mul("ij,ejl->eil", coupling, (received[:, 0], received[:, 1]))
        left = complex_mul("eij,jl->eil", temp, adjoint)
        z_real = energies[:, None] - level[None, :]
        mat_real = identity * z_real[:, None, :] - hopping[0] - sig[:, 0] - left[0]
        mat_imag = identity * ETA - hopping[1] - sig[:, 1] - left[1]
        green = newton_inverse(mat_real, mat_imag, "eij,ejl->eil", identity)
        return jnp.stack(green, axis=1)

    def backward(green, received):
        pair = (green[:, 0], green[:, 1])
        temp = complex_mul("eij,ejl->eil", pair, (received[:, 0], received[:, 1]))
        extra = complex_mul("eij,ejl->eil", temp, pair)
        full = (pair[0] + extra[0], pair[1] + extra[1])
        temp = complex_mul("ij,ejl->eil", adjoint, full)
        coupled = complex_mul("eij,jl->eil", temp, coupling)
        return (jnp.stack(full, axis=1), jnp.stack(coupled, axis=1))

    empty = jnp.zeros((e_local, 2, width, width), jnp.float32)

    def forward_step(step, green_all):
        received = shifted(green_all, "slab", 1)
        return lax.cond(
            slab_index == step, lambda: forward(received, energy, sigma), lambda: green_all
        )

    green_all = lax.fori_loop(0, slab_count, forward_step, empty)

    def backward_step(step, carry):
        received = shifted(carry[1], "slab", -1)
        return lax.cond(
            slab_index == slab_count - 1 - step,
            lambda: backward(green_all, received),
            lambda: carry,
        )

    full_all, coupled_all = lax.fori_loop(0, slab_count, backward_step, (empty, empty))
    phonon = phonon_matrix(shifts, mode_weight, total)
    blocks = full_all[:, None]
    mixed = jnp.einsum(
        "ef,fsrjl->esrjl",
        phonon,
        lax.all_to_all(blocks, "energy", split_axis=3, concat_axis=0, tiled=True),
        precision=HIGH,
    )
    result = lax.psum(mixed, "mom") / mom_count
    return result


VMEM_BYTES = 24 * 1024 * 1024


def halves(value):
    high = value.astype(jnp.bfloat16)
    low = (value - high.astype(jnp.float32)).astype(jnp.bfloat16)
    return high, low


def form(pair):
    return halves(pair[0]), halves(pair[1])


def three_terms(left, high, low, axis):
    (rh, rl), (ih, il) = left
    top = jnp.concatenate([rh, ih], axis=1)
    both = jnp.concatenate([top, jnp.concatenate([rl, il], axis=1)], axis=0)
    numbers = (((1,), (axis,)), ((), ()))
    main = lax.dot_general(both, high, numbers, preferred_element_type=jnp.float32)
    rest = lax.dot_general(top, low, numbers, preferred_element_type=jnp.float32)
    width = rh.shape[0]
    out = main[:width] + main[width:] + rest
    return out[:, :width], out[:, width:]


def mul(left, right):
    (rh, rl), (ih, il) = right

    def grid(real, imag):
        return jnp.concatenate(
            [jnp.concatenate([real, imag], axis=1), jnp.concatenate([-imag, real], axis=1)], axis=0
        )

    return three_terms(left, grid(rh, ih), grid(rl, il), 0)


def mul_adjoint(left, right):
    (rh, rl), (ih, il) = right

    def grid(real, imag):
        return jnp.concatenate(
            [jnp.concatenate([real, imag], axis=1), jnp.concatenate([-imag, real], axis=1)], axis=0
        )

    return three_terms(left, grid(rh, ih), grid(rl, il), 1)


def adjoint_form(pair):
    real = pair[0].T
    imag = -pair[1].T
    return form((real, imag))


def add(left, right):
    return left[0] + right[0], left[1] + right[1]


def read(ref):
    return ref[0], ref[1]


def write(ref, pair):
    ref[0] = pair[0]
    ref[1] = pair[1]


def choose(cond, left, right):
    return jnp.where(cond, left[0], right[0]), jnp.where(cond, left[1], right[1])


def inverse(mat):
    width = mat[0].shape[0]
    eye = lax.broadcasted_iota(jnp.int32, (width, width), 0) == lax.broadcasted_iota(
        jnp.int32, (width, width), 1
    )
    on_r = jnp.where(eye, mat[0], 0.0)
    on_i = jnp.where(eye, mat[1], 0.0)
    row_r = jnp.sum(on_r, axis=0, keepdims=True)
    row_i = jnp.sum(on_i, axis=0, keepdims=True)
    col_r = jnp.sum(on_r, axis=1, keepdims=True)
    col_i = jnp.sum(on_i, axis=1, keepdims=True)

    def invert(real, imag):
        denom = real * real + imag * imag
        return real / denom, -imag / denom

    xr, xi = invert(row_r, row_i)
    yr, yi = invert(col_r, col_i)
    off_r = jnp.where(eye, 0.0, mat[0])
    off_i = jnp.where(eye, 0.0, mat[1])
    e_r = off_r * xr - off_i * xi
    e_i = off_r * xi + off_i * xr
    e_form = form((e_r, e_i))
    sq = mul(e_form, e_form)
    cube = mul(e_form, form(sq))
    t_r = jnp.where(eye, 1.0, 0.0) - e_r + sq[0] - cube[0]
    t_i = sq[1] - e_i - cube[1]
    return yr * t_r - yi * t_i, yr * t_i + yi * t_r


def pick_block(y, x, slab, own, x_side, y_side, far):
    same_y = y == slab // 2
    same_x = x == slab % 2
    near = choose(same_x, read(own), read(x_side))
    away = choose(same_x, read(y_side), read(far))
    return choose(same_y, near, away)


def left_term(coupling, green_form):
    c_form = form(coupling)
    inner = mul_adjoint(green_form, c_form)
    return mul(c_form, form(inner))


def minus(left, right):
    return left[0] - right[0], left[1] - right[1]


def forward_kernel(
    place, b_own, b_x, b_y, b_far, c_own, c_x, c_third,
    g0_ref, g1_ref, p1_ref, q1_ref, k1_ref, g2_ref, p2_ref, q2_ref, k2_ref,
):
    y, x = place[0], place[1]
    blocks = (b_own, b_x, b_y, b_far)
    green = inverse(pick_block(y, x, 0, *blocks))
    write(g0_ref, green)
    couplings = (
        choose(y == 0, choose(x == 1, read(c_own), read(c_x)), read(c_third)),
        choose(y == 1, choose(x == 0, read(c_own), read(c_x)), read(c_third)),
    )
    outs = ((g1_ref, p1_ref, q1_ref, k1_ref), (g2_ref, p2_ref, q2_ref, k2_ref))
    for slab in (1, 2):
        coupling = couplings[slab - 1]
        mat = minus(pick_block(y, x, slab, *blocks), left_term(coupling, form(green)))
        green = inverse(mat)
        g_form = form(green)
        adjoint = adjoint_form(coupling)
        right = mul(g_form, form(coupling))
        g_ref, p_ref, q_ref, k_ref = outs[slab - 1]
        write(g_ref, green)
        write(p_ref, right)
        write(q_ref, mul(adjoint, g_form))
        write(k_ref, mul(adjoint, form(right)))


def backward_kernel(
    place, b_own, b_x, b_y, b_far, c_own, c_x, c_last,
    g0_ref, g1_ref, p1_ref, q1_ref, k1_ref, g2_ref, p2_ref, q2_ref, k2_ref,
    keep_ref, give_ref,
):
    y, x = place[0], place[1]

    def finish(slab, full):
        keep_ref[slab] = jnp.where(x == 0, full[0], full[1])
        give_ref[slab] = jnp.where(x == 0, full[1], full[0])

    coupling = choose(y == 0, read(c_last), choose(x == 1, read(c_own), read(c_x)))
    green2 = read(g2_ref)
    form2 = form(green2)
    mat = minus(pick_block(y, x, 3, b_own, b_x, b_y, b_far), left_term(coupling, form2))
    green3 = inverse(mat)
    finish(3, green3)
    inner = mul(form(green3), form(coupling))
    y3_form = form(mul(adjoint_form(coupling), form(inner)))
    y2 = add(read(k2_ref), mul(form(read(q2_ref)), form(mul(y3_form, form(read(p2_ref))))))
    finish(2, add(green2, mul(form2, form(mul(y3_form, form2)))))
    green1 = read(g1_ref)
    form1 = form(green1)
    y2_form = form(y2)
    y1 = add(read(k1_ref), mul(form(read(q1_ref)), form(mul(y2_form, form(read(p1_ref))))))
    finish(1, add(green1, mul(form1, form(mul(y2_form, form1)))))
    green0 = read(g0_ref)
    form0 = form(green0)
    finish(0, add(green0, mul(form0, form(mul(form(y1), form0)))))


def mix_kernel(phonon, parts_ref, out_ref):
    slots, rows, _ = parts_ref.shape
    energies = out_ref.shape[0]
    planes, step = slots // 4, 8

    def source(slot):
        return 2 * (slot % planes) + slot // planes // 2

    for row in range(0, rows, step):
        here = slice(row, row + step)
        values = [None] * energies
        for slot in range(slots):
            value = parts_ref[slot, here, :]
            held = values[source(slot)]
            values[source(slot)] = value if held is None else held + value
        for energy in range(energies):
            total = phonon[energy, 0] * values[0]
            for other in range(1, energies):
                total = total + phonon[energy, other] * values[other]
            out_ref[energy, here, :] = total


def prepare_kernel(place, scale, onsite_ref, hop_ref, sigma_ref, own_ref, other_ref):
    width = hop_ref.shape[-1]
    eye = lax.broadcasted_iota(jnp.int32, (width, width), 0) == lax.broadcasted_iota(
        jnp.int32, (width, width), 1
    )
    for ref, local, energy in ((other_ref, 1 - place[0], scale[1]), (own_ref, place[0], scale[0])):
        level = energy - onsite_ref[...]
        ref[0] = jnp.where(eye, level, 0.0) - hop_ref[0] - sigma_ref[local, 0]
        ref[1] = jnp.where(eye, ETA, 0.0) - hop_ref[1] - sigma_ref[local, 1]


def call(kernel, place, arrays, shape, count, products):
    width = arrays[0].shape[-1]
    vmem = pl.BlockSpec(memory_space=pltpu.VMEM)
    return pl.pallas_call(
        kernel,
        out_shape=[jax.ShapeDtypeStruct(shape, jnp.float32)] * count,
        in_specs=[pl.BlockSpec(memory_space=pltpu.SMEM)] + [vmem] * len(arrays),
        out_specs=[vmem] * count,
        compiler_params=pltpu.CompilerParams(vmem_limit_bytes=VMEM_BYTES),
        cost_estimate=pl.CostEstimate(
            flops=products * 9 * 2 * width**3,
            bytes_accessed=(len(arrays) + count) * 2 * width * width * 4,
            transcendentals=0,
        ),
    )(place, *arrays)


def owner_body(onsite, hop, couple, sigma_in, shifts, mode_weight):
    e_local = sigma_in.shape[0]
    width = onsite.shape[-1]
    energy_count = lax.axis_size("energy")
    mom_count = lax.axis_size("mom")
    total = e_local * energy_count
    axes = ("slab", "energy", "mom")
    slab = lax.axis_index("slab")
    z = lax.axis_index("energy")
    k = lax.axis_index("mom")
    y, x = slab // 2, slab % 2
    place = jnp.stack([y, x]).astype(jnp.int32)
    active = k == x

    def device(yy, xx, zz, kk):
        return ((2 * yy + xx) * energy_count + zz) * mom_count + kk

    chips = [(yy, xx, zz) for yy in range(2) for xx in range(2) for zz in range(energy_count)]
    x_feed = [(device(a, b, c, 1 - b), device(a, 1 - b, c, 1 - b)) for a, b, c in chips]
    x_feed_c = [(device(a, b, c, 1 - b), device(a, 1 - b, c, 1 - b)) for a, b, c in chips if a + b > 0]
    y_pass = [(device(a, b, c, b), device(1 - a, b, c, b)) for a, b, c in chips]
    y_down = [(device(a, b, c, b), device(1 - a, b, c, b)) for a, b, c in chips if a == 1]
    siblings = [(device(a, b, c, d), device(a, b, c, 1 - d)) for a, b, c in chips for d in range(2)]
    gift = [(device(a, b, c, b), device(a, b, c, 1 - b)) for a, b, c in chips]

    def send(value, pairs):
        return lax.ppermute(value, axes, pairs)

    def after(value, earlier):
        return lax.optimization_barrier((value, earlier))[0]

    locals_ = jnp.stack([y, 1 - y])
    energies = -0.5 + ((z * e_local + locals_).astype(jnp.float32) + 0.5) / total
    smem = pl.BlockSpec(memory_space=pltpu.SMEM)
    vmem = pl.BlockSpec(memory_space=pltpu.VMEM)
    block_shape = jax.ShapeDtypeStruct((2, width, width), jnp.float32)
    b_own, b_other = pl.pallas_call(
        prepare_kernel,
        out_shape=[block_shape] * 2,
        in_specs=[smem, smem, vmem, vmem, vmem],
        out_specs=[vmem] * 2,
        compiler_params=pltpu.CompilerParams(vmem_limit_bytes=VMEM_BYTES),
    )(place, energies, onsite[0], hop[0, 0], sigma_in[:, 0])

    coupling = couple[0, 0]
    b_far_sent = send(b_other, x_feed)
    c_x = send(coupling, x_feed_c)
    b_y = send(b_other, y_pass)
    b_x = send(after(b_own, c_x), x_feed)
    b_far = send(after(b_far_sent, b_y), y_pass)
    c_third = send(jnp.where(x != y, coupling, c_x), y_pass)
    c_last = send(after(jnp.where(x == 1, coupling, c_x), c_third), y_down)

    blocks = (b_own, b_x, b_y, b_far)
    shape = (2, width, width)
    chain = call(forward_kernel, place, (*blocks, coupling, c_x, c_third), shape, 9, 16)
    shape = (4, width, width)
    keep, give = call(
        backward_kernel, place, (*blocks, coupling, c_x, c_last, *chain), shape, 2, 16
    )
    half = jnp.where(active, keep, send(give, gift))

    rows = width // energy_count
    slots = 4 * energy_count
    parts = lax.all_to_all(
        half.reshape(slots, rows, width), ("slab", "energy"), 0, 0, tiled=True
    )
    phonon = phonon_matrix(shifts, mode_weight, total) / mom_count
    mixed = pl.pallas_call(
        mix_kernel,
        out_shape=jax.ShapeDtypeStruct((total, rows, width), jnp.float32),
        in_specs=[smem, vmem],
        out_specs=vmem,
        compiler_params=pltpu.CompilerParams(vmem_limit_bytes=VMEM_BYTES),
    )(phonon, parts)
    other = send(mixed, siblings)
    mine = jnp.arange(2)[:, None, None] == k
    result = jnp.where(mine, mixed[:, None], other[:, None])
    return result[:, None]


def solution(mesh):
    in_specs = (
        P("mom", "slab", None),
        P("mom", "slab", None, None, None),
        P("mom", "slab", None, None, None),
        P("energy", "slab", None, None, None),
        P(),
        P(),
    )
    out_specs = P(None, "slab", None, "energy", None)
    count = mesh.shape["energy"]

    def run(onsite, hop, couple, sigma_in, shifts, mode_weight):
        owned = (
            mesh.shape["slab"] == 4
            and mesh.shape["mom"] == 2
            and couple.shape[:2] == (2, 4)
            and sigma_in.shape[0] == 2 * count
            and count & (count - 1) == 0
        )
        inner = owner_body if owned else chain_body
        sharded = jax.shard_map(
            inner, mesh=mesh, in_specs=in_specs, out_specs=out_specs, check_vma=False
        )
        return sharded(onsite, hop, couple, sigma_in, shifts, mode_weight)

    return run
```

```python
import functools

import jax
import jax.numpy as jnp
from jax import lax
from jax.experimental import pallas as pl
from jax.experimental.pallas import tpu as pltpu
from jax.sharding import PartitionSpec as P

ETA = 0.5
HIGH = lax.Precision.HIGHEST


def shifted(shard, axis, by):
    length = lax.axis_size(axis)
    pairs = [(i, i + by) for i in range(length) if 0 <= i + by < length]
    return lax.ppermute(shard, axis, pairs)


def complex_mul(form, left, right):

    def product(first, second):
        return jnp.einsum(form, first, second, precision=HIGH)

    return (
        product(left[0], right[0]) - product(left[1], right[1]),
        product(left[0], right[1]) + product(left[1], right[0]),
    )


def newton_inverse(mat_real, mat_imag, form, identity):
    diag_real = jnp.diagonal(mat_real, axis1=-2, axis2=-1)
    diag_imag = jnp.diagonal(mat_imag, axis1=-2, axis2=-1)
    denom = diag_real * diag_real + diag_imag * diag_imag
    x_real = diag_real / denom
    x_imag = -diag_imag / denom
    rows_real = x_real[..., :, None] * mat_real - x_imag[..., :, None] * mat_imag
    rows_imag = x_real[..., :, None] * mat_imag + x_imag[..., :, None] * mat_real
    both_real = rows_real * x_real[..., None, :] - rows_imag * x_imag[..., None, :]
    both_imag = rows_real * x_imag[..., None, :] + rows_imag * x_real[..., None, :]
    first = (
        2.0 * identity * x_real[..., None, :] - both_real,
        2.0 * identity * x_imag[..., None, :] - both_imag,
    )
    resid = complex_mul(form, (mat_real, mat_imag), first)
    second = complex_mul(form, first, resid)
    return (2.0 * first[0] - second[0], 2.0 * first[1] - second[1])


def phonon_matrix(shifts, mode_weight, count):
    rows = jnp.arange(count)[:, None, None]
    cols = jnp.arange(count)[None, :, None]
    offset = shifts[None, None, :]
    upper = (cols == rows + offset).astype(jnp.float32)
    lower = (cols == rows - offset).astype(jnp.float32)
    return jnp.sum(upper * mode_weight[0] + lower * mode_weight[1], axis=2)


def chain_body(onsite, hop, couple, sigma_in, shifts, mode_weight):
    e_local = sigma_in.shape[0]
    width = onsite.shape[-1]
    slab_count = lax.axis_size("slab")
    slab_index = lax.axis_index("slab")
    energy_count = lax.axis_size("energy")
    mom_count = lax.axis_size("mom")
    total = e_local * energy_count
    identity = jnp.eye(width, dtype=jnp.float32)
    global_index = lax.axis_index("energy") * e_local + jnp.arange(e_local)
    energy = -0.5 + (global_index.astype(jnp.float32) + 0.5) / total
    coupling = (couple[0, 0, 0], couple[0, 0, 1])
    adjoint = (coupling[0].T, -coupling[1].T)
    hopping = (hop[0, 0, 0], hop[0, 0, 1])
    level = onsite[0, 0]
    sigma = sigma_in[:, 0]

    def forward(received, energies, sig):
        temp = complex_mul("ij,ejl->eil", coupling, (received[:, 0], received[:, 1]))
        left = complex_mul("eij,jl->eil", temp, adjoint)
        z_real = energies[:, None] - level[None, :]
        mat_real = identity * z_real[:, None, :] - hopping[0] - sig[:, 0] - left[0]
        mat_imag = identity * ETA - hopping[1] - sig[:, 1] - left[1]
        green = newton_inverse(mat_real, mat_imag, "eij,ejl->eil", identity)
        return jnp.stack(green, axis=1)

    def backward(green, received):
        pair = (green[:, 0], green[:, 1])
        temp = complex_mul("eij,ejl->eil", pair, (received[:, 0], received[:, 1]))
        extra = complex_mul("eij,ejl->eil", temp, pair)
        full = (pair[0] + extra[0], pair[1] + extra[1])
        temp = complex_mul("ij,ejl->eil", adjoint, full)
        coupled = complex_mul("eij,jl->eil", temp, coupling)
        return (jnp.stack(full, axis=1), jnp.stack(coupled, axis=1))

    empty = jnp.zeros((e_local, 2, width, width), jnp.float32)

    def forward_step(step, green_all):
        received = shifted(green_all, "slab", 1)
        return lax.cond(
            slab_index == step, lambda: forward(received, energy, sigma), lambda: green_all
        )

    green_all = lax.fori_loop(0, slab_count, forward_step, empty)

    def backward_step(step, carry):
        received = shifted(carry[1], "slab", -1)
        return lax.cond(
            slab_index == slab_count - 1 - step,
            lambda: backward(green_all, received),
            lambda: carry,
        )

    full_all, coupled_all = lax.fori_loop(0, slab_count, backward_step, (empty, empty))
    phonon = phonon_matrix(shifts, mode_weight, total)
    blocks = full_all[:, None]
    mixed = jnp.einsum(
        "ef,fsrjl->esrjl",
        phonon,
        lax.all_to_all(blocks, "energy", split_axis=3, concat_axis=0, tiled=True),
        precision=HIGH,
    )
    result = lax.psum(mixed, "mom") / mom_count
    return result


VMEM_BYTES = 24 * 1024 * 1024


BLOCKS = 2


def halves(value):
    high = value.astype(jnp.bfloat16)
    low = (value - high.astype(jnp.float32)).astype(jnp.bfloat16)
    return high, low


def form(pair):
    return halves(pair[0]), halves(pair[1]), halves(pair[0] + pair[1])


def adjoint_form(pair):
    return halves(pair[0]), halves(-pair[1]), halves(pair[0] - pair[1])


def real_dot(left, right, axis):
    rows = left[0].shape[0]
    numbers = (((1,), (axis,)), ((), ()))
    both = jnp.concatenate([left[0], left[1]], axis=0)
    main = lax.dot_general(both, right[0], numbers, preferred_element_type=jnp.float32)
    rest = lax.dot_general(left[0], right[1], numbers, preferred_element_type=jnp.float32)
    return main[:rows] + main[rows:] + rest


def mul(left, right, axis=0):
    first = real_dot(left[0], right[0], axis)
    second = real_dot(left[1], right[1], axis)
    third = real_dot(left[2], right[2], axis)
    return first - second, third - first - second


def mul_twice(blocks, right, last, axis=0):
    inner = [mul(block, right) for block in blocks]
    return [mul(form(block), last, axis) for block in inner]


def split_rows(pair):
    size = pair[0].shape[0] // BLOCKS
    return [tuple(part[b * size : (b + 1) * size] for part in pair) for b in range(BLOCKS)]


def join_rows(blocks):
    return tuple(jnp.concatenate([block[i] for block in blocks], axis=0) for i in range(2))


def form_rows(forms):
    return tuple(
        tuple(jnp.concatenate([f[plane][term] for f in forms], axis=0) for term in range(2))
        for plane in range(3)
    )


def read(ref):
    return ref[0], ref[1]


def write(ref, blocks):
    size = blocks[0][0].shape[0]
    for b, block in enumerate(blocks):
        ref[0, b * size : (b + 1) * size] = block[0]
        ref[1, b * size : (b + 1) * size] = block[1]


def choose(cond, left, right):
    return jnp.where(cond, left[0], right[0]), jnp.where(cond, left[1], right[1])


def times(left, right):
    return left[0] * right[0] - left[1] * right[1], left[0] * right[1] + left[1] * right[0]


def inverse(mats):
    size, width = mats[0][0].shape

    def invert(real, imag):
        denom = real * real + imag * imag
        return real / denom, -imag / denom

    eyes, scaled = [], []
    across = (0.0, 0.0)
    for b, mat in enumerate(mats):
        eye = lax.broadcasted_iota(jnp.int32, (size, width), 0) + b * size == (
            lax.broadcasted_iota(jnp.int32, (size, width), 1)
        )
        on = [jnp.where(eye, part, 0.0) for part in mat]
        off = [jnp.where(eye, 0.0, part) for part in mat]
        across = tuple(
            total + jnp.sum(part, axis=0, keepdims=True) for total, part in zip(across, on)
        )
        down = invert(*(jnp.sum(part, axis=1, keepdims=True) for part in on))
        eyes.append(eye)
        scaled.append(times(down, off))
    forms = [form(block) for block in scaled]
    right = form_rows(forms)
    squares = [mul(block, right) for block in forms]
    cubes = [mul(form(block), right) for block in squares]
    factor = invert(*across)
    out = []
    for eye, one, two, three in zip(eyes, scaled, squares, cubes):
        real = jnp.where(eye, 1.0, 0.0) - one[0] + two[0] - three[0]
        out.append(times((real, two[1] - one[1] - three[1]), factor))
    return out


def pick_block(y, x, slab, own, x_side, y_side, far):
    same_y = y == slab // 2
    same_x = x == slab % 2
    near = choose(same_x, read(own), read(x_side))
    away = choose(same_x, read(y_side), read(far))
    return choose(same_y, near, away)


def forward(block, coupling, green_form):
    lefts = [form(part) for part in split_rows(coupling)]
    terms = mul_twice(lefts, green_form, adjoint_form(coupling), axis=1)
    mats = [
        (part[0] - term[0], part[1] - term[1]) for part, term in zip(split_rows(block), terms)
    ]
    return inverse(mats)


def couple_down(coupling, full_form):
    lefts = [form(part) for part in split_rows((coupling[0].T, -coupling[1].T))]
    return mul_twice(lefts, full_form, form(coupling))


def complete(greens, coupled_form):
    forms = [form(block) for block in greens]
    extra = mul_twice(forms, coupled_form, form_rows(forms))
    return [(g[0] + e[0], g[1] + e[1]) for g, e in zip(greens, extra)]


def whole_form(blocks):
    return form_rows([form(block) for block in blocks])


def first_kernel(place, b_own, b_x, b_y, b_far, g_ref):
    y, x = place[0], place[1]
    write(g_ref, inverse(split_rows(pick_block(y, x, 0, b_own, b_x, b_y, b_far))))


def middle_coupling(y, x, slab, c_own, c_one, c_two):
    if slab == 1:
        return choose(x == y, read(c_one), choose(x == 1, read(c_own), read(c_two)))
    return choose(x == y, read(c_two), choose(x == 1, read(c_one), read(c_own)))


def forward_kernel(place, b_own, b_x, b_y, b_far, c_own, c_one, c_two, g0_ref, g1_ref, g2_ref):
    y, x = place[0], place[1]
    green_form = form(read(g0_ref))
    for slab, ref in ((1, g1_ref), (2, g2_ref)):
        block = pick_block(y, x, slab, b_own, b_x, b_y, b_far)
        greens = forward(block, middle_coupling(y, x, slab, c_own, c_one, c_two), green_form)
        write(ref, greens)
        green_form = whole_form(greens)


def backward_kernel(
    place, b_own, b_x, b_y, b_far, c_own, c_one, c_two, c_last, c_last_x,
    g0_ref, g1_ref, g2_ref, keep_ref, give_ref,
):
    y, x = place[0], place[1]

    def finish(slab, blocks):
        full = join_rows(blocks)
        keep_ref[slab] = jnp.where(x == 0, full[0], full[1])
        give_ref[slab] = jnp.where(x == 0, full[1], full[0])

    coupling = choose(y == 0, read(c_last), choose(x == 0, read(c_last_x), read(c_own)))
    block = pick_block(y, x, 3, b_own, b_x, b_y, b_far)
    fulls = forward(block, coupling, form(read(g2_ref)))
    finish(3, fulls)
    for slab, ref in ((2, g2_ref), (1, g1_ref), (0, g0_ref)):
        coupled = couple_down(coupling, whole_form(fulls))
        fulls = complete(split_rows(read(ref)), whole_form(coupled))
        finish(slab, fulls)
        if slab:
            coupling = middle_coupling(y, x, slab, c_own, c_one, c_two)


def mix_kernel(phonon, parts_ref, out_ref):
    slots, rows, _ = parts_ref.shape
    energies = out_ref.shape[0]
    planes, step = slots // 4, 8

    def source(slot):
        return 2 * (slot % planes) + slot // planes // 2

    for row in range(0, rows, step):
        here = slice(row, row + step)
        values = [None] * energies
        for slot in range(slots):
            value = parts_ref[slot, here, :]
            held = values[source(slot)]
            values[source(slot)] = value if held is None else held + value
        for energy in range(energies):
            total = phonon[energy, 0] * values[0]
            for other in range(1, energies):
                total = total + phonon[energy, other] * values[other]
            out_ref[energy, here, :] = total


def prepare_kernel(place, scale, onsite_ref, hop_ref, sigma_ref, own_ref, other_ref):
    width = hop_ref.shape[-1]
    eye = lax.broadcasted_iota(jnp.int32, (width, width), 0) == lax.broadcasted_iota(
        jnp.int32, (width, width), 1
    )
    for ref, local, energy in ((other_ref, 1 - place[0], scale[1]), (own_ref, place[0], scale[0])):
        level = energy - onsite_ref[...]
        ref[0] = jnp.where(eye, level, 0.0) - hop_ref[0] - sigma_ref[local, 0]
        ref[1] = jnp.where(eye, ETA, 0.0) - hop_ref[1] - sigma_ref[local, 1]


def call(kernel, place, arrays, shape, count, products):
    width = arrays[0].shape[-1]
    vmem = pl.BlockSpec(memory_space=pltpu.VMEM)
    return pl.pallas_call(
        kernel,
        out_shape=[jax.ShapeDtypeStruct(shape, jnp.float32)] * count,
        in_specs=[pl.BlockSpec(memory_space=pltpu.SMEM)] + [vmem] * len(arrays),
        out_specs=[vmem] * count,
        compiler_params=pltpu.CompilerParams(vmem_limit_bytes=VMEM_BYTES),
        cost_estimate=pl.CostEstimate(
            flops=products * 9 * 2 * width**3,
            bytes_accessed=(len(arrays) + count) * 2 * width * width * 4,
            transcendentals=0,
        ),
    )(place, *arrays)


def owner_body(onsite, hop, couple, sigma_in, shifts, mode_weight):
    e_local = sigma_in.shape[0]
    width = onsite.shape[-1]
    energy_count = lax.axis_size("energy")
    mom_count = lax.axis_size("mom")
    total = e_local * energy_count
    axes = ("slab", "energy", "mom")
    slab = lax.axis_index("slab")
    z = lax.axis_index("energy")
    k = lax.axis_index("mom")
    y, x = slab // 2, slab % 2
    place = jnp.stack([y, x]).astype(jnp.int32)
    active = k == x

    def device(yy, xx, zz, kk):
        return ((2 * yy + xx) * energy_count + zz) * mom_count + kk

    chips = [(yy, xx, zz) for yy in range(2) for xx in range(2) for zz in range(energy_count)]
    to_x = [(device(a, b, c, 1 - b), device(a, 1 - b, c, 1 - b)) for a, b, c in chips]
    to_y = [(device(a, b, c, b), device(1 - a, b, c, b)) for a, b, c in chips]
    to_far = [(device(a, b, c, 1 - b), device(1 - a, 1 - b, c, 1 - b)) for a, b, c in chips]

    def routes(*pairs):
        return [
            (device(*divmod(s, 2), zz, t % 2), device(*divmod(t, 2), zz, t % 2))
            for s, t in pairs
            for zz in range(energy_count)
        ]

    siblings = [(device(a, b, c, d), device(a, b, c, 1 - d)) for a, b, c in chips for d in range(2)]
    gift = [(device(a, b, c, b), device(a, b, c, 1 - b)) for a, b, c in chips]

    def send(value, pairs):
        return lax.ppermute(value, axes, pairs)

    locals_ = jnp.stack([y, 1 - y])
    energies = -0.5 + ((z * e_local + locals_).astype(jnp.float32) + 0.5) / total
    smem = pl.BlockSpec(memory_space=pltpu.SMEM)
    vmem = pl.BlockSpec(memory_space=pltpu.VMEM)
    block_shape = jax.ShapeDtypeStruct((2, width, width), jnp.float32)
    b_own, b_other = pl.pallas_call(
        prepare_kernel,
        out_shape=[block_shape] * 2,
        in_specs=[smem, smem, vmem, vmem, vmem],
        out_specs=[vmem] * 2,
        compiler_params=pltpu.CompilerParams(vmem_limit_bytes=VMEM_BYTES),
    )(place, energies, onsite[0], hop[0, 0], sigma_in[:, 0])

    coupling = couple[0, 0]
    c_one = send(coupling, routes((1, 0), (1, 3), (2, 1)))
    c_two = send(coupling, routes((1, 2), (2, 0), (2, 3)))
    b_far = send(b_other, to_far)
    b_y = send(b_other, to_y)
    b_x = send(b_own, to_x)
    c_last = send(coupling, routes((3, 0), (3, 1)))
    c_last_x = send(coupling, routes((3, 2)))

    blocks = (b_own, b_x, b_y, b_far)
    shape = (2, width, width)
    (g0,) = call(first_kernel, place, blocks, shape, 1, 2)
    middle = (coupling, c_one, c_two)
    g1, g2 = call(forward_kernel, place, (*blocks, *middle, g0), shape, 2, 8)
    shape = (4, width, width)
    keep, give = call(
        backward_kernel, place, (*blocks, *middle, c_last, c_last_x, g0, g1, g2), shape, 2, 16
    )
    half = jnp.where(active, keep, send(give, gift))

    rows = width // energy_count
    slots = 4 * energy_count
    parts = lax.all_to_all(
        half.reshape(slots, rows, width), ("slab", "energy"), 0, 0, tiled=True
    )
    phonon = phonon_matrix(shifts, mode_weight, total) / mom_count
    mixed = pl.pallas_call(
        mix_kernel,
        out_shape=jax.ShapeDtypeStruct((total, rows, width), jnp.float32),
        in_specs=[smem, vmem],
        out_specs=vmem,
        compiler_params=pltpu.CompilerParams(vmem_limit_bytes=VMEM_BYTES),
    )(phonon, parts)
    other = send(mixed, siblings)
    mine = jnp.arange(2)[:, None, None] == k
    result = jnp.where(mine, mixed[:, None], other[:, None])
    return result[:, None]


def solution(mesh):
    in_specs = (
        P("mom", "slab", None),
        P("mom", "slab", None, None, None),
        P("mom", "slab", None, None, None),
        P("energy", "slab", None, None, None),
        P(),
        P(),
    )
    out_specs = P(None, "slab", None, "energy", None)
    count = mesh.shape["energy"]

    def run(onsite, hop, couple, sigma_in, shifts, mode_weight):
        owned = (
            mesh.shape["slab"] == 4
            and mesh.shape["mom"] == 2
            and couple.shape[:2] == (2, 4)
            and sigma_in.shape[0] == 2 * count
            and count & (count - 1) == 0
        )
        inner = owner_body if owned else chain_body
        sharded = jax.shard_map(
            inner, mesh=mesh, in_specs=in_specs, out_specs=out_specs, check_vma=False
        )
        return sharded(onsite, hop, couple, sigma_in, shifts, mode_weight)

    return run
```

```python
import functools

import jax
import jax.numpy as jnp
from jax import lax
from jax.experimental import pallas as pl
from jax.experimental.pallas import tpu as pltpu
from jax.sharding import PartitionSpec as P

ETA = 0.5
HIGH = lax.Precision.HIGHEST


def shifted(shard, axis, by):
    length = lax.axis_size(axis)
    pairs = [(i, i + by) for i in range(length) if 0 <= i + by < length]
    return lax.ppermute(shard, axis, pairs)


def complex_mul(form, left, right):

    def product(first, second):
        return jnp.einsum(form, first, second, precision=HIGH)

    return (
        product(left[0], right[0]) - product(left[1], right[1]),
        product(left[0], right[1]) + product(left[1], right[0]),
    )


def newton_inverse(mat_real, mat_imag, form, identity):
    diag_real = jnp.diagonal(mat_real, axis1=-2, axis2=-1)
    diag_imag = jnp.diagonal(mat_imag, axis1=-2, axis2=-1)
    denom = diag_real * diag_real + diag_imag * diag_imag
    x_real = diag_real / denom
    x_imag = -diag_imag / denom
    rows_real = x_real[..., :, None] * mat_real - x_imag[..., :, None] * mat_imag
    rows_imag = x_real[..., :, None] * mat_imag + x_imag[..., :, None] * mat_real
    both_real = rows_real * x_real[..., None, :] - rows_imag * x_imag[..., None, :]
    both_imag = rows_real * x_imag[..., None, :] + rows_imag * x_real[..., None, :]
    first = (
        2.0 * identity * x_real[..., None, :] - both_real,
        2.0 * identity * x_imag[..., None, :] - both_imag,
    )
    resid = complex_mul(form, (mat_real, mat_imag), first)
    second = complex_mul(form, first, resid)
    return (2.0 * first[0] - second[0], 2.0 * first[1] - second[1])


def phonon_matrix(shifts, mode_weight, count):
    rows = jnp.arange(count)[:, None, None]
    cols = jnp.arange(count)[None, :, None]
    offset = shifts[None, None, :]
    upper = (cols == rows + offset).astype(jnp.float32)
    lower = (cols == rows - offset).astype(jnp.float32)
    return jnp.sum(upper * mode_weight[0] + lower * mode_weight[1], axis=2)


def chain_body(onsite, hop, couple, sigma_in, shifts, mode_weight):
    e_local = sigma_in.shape[0]
    width = onsite.shape[-1]
    slab_count = lax.axis_size("slab")
    slab_index = lax.axis_index("slab")
    energy_count = lax.axis_size("energy")
    mom_count = lax.axis_size("mom")
    total = e_local * energy_count
    identity = jnp.eye(width, dtype=jnp.float32)
    global_index = lax.axis_index("energy") * e_local + jnp.arange(e_local)
    energy = -0.5 + (global_index.astype(jnp.float32) + 0.5) / total
    coupling = (couple[0, 0, 0], couple[0, 0, 1])
    adjoint = (coupling[0].T, -coupling[1].T)
    hopping = (hop[0, 0, 0], hop[0, 0, 1])
    level = onsite[0, 0]
    sigma = sigma_in[:, 0]

    def forward(received, energies, sig):
        temp = complex_mul("ij,ejl->eil", coupling, (received[:, 0], received[:, 1]))
        left = complex_mul("eij,jl->eil", temp, adjoint)
        z_real = energies[:, None] - level[None, :]
        mat_real = identity * z_real[:, None, :] - hopping[0] - sig[:, 0] - left[0]
        mat_imag = identity * ETA - hopping[1] - sig[:, 1] - left[1]
        green = newton_inverse(mat_real, mat_imag, "eij,ejl->eil", identity)
        return jnp.stack(green, axis=1)

    def backward(green, received):
        pair = (green[:, 0], green[:, 1])
        temp = complex_mul("eij,ejl->eil", pair, (received[:, 0], received[:, 1]))
        extra = complex_mul("eij,ejl->eil", temp, pair)
        full = (pair[0] + extra[0], pair[1] + extra[1])
        temp = complex_mul("ij,ejl->eil", adjoint, full)
        coupled = complex_mul("eij,jl->eil", temp, coupling)
        return (jnp.stack(full, axis=1), jnp.stack(coupled, axis=1))

    empty = jnp.zeros((e_local, 2, width, width), jnp.float32)

    def forward_step(step, green_all):
        received = shifted(green_all, "slab", 1)
        return lax.cond(
            slab_index == step, lambda: forward(received, energy, sigma), lambda: green_all
        )

    green_all = lax.fori_loop(0, slab_count, forward_step, empty)

    def backward_step(step, carry):
        received = shifted(carry[1], "slab", -1)
        return lax.cond(
            slab_index == slab_count - 1 - step,
            lambda: backward(green_all, received),
            lambda: carry,
        )

    full_all, coupled_all = lax.fori_loop(0, slab_count, backward_step, (empty, empty))
    phonon = phonon_matrix(shifts, mode_weight, total)
    blocks = full_all[:, None]
    mixed = jnp.einsum(
        "ef,fsrjl->esrjl",
        phonon,
        lax.all_to_all(blocks, "energy", split_axis=3, concat_axis=0, tiled=True),
        precision=HIGH,
    )
    result = lax.psum(mixed, "mom") / mom_count
    return result


VMEM_BYTES = 24 * 1024 * 1024
ALL_VMEM_BYTES = 60 * 1024 * 1024


BLOCKS = 2


def halves(value):
    high = value.astype(jnp.bfloat16)
    low = (value - high.astype(jnp.float32)).astype(jnp.bfloat16)
    return high, low


def form(pair):
    return halves(pair[0]), halves(pair[1]), halves(pair[0] + pair[1])


def adjoint_form(pair):
    return halves(pair[0]), halves(-pair[1]), halves(pair[0] - pair[1])


def real_dot(left, right, axis):
    rows = left[0].shape[0]
    numbers = (((1,), (axis,)), ((), ()))
    both = jnp.concatenate([left[0], left[1]], axis=0)
    main = lax.dot_general(both, right[0], numbers, preferred_element_type=jnp.float32)
    rest = lax.dot_general(left[0], right[1], numbers, preferred_element_type=jnp.float32)
    return main[:rows] + main[rows:] + rest


def mul(left, right, axis=0):
    first = real_dot(left[0], right[0], axis)
    second = real_dot(left[1], right[1], axis)
    third = real_dot(left[2], right[2], axis)
    return first - second, third - first - second


def mul_twice(blocks, right, last, axis=0):
    inner = [mul(block, right) for block in blocks]
    return [mul(form(block), last, axis) for block in inner]


def split_rows(pair):
    size = pair[0].shape[0] // BLOCKS
    return [tuple(part[b * size : (b + 1) * size] for part in pair) for b in range(BLOCKS)]


def join_rows(blocks):
    return tuple(jnp.concatenate([block[i] for block in blocks], axis=0) for i in range(2))


def form_rows(forms):
    return tuple(
        tuple(jnp.concatenate([f[plane][term] for f in forms], axis=0) for term in range(2))
        for plane in range(3)
    )


def read(ref):
    return ref[0], ref[1]


def write(ref, blocks):
    size = blocks[0][0].shape[0]
    for b, block in enumerate(blocks):
        ref[0, b * size : (b + 1) * size] = block[0]
        ref[1, b * size : (b + 1) * size] = block[1]


def choose(cond, left, right):
    return jnp.where(cond, left[0], right[0]), jnp.where(cond, left[1], right[1])


def times(left, right):
    return left[0] * right[0] - left[1] * right[1], left[0] * right[1] + left[1] * right[0]


def inverse(mats):
    size, width = mats[0][0].shape

    def invert(real, imag):
        denom = real * real + imag * imag
        return real / denom, -imag / denom

    eyes, scaled = [], []
    across = (0.0, 0.0)
    for b, mat in enumerate(mats):
        eye = lax.broadcasted_iota(jnp.int32, (size, width), 0) + b * size == (
            lax.broadcasted_iota(jnp.int32, (size, width), 1)
        )
        on = [jnp.where(eye, part, 0.0) for part in mat]
        off = [jnp.where(eye, 0.0, part) for part in mat]
        across = tuple(
            total + jnp.sum(part, axis=0, keepdims=True) for total, part in zip(across, on)
        )
        down = invert(*(jnp.sum(part, axis=1, keepdims=True) for part in on))
        eyes.append(eye)
        scaled.append(times(down, off))
    forms = [form(block) for block in scaled]
    right = form_rows(forms)
    squares = [mul(block, right) for block in forms]
    cubes = [mul(form(block), right) for block in squares]
    factor = invert(*across)
    out = []
    for eye, one, two, three in zip(eyes, scaled, squares, cubes):
        real = jnp.where(eye, 1.0, 0.0) - one[0] + two[0] - three[0]
        out.append(times((real, two[1] - one[1] - three[1]), factor))
    return out


def pick_block(y, x, slab, own, x_side, y_side, far):
    same_y = y == slab // 2
    same_x = x == slab % 2
    near = choose(same_x, read(own), read(x_side))
    away = choose(same_x, read(y_side), read(far))
    return choose(same_y, near, away)


def forward(block, coupling, green_form):
    lefts = [form(part) for part in split_rows(coupling)]
    terms = mul_twice(lefts, green_form, adjoint_form(coupling), axis=1)
    mats = [
        (part[0] - term[0], part[1] - term[1]) for part, term in zip(split_rows(block), terms)
    ]
    return inverse(mats)


def couple_down(coupling, full_form):
    lefts = [form(part) for part in split_rows((coupling[0].T, -coupling[1].T))]
    return mul_twice(lefts, full_form, form(coupling))


def complete(greens, coupled_form):
    forms = [form(block) for block in greens]
    extra = mul_twice(forms, coupled_form, form_rows(forms))
    return [(g[0] + e[0], g[1] + e[1]) for g, e in zip(greens, extra)]


def whole_form(blocks):
    return form_rows([form(block) for block in blocks])


def first_kernel(place, b_own, b_x, b_y, b_far, g_ref):
    y, x = place[0], place[1]
    write(g_ref, inverse(split_rows(pick_block(y, x, 0, b_own, b_x, b_y, b_far))))


def two_halves(place, mine, theirs):
    first = place[2] == 0
    return tuple(
        jnp.concatenate(
            [jnp.where(first, mine[i], theirs[i]), jnp.where(first, theirs[i], mine[i])], axis=0
        )
        for i in range(2)
    )


def coupling_of(place, slab, c_own, *got):
    y, x = place[0], place[1]
    one, two, three = (two_halves(place, *got[i : i + 2]) for i in (0, 2, 4))
    if slab == 1:
        return choose(x == y, one, choose(x == 1, read(c_own), two))
    if slab == 2:
        return choose(x == y, two, choose(x == 1, one, read(c_own)))
    return choose(y == 0, choose(x == 0, three, two), choose(x == 0, one, read(c_own)))


def forward_kernel(place, b_own, b_x, b_y, b_far, *refs):
    *couplings, g0_ref, g1_ref, g2_ref = refs
    y, x = place[0], place[1]
    green_form = form(read(g0_ref))
    for slab, ref in ((1, g1_ref), (2, g2_ref)):
        block = pick_block(y, x, slab, b_own, b_x, b_y, b_far)
        greens = forward(block, coupling_of(place, slab, *couplings), green_form)
        write(ref, greens)
        green_form = whole_form(greens)


def backward_kernel(place, b_own, b_x, b_y, b_far, *refs):
    *couplings, g0_ref, g1_ref, g2_ref, keep_ref, give_ref = refs
    y, x = place[0], place[1]

    def finish(slab, blocks):
        full = join_rows(blocks)
        keep_ref[slab] = jnp.where(x == 0, full[0], full[1])
        give_ref[slab] = jnp.where(x == 0, full[1], full[0])

    coupling = coupling_of(place, 3, *couplings)
    block = pick_block(y, x, 3, b_own, b_x, b_y, b_far)
    fulls = forward(block, coupling, form(read(g2_ref)))
    finish(3, fulls)
    for slab, ref in ((2, g2_ref), (1, g1_ref), (0, g0_ref)):
        coupled = couple_down(coupling, whole_form(fulls))
        fulls = complete(split_rows(read(ref)), whole_form(coupled))
        finish(slab, fulls)
        if slab:
            coupling = coupling_of(place, slab, *couplings)


def mix_kernel(phonon, parts_ref, out_ref):
    slots, rows, _ = parts_ref.shape
    energies = out_ref.shape[0]
    planes, step = slots // 4, 8

    def source(slot):
        return 2 * (slot % planes) + slot // planes // 2

    for row in range(0, rows, step):
        here = slice(row, row + step)
        values = [None] * energies
        for slot in range(slots):
            value = parts_ref[slot, here, :]
            held = values[source(slot)]
            values[source(slot)] = value if held is None else held + value
        for energy in range(energies):
            total = phonon[energy, 0] * values[0]
            for other in range(1, energies):
                total = total + phonon[energy, other] * values[other]
            out_ref[energy, here, :] = total


def prepare_kernel(
    place, scale, onsite_ref, hop_hbm, sigma_hbm, couple_hbm, other_ref, own_ref, part_ref,
    hop_ref, sigma_ref, sems,
):
    width, rows = hop_ref.shape[-1], part_ref.shape[1]
    order = (1 - place[0], place[0])
    copies = [pltpu.make_async_copy(hop_hbm, hop_ref, sems.at[0])]
    for i, local in enumerate(order):
        copies.append(pltpu.make_async_copy(sigma_hbm.at[local], sigma_ref.at[i], sems.at[1 + i]))
    start = pl.multiple_of(place[2] * rows, rows)
    copies.append(pltpu.make_async_copy(couple_hbm.at[:, pl.ds(start, rows), :], part_ref, sems.at[3]))
    for copy in copies:
        copy.start()
    eye = lax.broadcasted_iota(jnp.int32, (width, width), 0) == lax.broadcasted_iota(
        jnp.int32, (width, width), 1
    )
    copies[0].wait()
    for i, ref in enumerate((other_ref, own_ref)):
        copies[1 + i].wait()
        level = scale[1 - i] - onsite_ref[...]
        ref[0] = jnp.where(eye, level, 0.0) - hop_ref[0] - sigma_ref[i, 0]
        ref[1] = jnp.where(eye, ETA, 0.0) - hop_ref[1] - sigma_ref[i, 1]
    copies[3].wait()


def call(kernel, place, arrays, shape, count, products):
    width = arrays[0].shape[-1]
    vmem = pl.BlockSpec(memory_space=pltpu.VMEM)
    return pl.pallas_call(
        kernel,
        out_shape=[jax.ShapeDtypeStruct(shape, jnp.float32)] * count,
        in_specs=[pl.BlockSpec(memory_space=pltpu.SMEM)] + [vmem] * len(arrays),
        out_specs=[vmem] * count,
        compiler_params=pltpu.CompilerParams(vmem_limit_bytes=VMEM_BYTES),
        cost_estimate=pl.CostEstimate(
            flops=products * 9 * 2 * width**3,
            bytes_accessed=(len(arrays) + count) * 2 * width * width * 4,
            transcendentals=0,
        ),
    )(place, *arrays)


def owner_body(onsite, hop, couple, sigma_in, shifts, mode_weight):
    e_local = sigma_in.shape[0]
    width = onsite.shape[-1]
    energy_count = lax.axis_size("energy")
    mom_count = lax.axis_size("mom")
    total = e_local * energy_count
    axes = ("slab", "energy", "mom")
    slab = lax.axis_index("slab")
    z = lax.axis_index("energy")
    k = lax.axis_index("mom")
    y, x = slab // 2, slab % 2
    place = jnp.stack([y, x, z % 2]).astype(jnp.int32)
    active = k == x

    def device(yy, xx, zz, kk):
        return ((2 * yy + xx) * energy_count + zz) * mom_count + kk

    chips = [(yy, xx, zz) for yy in range(2) for xx in range(2) for zz in range(energy_count)]
    to_x = [(device(a, b, c, 1 - b), device(a, 1 - b, c, 1 - b)) for a, b, c in chips]
    to_y = [(device(a, b, c, b), device(1 - a, b, c, b)) for a, b, c in chips]
    to_far = [(device(a, b, c, 1 - b), device(1 - a, 1 - b, c, 1 - b)) for a, b, c in chips]

    def routes(*pairs):
        return [
            (device(*divmod(s, 2), zz, t % 2), device(*divmod(t, 2), zz, t % 2))
            for s, t in pairs
            for zz in range(energy_count)
        ]

    beside = [(device(a, b, c, b), device(a, b, c ^ 1, b)) for a, b, c in chips]
    siblings = [(device(a, b, c, d), device(a, b, c, 1 - d)) for a, b, c in chips for d in range(2)]
    gift = [(device(a, b, c, b), device(a, b, c, 1 - b)) for a, b, c in chips]

    def send(value, pairs):
        return lax.ppermute(value, axes, pairs)

    locals_ = jnp.stack([y, 1 - y])
    energies = -0.5 + ((z * e_local + locals_).astype(jnp.float32) + 0.5) / total
    smem = pl.BlockSpec(memory_space=pltpu.SMEM)
    vmem = pl.BlockSpec(memory_space=pltpu.VMEM)
    block_shape = jax.ShapeDtypeStruct((2, width, width), jnp.float32)
    hbm = pl.BlockSpec(memory_space=pltpu.HBM)
    coupling = couple[0, 0]
    b_other, b_own, c_part = pl.pallas_call(
        prepare_kernel,
        out_shape=[block_shape] * 2 + [jax.ShapeDtypeStruct((2, width // 2, width), jnp.float32)],
        in_specs=[smem, smem, vmem, hbm, hbm, hbm],
        out_specs=[vmem] * 3,
        scratch_shapes=[
            pltpu.VMEM((2, width, width), jnp.float32),
            pltpu.VMEM((2, 2, width, width), jnp.float32),
            pltpu.SemaphoreType.DMA((4,)),
        ],
        compiler_params=pltpu.CompilerParams(vmem_limit_bytes=ALL_VMEM_BYTES),
    )(place, energies, onsite[0], hop[0, 0], sigma_in[:, 0], coupling)

    couplings = [coupling]
    for pairs in (
        routes((1, 0), (1, 3), (2, 1), (3, 2)),
        routes((2, 0), (2, 3), (1, 2), (3, 1)),
        routes((3, 0)),
    ):
        mine = send(c_part, pairs)
        couplings += [mine, send(mine, beside)]
    b_far = send(b_other, to_far)
    b_y = send(b_other, to_y)
    b_x = send(b_own, to_x)

    blocks = (b_own, b_x, b_y, b_far)
    shape = (2, width, width)
    (g0,) = call(first_kernel, place, blocks, shape, 1, 2)
    g1, g2 = call(forward_kernel, place, (*blocks, *couplings, g0), shape, 2, 8)
    shape = (4, width, width)
    keep, give = call(
        backward_kernel, place, (*blocks, *couplings, g0, g1, g2), shape, 2, 16
    )
    half = jnp.where(active, keep, send(give, gift))

    rows = width // energy_count
    slots = 4 * energy_count
    parts = lax.all_to_all(
        half.reshape(slots, rows, width), ("slab", "energy"), 0, 0, tiled=True
    )
    phonon = phonon_matrix(shifts, mode_weight, total) / mom_count
    mixed = pl.pallas_call(
        mix_kernel,
        out_shape=jax.ShapeDtypeStruct((total, rows, width), jnp.float32),
        in_specs=[smem, vmem],
        out_specs=vmem,
        compiler_params=pltpu.CompilerParams(vmem_limit_bytes=VMEM_BYTES),
    )(phonon, parts)
    other = send(mixed, siblings)
    mine = jnp.arange(2)[:, None, None] == k
    result = jnp.where(mine, mixed[:, None], other[:, None])
    return result[:, None]


def solution(mesh):
    in_specs = (
        P("mom", "slab", None),
        P("mom", "slab", None, None, None),
        P("mom", "slab", None, None, None),
        P("energy", "slab", None, None, None),
        P(),
        P(),
    )
    out_specs = P(None, "slab", None, "energy", None)
    count = mesh.shape["energy"]

    def run(onsite, hop, couple, sigma_in, shifts, mode_weight):
        owned = (
            mesh.shape["slab"] == 4
            and mesh.shape["mom"] == 2
            and couple.shape[:2] == (2, 4)
            and sigma_in.shape[0] == 2 * count
            and count & (count - 1) == 0
        )
        inner = owner_body if owned else chain_body
        sharded = jax.shard_map(
            inner, mesh=mesh, in_specs=in_specs, out_specs=out_specs, check_vma=False
        )
        return sharded(onsite, hop, couple, sigma_in, shifts, mode_weight)

    return run
```

```python
import functools

import jax
import jax.numpy as jnp
from jax import lax
from jax.experimental import pallas as pl
from jax.experimental.pallas import tpu as pltpu
from jax.sharding import PartitionSpec as P

ETA = 0.5
HIGH = lax.Precision.HIGHEST


def shifted(shard, axis, by):
    length = lax.axis_size(axis)
    pairs = [(i, i + by) for i in range(length) if 0 <= i + by < length]
    return lax.ppermute(shard, axis, pairs)


def complex_mul(form, left, right):

    def product(first, second):
        return jnp.einsum(form, first, second, precision=HIGH)

    return (
        product(left[0], right[0]) - product(left[1], right[1]),
        product(left[0], right[1]) + product(left[1], right[0]),
    )


def newton_inverse(mat_real, mat_imag, form, identity):
    diag_real = jnp.diagonal(mat_real, axis1=-2, axis2=-1)
    diag_imag = jnp.diagonal(mat_imag, axis1=-2, axis2=-1)
    denom = diag_real * diag_real + diag_imag * diag_imag
    x_real = diag_real / denom
    x_imag = -diag_imag / denom
    rows_real = x_real[..., :, None] * mat_real - x_imag[..., :, None] * mat_imag
    rows_imag = x_real[..., :, None] * mat_imag + x_imag[..., :, None] * mat_real
    both_real = rows_real * x_real[..., None, :] - rows_imag * x_imag[..., None, :]
    both_imag = rows_real * x_imag[..., None, :] + rows_imag * x_real[..., None, :]
    first = (
        2.0 * identity * x_real[..., None, :] - both_real,
        2.0 * identity * x_imag[..., None, :] - both_imag,
    )
    resid = complex_mul(form, (mat_real, mat_imag), first)
    second = complex_mul(form, first, resid)
    return (2.0 * first[0] - second[0], 2.0 * first[1] - second[1])


def phonon_matrix(shifts, mode_weight, count):
    rows = jnp.arange(count)[:, None, None]
    cols = jnp.arange(count)[None, :, None]
    offset = shifts[None, None, :]
    upper = (cols == rows + offset).astype(jnp.float32)
    lower = (cols == rows - offset).astype(jnp.float32)
    return jnp.sum(upper * mode_weight[0] + lower * mode_weight[1], axis=2)


def chain_body(onsite, hop, couple, sigma_in, shifts, mode_weight):
    e_local = sigma_in.shape[0]
    width = onsite.shape[-1]
    slab_count = lax.axis_size("slab")
    slab_index = lax.axis_index("slab")
    energy_count = lax.axis_size("energy")
    mom_count = lax.axis_size("mom")
    total = e_local * energy_count
    identity = jnp.eye(width, dtype=jnp.float32)
    global_index = lax.axis_index("energy") * e_local + jnp.arange(e_local)
    energy = -0.5 + (global_index.astype(jnp.float32) + 0.5) / total
    coupling = (couple[0, 0, 0], couple[0, 0, 1])
    adjoint = (coupling[0].T, -coupling[1].T)
    hopping = (hop[0, 0, 0], hop[0, 0, 1])
    level = onsite[0, 0]
    sigma = sigma_in[:, 0]

    def forward(received, energies, sig):
        temp = complex_mul("ij,ejl->eil", coupling, (received[:, 0], received[:, 1]))
        left = complex_mul("eij,jl->eil", temp, adjoint)
        z_real = energies[:, None] - level[None, :]
        mat_real = identity * z_real[:, None, :] - hopping[0] - sig[:, 0] - left[0]
        mat_imag = identity * ETA - hopping[1] - sig[:, 1] - left[1]
        green = newton_inverse(mat_real, mat_imag, "eij,ejl->eil", identity)
        return jnp.stack(green, axis=1)

    def backward(green, received):
        pair = (green[:, 0], green[:, 1])
        temp = complex_mul("eij,ejl->eil", pair, (received[:, 0], received[:, 1]))
        extra = complex_mul("eij,ejl->eil", temp, pair)
        full = (pair[0] + extra[0], pair[1] + extra[1])
        temp = complex_mul("ij,ejl->eil", adjoint, full)
        coupled = complex_mul("eij,jl->eil", temp, coupling)
        return (jnp.stack(full, axis=1), jnp.stack(coupled, axis=1))

    empty = jnp.zeros((e_local, 2, width, width), jnp.float32)

    def forward_step(step, green_all):
        received = shifted(green_all, "slab", 1)
        return lax.cond(
            slab_index == step, lambda: forward(received, energy, sigma), lambda: green_all
        )

    green_all = lax.fori_loop(0, slab_count, forward_step, empty)

    def backward_step(step, carry):
        received = shifted(carry[1], "slab", -1)
        return lax.cond(
            slab_index == slab_count - 1 - step,
            lambda: backward(green_all, received),
            lambda: carry,
        )

    full_all, coupled_all = lax.fori_loop(0, slab_count, backward_step, (empty, empty))
    phonon = phonon_matrix(shifts, mode_weight, total)
    blocks = full_all[:, None]
    mixed = jnp.einsum(
        "ef,fsrjl->esrjl",
        phonon,
        lax.all_to_all(blocks, "energy", split_axis=3, concat_axis=0, tiled=True),
        precision=HIGH,
    )
    result = lax.psum(mixed, "mom") / mom_count
    return result


VMEM_BYTES = 24 * 1024 * 1024


BLOCKS = 2


def halves(value):
    high = value.astype(jnp.bfloat16)
    low = (value - high.astype(jnp.float32)).astype(jnp.bfloat16)
    return high, low


def form(pair):
    return halves(pair[0]), halves(pair[1]), halves(pair[0] + pair[1])


def real_dot(left, right):
    rows = left[0].shape[0]
    both = jnp.concatenate([left[0], left[1]], axis=0)
    main = jnp.dot(both, right[0], preferred_element_type=jnp.float32)
    rest = jnp.dot(left[0], right[1], preferred_element_type=jnp.float32)
    return main[:rows] + main[rows:] + rest


def mul(left, right):
    first = real_dot(left[0], right[0])
    second = real_dot(left[1], right[1])
    third = real_dot(left[2], right[2])
    return first - second, third - first - second


def mul_twice(blocks, right, last):
    inner = [mul(block, right) for block in blocks]
    return [mul(form(block), last) for block in inner]


def split_rows(pair):
    size = pair[0].shape[0] // BLOCKS
    return [tuple(part[b * size : (b + 1) * size] for part in pair) for b in range(BLOCKS)]


def join_rows(blocks):
    return tuple(jnp.concatenate([block[i] for block in blocks], axis=0) for i in range(2))


def form_rows(forms):
    return tuple(
        tuple(jnp.concatenate([f[plane][term] for f in forms], axis=0) for term in range(2))
        for plane in range(3)
    )


def read(ref):
    return ref[0], ref[1]


def write(ref, blocks):
    size = blocks[0][0].shape[0]
    for b, block in enumerate(blocks):
        ref[0, b * size : (b + 1) * size] = block[0]
        ref[1, b * size : (b + 1) * size] = block[1]


def choose(cond, left, right):
    return jnp.where(cond, left[0], right[0]), jnp.where(cond, left[1], right[1])


def times(left, right):
    return left[0] * right[0] - left[1] * right[1], left[0] * right[1] + left[1] * right[0]


def inverse(mats):
    size, width = mats[0][0].shape

    def invert(real, imag):
        denom = real * real + imag * imag
        return real / denom, -imag / denom

    eyes, scaled = [], []
    across = (0.0, 0.0)
    for b, mat in enumerate(mats):
        eye = lax.broadcasted_iota(jnp.int32, (size, width), 0) + b * size == (
            lax.broadcasted_iota(jnp.int32, (size, width), 1)
        )
        on = [jnp.where(eye, part, 0.0) for part in mat]
        off = [jnp.where(eye, 0.0, part) for part in mat]
        across = tuple(
            total + jnp.sum(part, axis=0, keepdims=True) for total, part in zip(across, on)
        )
        down = invert(*(jnp.sum(part, axis=1, keepdims=True) for part in on))
        eyes.append(eye)
        scaled.append(times(down, off))
    forms = [form(block) for block in scaled]
    right = form_rows(forms)
    squares = [mul(block, right) for block in forms]
    cubes = [mul(form(block), right) for block in squares]
    factor = invert(*across)
    out = []
    for eye, one, two, three in zip(eyes, scaled, squares, cubes):
        real = jnp.where(eye, 1.0, 0.0) - one[0] + two[0] - three[0]
        out.append(times((real, two[1] - one[1] - three[1]), factor))
    return out


def pick_block(y, x, slab, own, x_side, y_side, far):
    same_y = y == slab // 2
    same_x = x == slab % 2
    near = choose(same_x, read(own), read(x_side))
    away = choose(same_x, read(y_side), read(far))
    return choose(same_y, near, away)


def stored_form(ref, slab, side):
    at = (slab - 1, side)
    return tuple(tuple(ref[(*at, 2 * plane + term)] for term in range(2)) for plane in range(3))


def stored_rows(ref, slab, side):
    size = ref.shape[-2] // BLOCKS
    at = (slab - 1, side)
    return [
        tuple(
            tuple(ref[(*at, 2 * plane + term, slice(b * size, (b + 1) * size))] for term in range(2))
            for plane in range(3)
        )
        for b in range(BLOCKS)
    ]


def coupling_kernel(place, c_own, c_x, c_y, c_far, out_ref):
    y, x = place[0], place[1]
    for slab in (1, 2, 3):
        real, imag = pick_block(y, x, slab, c_own, c_x, c_y, c_far)
        for side, pair in enumerate(((real, imag), (real.T, -imag.T))):
            for plane, terms in enumerate(form(pair)):
                for term in range(2):
                    out_ref[slab - 1, side, 2 * plane + term] = terms[term]


def chain_kernel(place, b_own, b_x, b_y, b_far, c_forms, keep_ref, give_ref):
    y, x = place[0], place[1]
    greens, forms = [], []
    for slab in range(4):
        mats = split_rows(pick_block(y, x, slab, b_own, b_x, b_y, b_far))
        if slab:
            terms = mul_twice(
                stored_rows(c_forms, slab, 0), form_rows(forms[-1]), stored_form(c_forms, slab, 1)
            )
            mats = [(m[0] - t[0], m[1] - t[1]) for m, t in zip(mats, terms)]
        greens.append(inverse(mats))
        forms.append([form(block) for block in greens[-1]])

    def finish(slab, blocks):
        full = join_rows(blocks)
        keep_ref[slab] = jnp.where(x == 0, full[0], full[1])
        give_ref[slab] = jnp.where(x == 0, full[1], full[0])

    finish(3, greens[3])
    full_form = form_rows(forms[3])
    for slab in (2, 1, 0):
        coupled = mul_twice(
            stored_rows(c_forms, slab + 1, 1), full_form, stored_form(c_forms, slab + 1, 0)
        )
        coupled_form = form_rows([form(block) for block in coupled])
        extra = mul_twice(forms[slab], coupled_form, form_rows(forms[slab]))
        fulls = [(g[0] + e[0], g[1] + e[1]) for g, e in zip(greens[slab], extra)]
        finish(slab, fulls)
        if slab:
            full_form = form_rows([form(block) for block in fulls])


def mix_kernel(phonon, parts_ref, out_ref):
    slots, rows, _ = parts_ref.shape
    energies = out_ref.shape[0]
    planes, step = slots // 4, 8

    def source(slot):
        return 2 * (slot % planes) + slot // planes // 2

    for row in range(0, rows, step):
        here = slice(row, row + step)
        values = [None] * energies
        for slot in range(slots):
            value = parts_ref[slot, here, :]
            held = values[source(slot)]
            values[source(slot)] = value if held is None else held + value
        for energy in range(energies):
            total = phonon[energy, 0] * values[0]
            for other in range(1, energies):
                total = total + phonon[energy, other] * values[other]
            out_ref[energy, here, :] = total


def prepare_kernel(place, scale, onsite_ref, hop_ref, sigma_ref, own_ref, other_ref):
    width = hop_ref.shape[-1]
    eye = lax.broadcasted_iota(jnp.int32, (width, width), 0) == lax.broadcasted_iota(
        jnp.int32, (width, width), 1
    )
    for ref, local, energy in ((other_ref, 1 - place[0], scale[1]), (own_ref, place[0], scale[0])):
        level = energy - onsite_ref[...]
        ref[0] = jnp.where(eye, level, 0.0) - hop_ref[0] - sigma_ref[local, 0]
        ref[1] = jnp.where(eye, ETA, 0.0) - hop_ref[1] - sigma_ref[local, 1]


def call(kernel, place, arrays, shape, count, products):
    width = arrays[0].shape[-1]
    vmem = pl.BlockSpec(memory_space=pltpu.VMEM)
    return pl.pallas_call(
        kernel,
        out_shape=[jax.ShapeDtypeStruct(shape, jnp.float32)] * count,
        in_specs=[pl.BlockSpec(memory_space=pltpu.SMEM)] + [vmem] * len(arrays),
        out_specs=[vmem] * count,
        compiler_params=pltpu.CompilerParams(vmem_limit_bytes=VMEM_BYTES),
        cost_estimate=pl.CostEstimate(
            flops=products * 9 * 2 * width**3,
            bytes_accessed=(len(arrays) + count) * 2 * width * width * 4,
            transcendentals=0,
        ),
    )(place, *arrays)


def owner_body(onsite, hop, couple, sigma_in, shifts, mode_weight):
    e_local = sigma_in.shape[0]
    width = onsite.shape[-1]
    energy_count = lax.axis_size("energy")
    mom_count = lax.axis_size("mom")
    total = e_local * energy_count
    axes = ("slab", "energy", "mom")
    slab = lax.axis_index("slab")
    z = lax.axis_index("energy")
    k = lax.axis_index("mom")
    y, x = slab // 2, slab % 2
    place = jnp.stack([y, x]).astype(jnp.int32)
    active = k == x

    def device(yy, xx, zz, kk):
        return ((2 * yy + xx) * energy_count + zz) * mom_count + kk

    chips = [(yy, xx, zz) for yy in range(2) for xx in range(2) for zz in range(energy_count)]
    to_x = [(device(a, b, c, 1 - b), device(a, 1 - b, c, 1 - b)) for a, b, c in chips]
    to_y = [(device(a, b, c, b), device(1 - a, b, c, b)) for a, b, c in chips]
    to_far = [(device(a, b, c, 1 - b), device(1 - a, 1 - b, c, 1 - b)) for a, b, c in chips]

    def routes(*pairs):
        return [
            (device(*divmod(s, 2), zz, t % 2), device(*divmod(t, 2), zz, t % 2))
            for s, t in pairs
            for zz in range(energy_count)
        ]

    siblings = [(device(a, b, c, d), device(a, b, c, 1 - d)) for a, b, c in chips for d in range(2)]
    gift = [(device(a, b, c, b), device(a, b, c, 1 - b)) for a, b, c in chips]

    def send(value, pairs):
        return lax.ppermute(value, axes, pairs)

    locals_ = jnp.stack([y, 1 - y])
    energies = -0.5 + ((z * e_local + locals_).astype(jnp.float32) + 0.5) / total
    smem = pl.BlockSpec(memory_space=pltpu.SMEM)
    vmem = pl.BlockSpec(memory_space=pltpu.VMEM)
    block_shape = jax.ShapeDtypeStruct((2, width, width), jnp.float32)
    b_own, b_other = pl.pallas_call(
        prepare_kernel,
        out_shape=[block_shape] * 2,
        in_specs=[smem, smem, vmem, vmem, vmem],
        out_specs=[vmem] * 2,
        compiler_params=pltpu.CompilerParams(vmem_limit_bytes=VMEM_BYTES),
    )(place, energies, onsite[0], hop[0, 0], sigma_in[:, 0])

    coupling = couple[0, 0]
    c_x = send(coupling, routes((1, 0), (2, 3), (3, 2)))
    c_y = send(coupling, routes((1, 3), (2, 0), (3, 1)))
    c_far = send(coupling, routes((1, 2), (2, 1), (3, 0)))
    b_far = send(b_other, to_far)
    b_x = send(b_own, to_x)
    b_y = send(b_other, to_y)

    c_forms = pl.pallas_call(
        coupling_kernel,
        out_shape=jax.ShapeDtypeStruct((3, 2, 6, width, width), jnp.bfloat16),
        in_specs=[smem] + [vmem] * 4,
        out_specs=vmem,
        compiler_params=pltpu.CompilerParams(vmem_limit_bytes=VMEM_BYTES),
    )(place, coupling, c_x, c_y, c_far)
    shape = (4, width, width)
    keep, give = call(chain_kernel, place, (b_own, b_x, b_y, b_far, c_forms), shape, 2, 26)
    half = jnp.where(active, keep, send(give, gift))

    rows = width // energy_count
    slots = 4 * energy_count
    parts = lax.all_to_all(
        half.reshape(slots, rows, width), ("slab", "energy"), 0, 0, tiled=True
    )
    phonon = phonon_matrix(shifts, mode_weight, total) / mom_count
    mixed = pl.pallas_call(
        mix_kernel,
        out_shape=jax.ShapeDtypeStruct((total, rows, width), jnp.float32),
        in_specs=[smem, vmem],
        out_specs=vmem,
        compiler_params=pltpu.CompilerParams(vmem_limit_bytes=VMEM_BYTES),
    )(phonon, parts)
    other = send(mixed, siblings)
    mine = jnp.arange(2)[:, None, None] == k
    result = jnp.where(mine, mixed[:, None], other[:, None])
    return result[:, None]


def solution(mesh):
    in_specs = (
        P("mom", "slab", None),
        P("mom", "slab", None, None, None),
        P("mom", "slab", None, None, None),
        P("energy", "slab", None, None, None),
        P(),
        P(),
    )
    out_specs = P(None, "slab", None, "energy", None)
    count = mesh.shape["energy"]

    def run(onsite, hop, couple, sigma_in, shifts, mode_weight):
        owned = (
            mesh.shape["slab"] == 4
            and mesh.shape["mom"] == 2
            and couple.shape[:2] == (2, 4)
            and sigma_in.shape[0] == 2 * count
            and count & (count - 1) == 0
        )
        inner = owner_body if owned else chain_body
        sharded = jax.shard_map(
            inner, mesh=mesh, in_specs=in_specs, out_specs=out_specs, check_vma=False
        )
        return sharded(onsite, hop, couple, sigma_in, shifts, mode_weight)

    return run
```

```python
import functools

import jax
import jax.numpy as jnp
from jax import lax
from jax.experimental import pallas as pl
from jax.experimental.pallas import tpu as pltpu
from jax.sharding import PartitionSpec as P

ETA = 0.5
HIGH = lax.Precision.HIGHEST


def shifted(shard, axis, by):
    length = lax.axis_size(axis)
    pairs = [(i, i + by) for i in range(length) if 0 <= i + by < length]
    return lax.ppermute(shard, axis, pairs)


def complex_mul(form, left, right):

    def product(first, second):
        return jnp.einsum(form, first, second, precision=HIGH)

    return (
        product(left[0], right[0]) - product(left[1], right[1]),
        product(left[0], right[1]) + product(left[1], right[0]),
    )


def newton_inverse(mat_real, mat_imag, form, identity):
    diag_real = jnp.diagonal(mat_real, axis1=-2, axis2=-1)
    diag_imag = jnp.diagonal(mat_imag, axis1=-2, axis2=-1)
    denom = diag_real * diag_real + diag_imag * diag_imag
    x_real = diag_real / denom
    x_imag = -diag_imag / denom
    rows_real = x_real[..., :, None] * mat_real - x_imag[..., :, None] * mat_imag
    rows_imag = x_real[..., :, None] * mat_imag + x_imag[..., :, None] * mat_real
    both_real = rows_real * x_real[..., None, :] - rows_imag * x_imag[..., None, :]
    both_imag = rows_real * x_imag[..., None, :] + rows_imag * x_real[..., None, :]
    first = (
        2.0 * identity * x_real[..., None, :] - both_real,
        2.0 * identity * x_imag[..., None, :] - both_imag,
    )
    resid = complex_mul(form, (mat_real, mat_imag), first)
    second = complex_mul(form, first, resid)
    return (2.0 * first[0] - second[0], 2.0 * first[1] - second[1])


def phonon_matrix(shifts, mode_weight, count):
    rows = jnp.arange(count)[:, None, None]
    cols = jnp.arange(count)[None, :, None]
    offset = shifts[None, None, :]
    upper = (cols == rows + offset).astype(jnp.float32)
    lower = (cols == rows - offset).astype(jnp.float32)
    return jnp.sum(upper * mode_weight[0] + lower * mode_weight[1], axis=2)


def chain_body(onsite, hop, couple, sigma_in, shifts, mode_weight):
    e_local = sigma_in.shape[0]
    width = onsite.shape[-1]
    slab_count = lax.axis_size("slab")
    slab_index = lax.axis_index("slab")
    energy_count = lax.axis_size("energy")
    mom_count = lax.axis_size("mom")
    total = e_local * energy_count
    identity = jnp.eye(width, dtype=jnp.float32)
    global_index = lax.axis_index("energy") * e_local + jnp.arange(e_local)
    energy = -0.5 + (global_index.astype(jnp.float32) + 0.5) / total
    coupling = (couple[0, 0, 0], couple[0, 0, 1])
    adjoint = (coupling[0].T, -coupling[1].T)
    hopping = (hop[0, 0, 0], hop[0, 0, 1])
    level = onsite[0, 0]
    sigma = sigma_in[:, 0]

    def forward(received, energies, sig):
        temp = complex_mul("ij,ejl->eil", coupling, (received[:, 0], received[:, 1]))
        left = complex_mul("eij,jl->eil", temp, adjoint)
        z_real = energies[:, None] - level[None, :]
        mat_real = identity * z_real[:, None, :] - hopping[0] - sig[:, 0] - left[0]
        mat_imag = identity * ETA - hopping[1] - sig[:, 1] - left[1]
        green = newton_inverse(mat_real, mat_imag, "eij,ejl->eil", identity)
        return jnp.stack(green, axis=1)

    def backward(green, received):
        pair = (green[:, 0], green[:, 1])
        temp = complex_mul("eij,ejl->eil", pair, (received[:, 0], received[:, 1]))
        extra = complex_mul("eij,ejl->eil", temp, pair)
        full = (pair[0] + extra[0], pair[1] + extra[1])
        temp = complex_mul("ij,ejl->eil", adjoint, full)
        coupled = complex_mul("eij,jl->eil", temp, coupling)
        return (jnp.stack(full, axis=1), jnp.stack(coupled, axis=1))

    empty = jnp.zeros((e_local, 2, width, width), jnp.float32)

    def forward_step(step, green_all):
        received = shifted(green_all, "slab", 1)
        return lax.cond(
            slab_index == step, lambda: forward(received, energy, sigma), lambda: green_all
        )

    green_all = lax.fori_loop(0, slab_count, forward_step, empty)

    def backward_step(step, carry):
        received = shifted(carry[1], "slab", -1)
        return lax.cond(
            slab_index == slab_count - 1 - step,
            lambda: backward(green_all, received),
            lambda: carry,
        )

    full_all, coupled_all = lax.fori_loop(0, slab_count, backward_step, (empty, empty))
    phonon = phonon_matrix(shifts, mode_weight, total)
    blocks = full_all[:, None]
    mixed = jnp.einsum(
        "ef,fsrjl->esrjl",
        phonon,
        lax.all_to_all(blocks, "energy", split_axis=3, concat_axis=0, tiled=True),
        precision=HIGH,
    )
    result = lax.psum(mixed, "mom") / mom_count
    return result


VMEM_BYTES = 24 * 1024 * 1024


BLOCKS = 2


def halves(value):
    high = value.astype(jnp.bfloat16)
    low = (value - high.astype(jnp.float32)).astype(jnp.bfloat16)
    return high, low


def form(pair):
    return halves(pair[0]), halves(pair[1]), halves(pair[0] + pair[1])


def real_dot(left, right):
    lhs = jnp.concatenate([left[0], left[1], left[0]], axis=1)
    rhs = jnp.concatenate([right[0], right[0], right[1]], axis=0)
    return jnp.dot(lhs, rhs, preferred_element_type=jnp.float32)


def mul(left, right):
    first = real_dot(left[0], right[0])
    second = real_dot(left[1], right[1])
    third = real_dot(left[2], right[2])
    return first - second, third - first - second


def mul_twice(blocks, right, last):
    inner = [mul(block, right) for block in blocks]
    return [mul(form(block), last) for block in inner]


def split_rows(pair):
    size = pair[0].shape[0] // BLOCKS
    return [tuple(part[b * size : (b + 1) * size] for part in pair) for b in range(BLOCKS)]


def join_rows(blocks):
    return tuple(jnp.concatenate([block[i] for block in blocks], axis=0) for i in range(2))


def form_rows(forms):
    return tuple(
        tuple(jnp.concatenate([f[plane][term] for f in forms], axis=0) for term in range(2))
        for plane in range(3)
    )


def read(ref):
    return ref[0], ref[1]


def write(ref, blocks):
    size = blocks[0][0].shape[0]
    for b, block in enumerate(blocks):
        ref[0, b * size : (b + 1) * size] = block[0]
        ref[1, b * size : (b + 1) * size] = block[1]


def choose(cond, left, right):
    return jnp.where(cond, left[0], right[0]), jnp.where(cond, left[1], right[1])


def times(left, right):
    return left[0] * right[0] - left[1] * right[1], left[0] * right[1] + left[1] * right[0]


def inverse(mats):
    size, width = mats[0][0].shape

    def invert(real, imag):
        denom = real * real + imag * imag
        return real / denom, -imag / denom

    eyes, scaled = [], []
    across = (0.0, 0.0)
    for b, mat in enumerate(mats):
        eye = lax.broadcasted_iota(jnp.int32, (size, width), 0) + b * size == (
            lax.broadcasted_iota(jnp.int32, (size, width), 1)
        )
        on = [jnp.where(eye, part, 0.0) for part in mat]
        off = [jnp.where(eye, 0.0, part) for part in mat]
        across = tuple(
            total + jnp.sum(part, axis=0, keepdims=True) for total, part in zip(across, on)
        )
        down = invert(*(jnp.sum(part, axis=1, keepdims=True) for part in on))
        eyes.append(eye)
        scaled.append(times(down, off))
    forms = [form(block) for block in scaled]
    right = form_rows(forms)
    squares = [mul(block, right) for block in forms]
    cubes = [mul(form(block), right) for block in squares]
    factor = invert(*across)
    out = []
    for eye, one, two, three in zip(eyes, scaled, squares, cubes):
        real = jnp.where(eye, 1.0, 0.0) - one[0] + two[0] - three[0]
        out.append(times((real, two[1] - one[1] - three[1]), factor))
    return out


def pick_block(y, x, slab, own, x_side, y_side, far):
    same_y = y == slab // 2
    same_x = x == slab % 2
    near = choose(same_x, read(own), read(x_side))
    away = choose(same_x, read(y_side), read(far))
    return choose(same_y, near, away)


def stored_form(ref, slab, side):
    at = (slab - 1, side)
    return tuple(tuple(ref[(*at, 2 * plane + term)] for term in range(2)) for plane in range(3))


def stored_rows(ref, slab, side):
    size = ref.shape[-2] // BLOCKS
    at = (slab - 1, side)
    return [
        tuple(
            tuple(ref[(*at, 2 * plane + term, slice(b * size, (b + 1) * size))] for term in range(2))
            for plane in range(3)
        )
        for b in range(BLOCKS)
    ]


def coupling_kernel(place, c_own, c_x, c_y, far_mine, far_theirs, out_ref, c_far):
    y, x = place[0], place[1]
    first, rows = place[2] == 0, far_mine.shape[1]
    for part in range(2):
        mine, theirs = far_mine[part], far_theirs[part]
        c_far[part, :rows] = jnp.where(first, mine, theirs)
        c_far[part, rows:] = jnp.where(first, theirs, mine)
    for slab in (1, 2, 3):
        real, imag = pick_block(y, x, slab, c_own, c_x, c_y, c_far)
        for side, pair in enumerate(((real, imag), (real.T, -imag.T))):
            for plane, terms in enumerate(form(pair)):
                for term in range(2):
                    out_ref[slab - 1, side, 2 * plane + term] = terms[term]


def chain_kernel(place, b_own, b_x, b_y, b_far, c_forms, keep_ref, give_ref):
    y, x = place[0], place[1]
    greens, forms = [], []
    for slab in range(4):
        mats = split_rows(pick_block(y, x, slab, b_own, b_x, b_y, b_far))
        if slab:
            terms = mul_twice(
                stored_rows(c_forms, slab, 0), form_rows(forms[-1]), stored_form(c_forms, slab, 1)
            )
            mats = [(m[0] - t[0], m[1] - t[1]) for m, t in zip(mats, terms)]
        greens.append(inverse(mats))
        forms.append([form(block) for block in greens[-1]])

    def finish(slab, blocks):
        full = join_rows(blocks)
        keep_ref[slab] = jnp.where(x == 0, full[0], full[1])
        give_ref[slab] = jnp.where(x == 0, full[1], full[0])

    finish(3, greens[3])
    full_form = form_rows(forms[3])
    for slab in (2, 1, 0):
        coupled = mul_twice(
            stored_rows(c_forms, slab + 1, 1), full_form, stored_form(c_forms, slab + 1, 0)
        )
        coupled_form = form_rows([form(block) for block in coupled])
        extra = mul_twice(forms[slab], coupled_form, form_rows(forms[slab]))
        fulls = [(g[0] + e[0], g[1] + e[1]) for g, e in zip(greens[slab], extra)]
        finish(slab, fulls)
        if slab:
            full_form = form_rows([form(block) for block in fulls])


def mix_kernel(phonon, parts_ref, out_ref):
    slots, rows, _ = parts_ref.shape
    energies = out_ref.shape[0]
    planes, step = slots // 4, 8

    def source(slot):
        return 2 * (slot % planes) + slot // planes // 2

    for row in range(0, rows, step):
        here = slice(row, row + step)
        values = [None] * energies
        for slot in range(slots):
            value = parts_ref[slot, here, :]
            held = values[source(slot)]
            values[source(slot)] = value if held is None else held + value
        for energy in range(energies):
            total = phonon[energy, 0] * values[0]
            for other in range(1, energies):
                total = total + phonon[energy, other] * values[other]
            out_ref[energy, here, :] = total


def pick_kernel(active, keep_ref, got_ref, out_ref):
    for slab in range(out_ref.shape[0]):
        out_ref[slab] = jnp.where(active[0] == 1, keep_ref[slab], got_ref[slab])


def join_kernel(core, mine_ref, other_ref, out_ref):
    energy = pl.program_id(0)
    mine, other = mine_ref[energy], other_ref[energy]
    out_ref[0, 0] = jnp.where(core[0] == 0, mine, other)
    out_ref[0, 1] = jnp.where(core[0] == 0, other, mine)


def prepare_kernel(place, scale, onsite_ref, hop_ref, sigma_ref, own_ref, other_ref):
    width = hop_ref.shape[-1]
    eye = lax.broadcasted_iota(jnp.int32, (width, width), 0) == lax.broadcasted_iota(
        jnp.int32, (width, width), 1
    )
    for ref, local, energy in ((other_ref, 1 - place[0], scale[1]), (own_ref, place[0], scale[0])):
        level = energy - onsite_ref[...]
        ref[0] = jnp.where(eye, level, 0.0) - hop_ref[0] - sigma_ref[local, 0]
        ref[1] = jnp.where(eye, ETA, 0.0) - hop_ref[1] - sigma_ref[local, 1]


def call(kernel, place, arrays, shape, count, products):
    width = arrays[0].shape[-1]
    vmem = pl.BlockSpec(memory_space=pltpu.VMEM)
    return pl.pallas_call(
        kernel,
        out_shape=[jax.ShapeDtypeStruct(shape, jnp.float32)] * count,
        in_specs=[pl.BlockSpec(memory_space=pltpu.SMEM)] + [vmem] * len(arrays),
        out_specs=[vmem] * count,
        compiler_params=pltpu.CompilerParams(vmem_limit_bytes=VMEM_BYTES),
        cost_estimate=pl.CostEstimate(
            flops=products * 9 * 2 * width**3,
            bytes_accessed=(len(arrays) + count) * 2 * width * width * 4,
            transcendentals=0,
        ),
    )(place, *arrays)


def owner_body(onsite, hop, couple, sigma_in, shifts, mode_weight):
    e_local = sigma_in.shape[0]
    width = onsite.shape[-1]
    energy_count = lax.axis_size("energy")
    mom_count = lax.axis_size("mom")
    total = e_local * energy_count
    axes = ("slab", "energy", "mom")
    slab = lax.axis_index("slab")
    z = lax.axis_index("energy")
    k = lax.axis_index("mom")
    y, x = slab // 2, slab % 2
    place = jnp.stack([y, x, z % 2]).astype(jnp.int32)
    active = k == x

    def device(yy, xx, zz, kk):
        return ((2 * yy + xx) * energy_count + zz) * mom_count + kk

    chips = [(yy, xx, zz) for yy in range(2) for xx in range(2) for zz in range(energy_count)]
    to_x = [(device(a, b, c, 1 - b), device(a, 1 - b, c, 1 - b)) for a, b, c in chips]
    to_y = [(device(a, b, c, b), device(1 - a, b, c, b)) for a, b, c in chips]
    to_far = [(device(a, b, c, 1 - b), device(1 - a, 1 - b, c, 1 - b)) for a, b, c in chips]

    def routes(*pairs):
        return [
            (device(*divmod(s, 2), zz, t % 2), device(*divmod(t, 2), zz, t % 2))
            for s, t in pairs
            for zz in range(energy_count)
        ]

    beside = [(device(a, b, c, b), device(a, b, c ^ 1, b)) for a, b, c in chips]
    siblings = [(device(a, b, c, d), device(a, b, c, 1 - d)) for a, b, c in chips for d in range(2)]
    gift = [(device(a, b, c, b), device(a, b, c, 1 - b)) for a, b, c in chips]

    def send(value, pairs):
        return lax.ppermute(value, axes, pairs)

    locals_ = jnp.stack([y, 1 - y])
    energies = -0.5 + ((z * e_local + locals_).astype(jnp.float32) + 0.5) / total
    smem = pl.BlockSpec(memory_space=pltpu.SMEM)
    vmem = pl.BlockSpec(memory_space=pltpu.VMEM)
    block_shape = jax.ShapeDtypeStruct((2, width, width), jnp.float32)
    b_own, b_other = pl.pallas_call(
        prepare_kernel,
        out_shape=[block_shape] * 2,
        in_specs=[smem, smem, vmem, vmem, vmem],
        out_specs=[vmem] * 2,
        compiler_params=pltpu.CompilerParams(vmem_limit_bytes=VMEM_BYTES),
    )(place, energies, onsite[0], hop[0, 0], sigma_in[:, 0])

    coupling = couple[0, 0]
    c_part = lax.dynamic_slice_in_dim(coupling, (z % 2) * (width // 2), width // 2, axis=1)
    far_mine = send(c_part, routes((1, 2), (2, 1), (3, 0)))
    c_x = send(coupling, routes((1, 0), (2, 3), (3, 2)))
    c_y = send(coupling, routes((1, 3), (2, 0), (3, 1)))
    far_mine, c_x, c_y = lax.optimization_barrier((far_mine, c_x, c_y))
    far_theirs = send(far_mine, beside)
    b_far = send(b_other, to_far)
    b_x = send(b_own, to_x)
    b_y = send(b_other, to_y)

    c_forms = pl.pallas_call(
        coupling_kernel,
        out_shape=jax.ShapeDtypeStruct((3, 2, 6, width, width), jnp.bfloat16),
        in_specs=[smem] + [vmem] * 5,
        out_specs=vmem,
        scratch_shapes=[pltpu.VMEM((2, width, width), jnp.float32)],
        compiler_params=pltpu.CompilerParams(vmem_limit_bytes=VMEM_BYTES),
    )(place, coupling, c_x, c_y, far_mine, far_theirs)
    shape = (4, width, width)
    keep, give = call(chain_kernel, place, (b_own, b_x, b_y, b_far, c_forms), shape, 2, 26)
    half = pl.pallas_call(
        pick_kernel,
        out_shape=jax.ShapeDtypeStruct(shape, jnp.float32),
        in_specs=[smem, vmem, vmem],
        out_specs=vmem,
        compiler_params=pltpu.CompilerParams(vmem_limit_bytes=VMEM_BYTES),
    )(active[None].astype(jnp.int32), keep, send(give, gift))

    rows = width // energy_count
    slots = 4 * energy_count
    parts = lax.all_to_all(
        half.reshape(slots, rows, width), ("slab", "energy"), 0, 0, tiled=True
    )
    phonon = phonon_matrix(shifts, mode_weight, total) / mom_count
    mixed = pl.pallas_call(
        mix_kernel,
        out_shape=jax.ShapeDtypeStruct((total, rows, width), jnp.float32),
        in_specs=[smem, vmem],
        out_specs=vmem,
        compiler_params=pltpu.CompilerParams(vmem_limit_bytes=VMEM_BYTES),
    )(phonon, parts)
    other = send(mixed, siblings)
    result = pl.pallas_call(
        join_kernel,
        grid=(total,),
        out_shape=jax.ShapeDtypeStruct((total, 2, rows, width), jnp.float32),
        in_specs=[smem, vmem, vmem],
        out_specs=pl.BlockSpec((1, 2, rows, width), lambda energy: (energy, 0, 0, 0)),
        compiler_params=pltpu.CompilerParams(vmem_limit_bytes=VMEM_BYTES),
    )(k[None].astype(jnp.int32), mixed, other)
    return result[:, None]


def solution(mesh):
    in_specs = (
        P("mom", "slab", None),
        P("mom", "slab", None, None, None),
        P("mom", "slab", None, None, None),
        P("energy", "slab", None, None, None),
        P(),
        P(),
    )
    out_specs = P(None, "slab", None, "energy", None)
    count = mesh.shape["energy"]

    def run(onsite, hop, couple, sigma_in, shifts, mode_weight):
        owned = (
            mesh.shape["slab"] == 4
            and mesh.shape["mom"] == 2
            and couple.shape[:2] == (2, 4)
            and sigma_in.shape[0] == 2 * count
            and count & (count - 1) == 0
        )
        inner = owner_body if owned else chain_body
        sharded = jax.shard_map(
            inner, mesh=mesh, in_specs=in_specs, out_specs=out_specs, check_vma=False
        )
        return sharded(onsite, hop, couple, sigma_in, shifts, mode_weight)

    return run
```

```python
import functools

import jax
import jax.numpy as jnp
from jax import lax
from jax.experimental import pallas as pl
from jax.experimental.pallas import tpu as pltpu
from jax.sharding import PartitionSpec as P

ETA = 0.5
HIGH = lax.Precision.HIGHEST


def shifted(shard, axis, by):
    length = lax.axis_size(axis)
    pairs = [(i, i + by) for i in range(length) if 0 <= i + by < length]
    return lax.ppermute(shard, axis, pairs)


def complex_mul(form, left, right):

    def product(first, second):
        return jnp.einsum(form, first, second, precision=HIGH)

    return (
        product(left[0], right[0]) - product(left[1], right[1]),
        product(left[0], right[1]) + product(left[1], right[0]),
    )


def newton_inverse(mat_real, mat_imag, form, identity):
    diag_real = jnp.diagonal(mat_real, axis1=-2, axis2=-1)
    diag_imag = jnp.diagonal(mat_imag, axis1=-2, axis2=-1)
    denom = diag_real * diag_real + diag_imag * diag_imag
    x_real = diag_real / denom
    x_imag = -diag_imag / denom
    rows_real = x_real[..., :, None] * mat_real - x_imag[..., :, None] * mat_imag
    rows_imag = x_real[..., :, None] * mat_imag + x_imag[..., :, None] * mat_real
    both_real = rows_real * x_real[..., None, :] - rows_imag * x_imag[..., None, :]
    both_imag = rows_real * x_imag[..., None, :] + rows_imag * x_real[..., None, :]
    first = (
        2.0 * identity * x_real[..., None, :] - both_real,
        2.0 * identity * x_imag[..., None, :] - both_imag,
    )
    resid = complex_mul(form, (mat_real, mat_imag), first)
    second = complex_mul(form, first, resid)
    return (2.0 * first[0] - second[0], 2.0 * first[1] - second[1])


def phonon_matrix(shifts, mode_weight, count):
    rows = jnp.arange(count)[:, None, None]
    cols = jnp.arange(count)[None, :, None]
    offset = shifts[None, None, :]
    upper = (cols == rows + offset).astype(jnp.float32)
    lower = (cols == rows - offset).astype(jnp.float32)
    return jnp.sum(upper * mode_weight[0] + lower * mode_weight[1], axis=2)


def chain_body(onsite, hop, couple, sigma_in, shifts, mode_weight):
    e_local = sigma_in.shape[0]
    width = onsite.shape[-1]
    slab_count = lax.axis_size("slab")
    slab_index = lax.axis_index("slab")
    energy_count = lax.axis_size("energy")
    mom_count = lax.axis_size("mom")
    total = e_local * energy_count
    identity = jnp.eye(width, dtype=jnp.float32)
    global_index = lax.axis_index("energy") * e_local + jnp.arange(e_local)
    energy = -0.5 + (global_index.astype(jnp.float32) + 0.5) / total
    coupling = (couple[0, 0, 0], couple[0, 0, 1])
    adjoint = (coupling[0].T, -coupling[1].T)
    hopping = (hop[0, 0, 0], hop[0, 0, 1])
    level = onsite[0, 0]
    sigma = sigma_in[:, 0]

    def forward(received, energies, sig):
        temp = complex_mul("ij,ejl->eil", coupling, (received[:, 0], received[:, 1]))
        left = complex_mul("eij,jl->eil", temp, adjoint)
        z_real = energies[:, None] - level[None, :]
        mat_real = identity * z_real[:, None, :] - hopping[0] - sig[:, 0] - left[0]
        mat_imag = identity * ETA - hopping[1] - sig[:, 1] - left[1]
        green = newton_inverse(mat_real, mat_imag, "eij,ejl->eil", identity)
        return jnp.stack(green, axis=1)

    def backward(green, received):
        pair = (green[:, 0], green[:, 1])
        temp = complex_mul("eij,ejl->eil", pair, (received[:, 0], received[:, 1]))
        extra = complex_mul("eij,ejl->eil", temp, pair)
        full = (pair[0] + extra[0], pair[1] + extra[1])
        temp = complex_mul("ij,ejl->eil", adjoint, full)
        coupled = complex_mul("eij,jl->eil", temp, coupling)
        return (jnp.stack(full, axis=1), jnp.stack(coupled, axis=1))

    empty = jnp.zeros((e_local, 2, width, width), jnp.float32)

    def forward_step(step, green_all):
        received = shifted(green_all, "slab", 1)
        return lax.cond(
            slab_index == step, lambda: forward(received, energy, sigma), lambda: green_all
        )

    green_all = lax.fori_loop(0, slab_count, forward_step, empty)

    def backward_step(step, carry):
        received = shifted(carry[1], "slab", -1)
        return lax.cond(
            slab_index == slab_count - 1 - step,
            lambda: backward(green_all, received),
            lambda: carry,
        )

    full_all, coupled_all = lax.fori_loop(0, slab_count, backward_step, (empty, empty))
    phonon = phonon_matrix(shifts, mode_weight, total)
    blocks = full_all[:, None]
    mixed = jnp.einsum(
        "ef,fsrjl->esrjl",
        phonon,
        lax.all_to_all(blocks, "energy", split_axis=3, concat_axis=0, tiled=True),
        precision=HIGH,
    )
    result = lax.psum(mixed, "mom") / mom_count
    return result


VMEM_BYTES = 24 * 1024 * 1024


BLOCKS = 4


def halves(value):
    high = value.astype(jnp.bfloat16)
    low = (value - high.astype(jnp.float32)).astype(jnp.bfloat16)
    return high, low


def form(pair):
    return halves(pair[0]), halves(pair[1]), halves(pair[0] + pair[1])


def real_dot(left, right):
    rows = left[0].shape[0]
    both = jnp.concatenate([left[0], left[1]], axis=0)
    main = jnp.dot(both, right[0], preferred_element_type=jnp.float32)
    rest = jnp.dot(left[0], right[1], preferred_element_type=jnp.float32)
    return main[:rows] + main[rows:] + rest


def mul(left, right):
    first = real_dot(left[0], right[0])
    second = real_dot(left[1], right[1])
    third = real_dot(left[2], right[2])
    return first - second, third - first - second


def mul_twice(blocks, right, last):
    inner = [mul(block, right) for block in blocks]
    return [mul(form(block), last) for block in inner]


def split_rows(pair):
    size = pair[0].shape[0] // BLOCKS
    return [tuple(part[b * size : (b + 1) * size] for part in pair) for b in range(BLOCKS)]


def join_rows(blocks):
    return tuple(jnp.concatenate([block[i] for block in blocks], axis=0) for i in range(2))


def form_rows(forms):
    return tuple(
        tuple(jnp.concatenate([f[plane][term] for f in forms], axis=0) for term in range(2))
        for plane in range(3)
    )


def read(ref):
    return ref[0], ref[1]


def write(ref, blocks):
    size = blocks[0][0].shape[0]
    for b, block in enumerate(blocks):
        ref[0, b * size : (b + 1) * size] = block[0]
        ref[1, b * size : (b + 1) * size] = block[1]


def choose(cond, left, right):
    return jnp.where(cond, left[0], right[0]), jnp.where(cond, left[1], right[1])


def times(left, right):
    return left[0] * right[0] - left[1] * right[1], left[0] * right[1] + left[1] * right[0]


def inverse(mats):
    size, width = mats[0][0].shape

    def invert(real, imag):
        denom = real * real + imag * imag
        return real / denom, -imag / denom

    eyes, scaled = [], []
    across = (0.0, 0.0)
    for b, mat in enumerate(mats):
        eye = lax.broadcasted_iota(jnp.int32, (size, width), 0) + b * size == (
            lax.broadcasted_iota(jnp.int32, (size, width), 1)
        )
        on = [jnp.where(eye, part, 0.0) for part in mat]
        off = [jnp.where(eye, 0.0, part) for part in mat]
        across = tuple(
            total + jnp.sum(part, axis=0, keepdims=True) for total, part in zip(across, on)
        )
        down = invert(*(jnp.sum(part, axis=1, keepdims=True) for part in on))
        eyes.append(eye)
        scaled.append(times(down, off))
    forms = [form(block) for block in scaled]
    right = form_rows(forms)
    squares = [mul(block, right) for block in forms]
    cubes = [mul(form(block), right) for block in squares]
    factor = invert(*across)
    out = []
    for eye, one, two, three in zip(eyes, scaled, squares, cubes):
        real = jnp.where(eye, 1.0, 0.0) - one[0] + two[0] - three[0]
        out.append(times((real, two[1] - one[1] - three[1]), factor))
    return out


def pick_block(y, x, slab, own, x_side, y_side, far):
    same_y = y == slab // 2
    same_x = x == slab % 2
    near = choose(same_x, read(own), read(x_side))
    away = choose(same_x, read(y_side), read(far))
    return choose(same_y, near, away)


def stored_form(ref, slab, side):
    at = (slab - 1, side)
    return tuple(tuple(ref[(*at, 2 * plane + term)] for term in range(2)) for plane in range(3))


def stored_rows(ref, slab, side):
    size = ref.shape[-2] // BLOCKS
    at = (slab - 1, side)
    return [
        tuple(
            tuple(ref[(*at, 2 * plane + term, slice(b * size, (b + 1) * size))] for term in range(2))
            for plane in range(3)
        )
        for b in range(BLOCKS)
    ]


def coupling_kernel(place, c_own, c_x, c_y, c_far, out_ref):
    y, x = place[0], place[1]
    for slab in (1, 2, 3):
        real, imag = pick_block(y, x, slab, c_own, c_x, c_y, c_far)
        for side, pair in enumerate(((real, imag), (real.T, -imag.T))):
            for plane, terms in enumerate(form(pair)):
                for term in range(2):
                    out_ref[slab - 1, side, 2 * plane + term] = terms[term]


def chain_kernel(place, b_own, b_x, b_y, b_far, c_forms, keep_ref, give_ref):
    y, x = place[0], place[1]
    greens, forms = [], []
    for slab in range(4):
        mats = split_rows(pick_block(y, x, slab, b_own, b_x, b_y, b_far))
        if slab:
            terms = mul_twice(
                stored_rows(c_forms, slab, 0), form_rows(forms[-1]), stored_form(c_forms, slab, 1)
            )
            mats = [(m[0] - t[0], m[1] - t[1]) for m, t in zip(mats, terms)]
        greens.append(inverse(mats))
        forms.append([form(block) for block in greens[-1]])

    def finish(slab, blocks):
        full = join_rows(blocks)
        keep_ref[slab] = jnp.where(x == 0, full[0], full[1])
        give_ref[slab] = jnp.where(x == 0, full[1], full[0])

    finish(3, greens[3])
    full_form = form_rows(forms[3])
    for slab in (2, 1, 0):
        coupled = mul_twice(
            stored_rows(c_forms, slab + 1, 1), full_form, stored_form(c_forms, slab + 1, 0)
        )
        coupled_form = form_rows([form(block) for block in coupled])
        extra = mul_twice(forms[slab], coupled_form, form_rows(forms[slab]))
        fulls = [(g[0] + e[0], g[1] + e[1]) for g, e in zip(greens[slab], extra)]
        finish(slab, fulls)
        if slab:
            full_form = form_rows([form(block) for block in fulls])


def mix_kernel(phonon, parts_ref, out_ref):
    slots, rows, _ = parts_ref.shape
    energies = out_ref.shape[0]
    planes, step = slots // 4, 8

    def source(slot):
        return 2 * (slot % planes) + slot // planes // 2

    for row in range(0, rows, step):
        here = slice(row, row + step)
        values = [None] * energies
        for slot in range(slots):
            value = parts_ref[slot, here, :]
            held = values[source(slot)]
            values[source(slot)] = value if held is None else held + value
        for energy in range(energies):
            total = phonon[energy, 0] * values[0]
            for other in range(1, energies):
                total = total + phonon[energy, other] * values[other]
            out_ref[energy, here, :] = total


def call(kernel, place, arrays, shape, count, products):
    width = arrays[0].shape[-1]
    vmem = pl.BlockSpec(memory_space=pltpu.VMEM)
    return pl.pallas_call(
        kernel,
        out_shape=[jax.ShapeDtypeStruct(shape, jnp.float32)] * count,
        in_specs=[pl.BlockSpec(memory_space=pltpu.SMEM)] + [vmem] * len(arrays),
        out_specs=[vmem] * count,
        compiler_params=pltpu.CompilerParams(vmem_limit_bytes=VMEM_BYTES),
        cost_estimate=pl.CostEstimate(
            flops=products * 9 * 2 * width**3,
            bytes_accessed=(len(arrays) + count) * 2 * width * width * 4,
            transcendentals=0,
        ),
    )(place, *arrays)


def owner_body(onsite, hop, couple, sigma_in, shifts, mode_weight):
    e_local = sigma_in.shape[0]
    width = onsite.shape[-1]
    energy_count = lax.axis_size("energy")
    mom_count = lax.axis_size("mom")
    total = e_local * energy_count
    axes = ("slab", "energy", "mom")
    slab = lax.axis_index("slab")
    z = lax.axis_index("energy")
    k = lax.axis_index("mom")
    y, x = slab // 2, slab % 2
    place = jnp.stack([y, x]).astype(jnp.int32)
    active = k == x

    def device(yy, xx, zz, kk):
        return ((2 * yy + xx) * energy_count + zz) * mom_count + kk

    chips = [(yy, xx, zz) for yy in range(2) for xx in range(2) for zz in range(energy_count)]
    to_x = [(device(a, b, c, 1 - b), device(a, 1 - b, c, 1 - b)) for a, b, c in chips]
    to_y = [(device(a, b, c, b), device(1 - a, b, c, b)) for a, b, c in chips]
    to_far = [(device(a, b, c, 1 - b), device(1 - a, 1 - b, c, 1 - b)) for a, b, c in chips]

    def routes(*pairs):
        return [
            (device(*divmod(s, 2), zz, t % 2), device(*divmod(t, 2), zz, t % 2))
            for s, t in pairs
            for zz in range(energy_count)
        ]

    siblings = [(device(a, b, c, d), device(a, b, c, 1 - d)) for a, b, c in chips for d in range(2)]
    gift = [(device(a, b, c, b), device(a, b, c, 1 - b)) for a, b, c in chips]

    def send(value, pairs):
        return lax.ppermute(value, axes, pairs)

    smem = pl.BlockSpec(memory_space=pltpu.SMEM)
    vmem = pl.BlockSpec(memory_space=pltpu.VMEM)
    eye = jnp.eye(width, dtype=bool)

    def block(local):
        index = (z * e_local + local).astype(jnp.float32)
        energy = -0.5 + (index + 0.5) / total
        sigma = lax.dynamic_index_in_dim(sigma_in[:, 0], local, 0, keepdims=False)
        real = jnp.where(eye, (energy - onsite[0, 0])[None, :], 0.0) - hop[0, 0, 0] - sigma[0]
        imag = jnp.where(eye, ETA, 0.0) - hop[0, 0, 1] - sigma[1]
        return jnp.stack([real, imag])

    b_other, b_own = block(1 - y), block(y)
    coupling = couple[0, 0]
    c_x = send(coupling, routes((1, 0), (2, 3), (3, 2)))
    c_y = send(coupling, routes((1, 3), (2, 0), (3, 1)))
    c_far = send(coupling, routes((1, 2), (2, 1), (3, 0)))
    b_far = send(b_other, to_far)
    b_x = send(b_own, to_x)
    b_y = send(lax.optimization_barrier((b_other, c_y))[0], to_y)

    c_forms = pl.pallas_call(
        coupling_kernel,
        out_shape=jax.ShapeDtypeStruct((3, 2, 6, width, width), jnp.bfloat16),
        in_specs=[smem] + [vmem] * 4,
        out_specs=vmem,
        compiler_params=pltpu.CompilerParams(vmem_limit_bytes=VMEM_BYTES),
    )(place, coupling, c_x, c_y, c_far)
    shape = (4, width, width)
    keep, give = call(chain_kernel, place, (b_own, b_x, b_y, b_far, c_forms), shape, 2, 26)
    half = jnp.where(active, keep, send(give, gift))

    rows = width // energy_count
    slots = 4 * energy_count
    parts = lax.all_to_all(
        half.reshape(slots, rows, width), ("slab", "energy"), 0, 0, tiled=True
    )
    phonon = phonon_matrix(shifts, mode_weight, total) / mom_count
    mixed = pl.pallas_call(
        mix_kernel,
        out_shape=jax.ShapeDtypeStruct((total, rows, width), jnp.float32),
        in_specs=[smem, vmem],
        out_specs=vmem,
        compiler_params=pltpu.CompilerParams(vmem_limit_bytes=VMEM_BYTES),
    )(phonon, parts)
    other = send(mixed, siblings)
    mine = jnp.arange(2)[:, None, None] == k
    result = jnp.where(mine, mixed[:, None], other[:, None])
    return result[:, None]


def solution(mesh):
    in_specs = (
        P("mom", "slab", None),
        P("mom", "slab", None, None, None),
        P("mom", "slab", None, None, None),
        P("energy", "slab", None, None, None),
        P(),
        P(),
    )
    out_specs = P(None, "slab", None, "energy", None)
    count = mesh.shape["energy"]

    def run(onsite, hop, couple, sigma_in, shifts, mode_weight):
        owned = (
            mesh.shape["slab"] == 4
            and mesh.shape["mom"] == 2
            and couple.shape[:2] == (2, 4)
            and sigma_in.shape[0] == 2 * count
            and count & (count - 1) == 0
        )
        inner = owner_body if owned else chain_body
        sharded = jax.shard_map(
            inner, mesh=mesh, in_specs=in_specs, out_specs=out_specs, check_vma=False
        )
        return sharded(onsite, hop, couple, sigma_in, shifts, mode_weight)

    return run
```

```python
import functools

import jax
import jax.numpy as jnp
from jax import lax
from jax.experimental import pallas as pl
from jax.experimental.pallas import tpu as pltpu
from jax.sharding import PartitionSpec as P

ETA = 0.5
HIGH = lax.Precision.HIGHEST


def shifted(shard, axis, by):
    length = lax.axis_size(axis)
    pairs = [(i, i + by) for i in range(length) if 0 <= i + by < length]
    return lax.ppermute(shard, axis, pairs)


def complex_mul(form, left, right):

    def product(first, second):
        return jnp.einsum(form, first, second, precision=HIGH)

    return (
        product(left[0], right[0]) - product(left[1], right[1]),
        product(left[0], right[1]) + product(left[1], right[0]),
    )


def newton_inverse(mat_real, mat_imag, form, identity):
    diag_real = jnp.diagonal(mat_real, axis1=-2, axis2=-1)
    diag_imag = jnp.diagonal(mat_imag, axis1=-2, axis2=-1)
    denom = diag_real * diag_real + diag_imag * diag_imag
    x_real = diag_real / denom
    x_imag = -diag_imag / denom
    rows_real = x_real[..., :, None] * mat_real - x_imag[..., :, None] * mat_imag
    rows_imag = x_real[..., :, None] * mat_imag + x_imag[..., :, None] * mat_real
    both_real = rows_real * x_real[..., None, :] - rows_imag * x_imag[..., None, :]
    both_imag = rows_real * x_imag[..., None, :] + rows_imag * x_real[..., None, :]
    first = (
        2.0 * identity * x_real[..., None, :] - both_real,
        2.0 * identity * x_imag[..., None, :] - both_imag,
    )
    resid = complex_mul(form, (mat_real, mat_imag), first)
    second = complex_mul(form, first, resid)
    return (2.0 * first[0] - second[0], 2.0 * first[1] - second[1])


def phonon_matrix(shifts, mode_weight, count):
    rows = jnp.arange(count)[:, None, None]
    cols = jnp.arange(count)[None, :, None]
    offset = shifts[None, None, :]
    upper = (cols == rows + offset).astype(jnp.float32)
    lower = (cols == rows - offset).astype(jnp.float32)
    return jnp.sum(upper * mode_weight[0] + lower * mode_weight[1], axis=2)


def chain_body(onsite, hop, couple, sigma_in, shifts, mode_weight):
    e_local = sigma_in.shape[0]
    width = onsite.shape[-1]
    slab_count = lax.axis_size("slab")
    slab_index = lax.axis_index("slab")
    energy_count = lax.axis_size("energy")
    mom_count = lax.axis_size("mom")
    total = e_local * energy_count
    identity = jnp.eye(width, dtype=jnp.float32)
    global_index = lax.axis_index("energy") * e_local + jnp.arange(e_local)
    energy = -0.5 + (global_index.astype(jnp.float32) + 0.5) / total
    coupling = (couple[0, 0, 0], couple[0, 0, 1])
    adjoint = (coupling[0].T, -coupling[1].T)
    hopping = (hop[0, 0, 0], hop[0, 0, 1])
    level = onsite[0, 0]
    sigma = sigma_in[:, 0]

    def forward(received, energies, sig):
        temp = complex_mul("ij,ejl->eil", coupling, (received[:, 0], received[:, 1]))
        left = complex_mul("eij,jl->eil", temp, adjoint)
        z_real = energies[:, None] - level[None, :]
        mat_real = identity * z_real[:, None, :] - hopping[0] - sig[:, 0] - left[0]
        mat_imag = identity * ETA - hopping[1] - sig[:, 1] - left[1]
        green = newton_inverse(mat_real, mat_imag, "eij,ejl->eil", identity)
        return jnp.stack(green, axis=1)

    def backward(green, received):
        pair = (green[:, 0], green[:, 1])
        temp = complex_mul("eij,ejl->eil", pair, (received[:, 0], received[:, 1]))
        extra = complex_mul("eij,ejl->eil", temp, pair)
        full = (pair[0] + extra[0], pair[1] + extra[1])
        temp = complex_mul("ij,ejl->eil", adjoint, full)
        coupled = complex_mul("eij,jl->eil", temp, coupling)
        return (jnp.stack(full, axis=1), jnp.stack(coupled, axis=1))

    empty = jnp.zeros((e_local, 2, width, width), jnp.float32)

    def forward_step(step, green_all):
        received = shifted(green_all, "slab", 1)
        return lax.cond(
            slab_index == step, lambda: forward(received, energy, sigma), lambda: green_all
        )

    green_all = lax.fori_loop(0, slab_count, forward_step, empty)

    def backward_step(step, carry):
        received = shifted(carry[1], "slab", -1)
        return lax.cond(
            slab_index == slab_count - 1 - step,
            lambda: backward(green_all, received),
            lambda: carry,
        )

    full_all, coupled_all = lax.fori_loop(0, slab_count, backward_step, (empty, empty))
    phonon = phonon_matrix(shifts, mode_weight, total)
    blocks = full_all[:, None]
    mixed = jnp.einsum(
        "ef,fsrjl->esrjl",
        phonon,
        lax.all_to_all(blocks, "energy", split_axis=3, concat_axis=0, tiled=True),
        precision=HIGH,
    )
    result = lax.psum(mixed, "mom") / mom_count
    return result


VMEM_BYTES = 24 * 1024 * 1024


BLOCKS = 1


def halves(value):
    high = value.astype(jnp.bfloat16)
    low = (value - high.astype(jnp.float32)).astype(jnp.bfloat16)
    return high, low


def form(pair):
    return halves(pair[0]), halves(pair[1]), halves(pair[0] + pair[1])


def real_dot(left, right):
    rows = left[0].shape[0]
    both = jnp.concatenate([left[0], left[1]], axis=0)
    main = jnp.dot(both, right[0], preferred_element_type=jnp.float32)
    rest = jnp.dot(left[0], right[1], preferred_element_type=jnp.float32)
    return main[:rows] + main[rows:] + rest


def mul(left, right):
    first = real_dot(left[0], right[0])
    second = real_dot(left[1], right[1])
    third = real_dot(left[2], right[2])
    return first - second, third - first - second


def mul_twice(blocks, right, last):
    inner = [mul(block, right) for block in blocks]
    return [mul(form(block), last) for block in inner]


def split_rows(pair):
    size = pair[0].shape[0] // BLOCKS
    return [tuple(part[b * size : (b + 1) * size] for part in pair) for b in range(BLOCKS)]


def join_rows(blocks):
    return tuple(jnp.concatenate([block[i] for block in blocks], axis=0) for i in range(2))


def form_rows(forms):
    return tuple(
        tuple(jnp.concatenate([f[plane][term] for f in forms], axis=0) for term in range(2))
        for plane in range(3)
    )


def read(ref):
    return ref[0], ref[1]


def write(ref, blocks):
    size = blocks[0][0].shape[0]
    for b, block in enumerate(blocks):
        ref[0, b * size : (b + 1) * size] = block[0]
        ref[1, b * size : (b + 1) * size] = block[1]


def choose(cond, left, right):
    return jnp.where(cond, left[0], right[0]), jnp.where(cond, left[1], right[1])


def times(left, right):
    return left[0] * right[0] - left[1] * right[1], left[0] * right[1] + left[1] * right[0]


def inverse(mats):
    size, width = mats[0][0].shape

    def invert(real, imag):
        denom = real * real + imag * imag
        return real / denom, -imag / denom

    eyes, scaled = [], []
    across = (0.0, 0.0)
    for b, mat in enumerate(mats):
        eye = lax.broadcasted_iota(jnp.int32, (size, width), 0) + b * size == (
            lax.broadcasted_iota(jnp.int32, (size, width), 1)
        )
        on = [jnp.where(eye, part, 0.0) for part in mat]
        off = [jnp.where(eye, 0.0, part) for part in mat]
        across = tuple(
            total + jnp.sum(part, axis=0, keepdims=True) for total, part in zip(across, on)
        )
        down = invert(*(jnp.sum(part, axis=1, keepdims=True) for part in on))
        eyes.append(eye)
        scaled.append(times(down, off))
    forms = [form(block) for block in scaled]
    right = form_rows(forms)
    squares = [mul(block, right) for block in forms]
    cubes = [mul(form(block), right) for block in squares]
    factor = invert(*across)
    out = []
    for eye, one, two, three in zip(eyes, scaled, squares, cubes):
        real = jnp.where(eye, 1.0, 0.0) - one[0] + two[0] - three[0]
        out.append(times((real, two[1] - one[1] - three[1]), factor))
    return out


def pick_block(y, x, slab, own, x_side, y_side, far):
    same_y = y == slab // 2
    same_x = x == slab % 2
    near = choose(same_x, read(own), read(x_side))
    away = choose(same_x, read(y_side), read(far))
    return choose(same_y, near, away)


def stored_form(ref, slab, side):
    at = (slab - 1, side)
    return tuple(tuple(ref[(*at, 2 * plane + term)] for term in range(2)) for plane in range(3))


def stored_rows(ref, slab, side):
    size = ref.shape[-2] // BLOCKS
    at = (slab - 1, side)
    return [
        tuple(
            tuple(ref[(*at, 2 * plane + term, slice(b * size, (b + 1) * size))] for term in range(2))
            for plane in range(3)
        )
        for b in range(BLOCKS)
    ]


def coupling_kernel(place, c_own, c_x, c_y, far, out_ref):
    y, x = place[0], place[1]
    c_far = far.at[2:]
    for slab in (1, 2, 3):
        real, imag = pick_block(y, x, slab, c_own, c_x, c_y, c_far)
        for side, pair in enumerate(((real, imag), (real.T, -imag.T))):
            for plane, terms in enumerate(form(pair)):
                for term in range(2):
                    out_ref[slab - 1, side, 2 * plane + term] = terms[term]


def chain_kernel(place, b_own, b_x, b_y, b_far, c_forms, keep_ref, give_ref):
    y, x = place[0], place[1]
    greens, forms = [], []
    for slab in range(4):
        mats = split_rows(pick_block(y, x, slab, b_own, b_x, b_y, b_far))
        if slab:
            terms = mul_twice(
                stored_rows(c_forms, slab, 0), form_rows(forms[-1]), stored_form(c_forms, slab, 1)
            )
            mats = [(m[0] - t[0], m[1] - t[1]) for m, t in zip(mats, terms)]
        greens.append(inverse(mats))
        forms.append([form(block) for block in greens[-1]])

    def finish(slab, blocks):
        full = join_rows(blocks)
        keep_ref[slab] = jnp.where(x == 0, full[0], full[1])
        give_ref[slab] = jnp.where(x == 0, full[1], full[0])

    finish(3, greens[3])
    full_form = form_rows(forms[3])
    for slab in (2, 1, 0):
        coupled = mul_twice(
            stored_rows(c_forms, slab + 1, 1), full_form, stored_form(c_forms, slab + 1, 0)
        )
        coupled_form = form_rows([form(block) for block in coupled])
        extra = mul_twice(forms[slab], coupled_form, form_rows(forms[slab]))
        fulls = [(g[0] + e[0], g[1] + e[1]) for g, e in zip(greens[slab], extra)]
        finish(slab, fulls)
        if slab:
            full_form = form_rows([form(block) for block in fulls])


def mix_kernel(phonon, parts_ref, out_ref):
    slots, rows, _ = parts_ref.shape
    energies = out_ref.shape[0]
    planes, step = slots // 4, 8

    def source(slot):
        return 2 * (slot % planes) + slot // planes // 2

    for row in range(0, rows, step):
        here = slice(row, row + step)
        values = [None] * energies
        for slot in range(slots):
            value = parts_ref[slot, here, :]
            held = values[source(slot)]
            values[source(slot)] = value if held is None else held + value
        for energy in range(energies):
            total = phonon[energy, 0] * values[0]
            for other in range(1, energies):
                total = total + phonon[energy, other] * values[other]
            out_ref[energy, here, :] = total


def call(kernel, place, arrays, shape, count, products):
    width = arrays[0].shape[-1]
    vmem = pl.BlockSpec(memory_space=pltpu.VMEM)
    return pl.pallas_call(
        kernel,
        out_shape=[jax.ShapeDtypeStruct(shape, jnp.float32)] * count,
        in_specs=[pl.BlockSpec(memory_space=pltpu.SMEM)] + [vmem] * len(arrays),
        out_specs=[vmem] * count,
        compiler_params=pltpu.CompilerParams(vmem_limit_bytes=VMEM_BYTES),
        cost_estimate=pl.CostEstimate(
            flops=products * 9 * 2 * width**3,
            bytes_accessed=(len(arrays) + count) * 2 * width * width * 4,
            transcendentals=0,
        ),
    )(place, *arrays)


def owner_body(onsite, hop, couple, sigma_in, shifts, mode_weight):
    e_local = sigma_in.shape[0]
    width = onsite.shape[-1]
    energy_count = lax.axis_size("energy")
    mom_count = lax.axis_size("mom")
    total = e_local * energy_count
    axes = ("slab", "energy", "mom")
    slab = lax.axis_index("slab")
    z = lax.axis_index("energy")
    k = lax.axis_index("mom")
    y, x = slab // 2, slab % 2
    place = jnp.stack([y, x]).astype(jnp.int32)
    active = k == x

    def device(yy, xx, zz, kk):
        return ((2 * yy + xx) * energy_count + zz) * mom_count + kk

    chips = [(yy, xx, zz) for yy in range(2) for xx in range(2) for zz in range(energy_count)]
    to_x = [(device(a, b, c, 1 - b), device(a, 1 - b, c, 1 - b)) for a, b, c in chips]
    to_y = [(device(a, b, c, b), device(1 - a, b, c, b)) for a, b, c in chips]
    to_far = [(device(a, b, c, 1 - b), device(1 - a, 1 - b, c, 1 - b)) for a, b, c in chips]

    def routes(*pairs):
        return [
            (device(*divmod(s, 2), zz, t % 2), device(*divmod(t, 2), zz, t % 2))
            for s, t in pairs
            for zz in range(energy_count)
        ]

    siblings = [(device(a, b, c, d), device(a, b, c, 1 - d)) for a, b, c in chips for d in range(2)]
    gift = [(device(a, b, c, b), device(a, b, c, 1 - b)) for a, b, c in chips]

    def send(value, pairs):
        return lax.ppermute(value, axes, pairs)

    smem = pl.BlockSpec(memory_space=pltpu.SMEM)
    vmem = pl.BlockSpec(memory_space=pltpu.VMEM)
    eye = jnp.eye(width, dtype=bool)

    def block(local):
        index = (z * e_local + local).astype(jnp.float32)
        energy = -0.5 + (index + 0.5) / total
        sigma = lax.dynamic_index_in_dim(sigma_in[:, 0], local, 0, keepdims=False)
        real = jnp.where(eye, (energy - onsite[0, 0])[None, :], 0.0) - hop[0, 0, 0] - sigma[0]
        imag = jnp.where(eye, ETA, 0.0) - hop[0, 0, 1] - sigma[1]
        return jnp.stack([real, imag])

    b_other, b_own = block(1 - y), block(y)
    coupling = couple[0, 0]
    c_x = send(coupling, routes((1, 0), (2, 3), (3, 2)))
    c_y = send(coupling, routes((1, 3), (2, 0), (3, 1)))
    far = send(jnp.concatenate([b_other, coupling]), to_far)
    b_x = send(b_own, to_x)
    b_y = send(b_other, to_y)

    c_forms = pl.pallas_call(
        coupling_kernel,
        out_shape=jax.ShapeDtypeStruct((3, 2, 6, width, width), jnp.bfloat16),
        in_specs=[smem] + [vmem] * 4,
        out_specs=vmem,
        compiler_params=pltpu.CompilerParams(vmem_limit_bytes=VMEM_BYTES),
    )(place, coupling, c_x, c_y, far)
    shape = (4, width, width)
    keep, give = call(chain_kernel, place, (b_own, b_x, b_y, far, c_forms), shape, 2, 26)
    half = jnp.where(active, keep, send(give, gift))

    rows = width // energy_count
    slots = 4 * energy_count
    parts = lax.all_to_all(
        half.reshape(slots, rows, width), ("slab", "energy"), 0, 0, tiled=True
    )
    phonon = phonon_matrix(shifts, mode_weight, total) / mom_count
    mixed = pl.pallas_call(
        mix_kernel,
        out_shape=jax.ShapeDtypeStruct((total, rows, width), jnp.float32),
        in_specs=[smem, vmem],
        out_specs=vmem,
        compiler_params=pltpu.CompilerParams(vmem_limit_bytes=VMEM_BYTES),
    )(phonon, parts)
    other = send(mixed, siblings)
    mine = jnp.arange(2)[:, None, None] == k
    result = jnp.where(mine, mixed[:, None], other[:, None])
    return result[:, None]


def solution(mesh):
    in_specs = (
        P("mom", "slab", None),
        P("mom", "slab", None, None, None),
        P("mom", "slab", None, None, None),
        P("energy", "slab", None, None, None),
        P(),
        P(),
    )
    out_specs = P(None, "slab", None, "energy", None)
    count = mesh.shape["energy"]

    def run(onsite, hop, couple, sigma_in, shifts, mode_weight):
        owned = (
            mesh.shape["slab"] == 4
            and mesh.shape["mom"] == 2
            and couple.shape[:2] == (2, 4)
            and sigma_in.shape[0] == 2 * count
            and count & (count - 1) == 0
        )
        inner = owner_body if owned else chain_body
        sharded = jax.shard_map(
            inner, mesh=mesh, in_specs=in_specs, out_specs=out_specs, check_vma=False
        )
        return sharded(onsite, hop, couple, sigma_in, shifts, mode_weight)

    return run
```

```python
import functools

import jax
import jax.numpy as jnp
from jax import lax
from jax.experimental import pallas as pl
from jax.experimental.pallas import tpu as pltpu
from jax.sharding import PartitionSpec as P

ETA = 0.5
HIGH = lax.Precision.HIGHEST


def shifted(shard, axis, by):
    length = lax.axis_size(axis)
    pairs = [(i, i + by) for i in range(length) if 0 <= i + by < length]
    return lax.ppermute(shard, axis, pairs)


def complex_mul(form, left, right):

    def product(first, second):
        return jnp.einsum(form, first, second, precision=HIGH)

    return (
        product(left[0], right[0]) - product(left[1], right[1]),
        product(left[0], right[1]) + product(left[1], right[0]),
    )


def newton_inverse(mat_real, mat_imag, form, identity):
    diag_real = jnp.diagonal(mat_real, axis1=-2, axis2=-1)
    diag_imag = jnp.diagonal(mat_imag, axis1=-2, axis2=-1)
    denom = diag_real * diag_real + diag_imag * diag_imag
    x_real = diag_real / denom
    x_imag = -diag_imag / denom
    rows_real = x_real[..., :, None] * mat_real - x_imag[..., :, None] * mat_imag
    rows_imag = x_real[..., :, None] * mat_imag + x_imag[..., :, None] * mat_real
    both_real = rows_real * x_real[..., None, :] - rows_imag * x_imag[..., None, :]
    both_imag = rows_real * x_imag[..., None, :] + rows_imag * x_real[..., None, :]
    first = (
        2.0 * identity * x_real[..., None, :] - both_real,
        2.0 * identity * x_imag[..., None, :] - both_imag,
    )
    resid = complex_mul(form, (mat_real, mat_imag), first)
    second = complex_mul(form, first, resid)
    return (2.0 * first[0] - second[0], 2.0 * first[1] - second[1])


def phonon_matrix(shifts, mode_weight, count):
    rows = jnp.arange(count)[:, None, None]
    cols = jnp.arange(count)[None, :, None]
    offset = shifts[None, None, :]
    upper = (cols == rows + offset).astype(jnp.float32)
    lower = (cols == rows - offset).astype(jnp.float32)
    return jnp.sum(upper * mode_weight[0] + lower * mode_weight[1], axis=2)


def chain_body(onsite, hop, couple, sigma_in, shifts, mode_weight):
    e_local = sigma_in.shape[0]
    width = onsite.shape[-1]
    slab_count = lax.axis_size("slab")
    slab_index = lax.axis_index("slab")
    energy_count = lax.axis_size("energy")
    mom_count = lax.axis_size("mom")
    total = e_local * energy_count
    identity = jnp.eye(width, dtype=jnp.float32)
    global_index = lax.axis_index("energy") * e_local + jnp.arange(e_local)
    energy = -0.5 + (global_index.astype(jnp.float32) + 0.5) / total
    coupling = (couple[0, 0, 0], couple[0, 0, 1])
    adjoint = (coupling[0].T, -coupling[1].T)
    hopping = (hop[0, 0, 0], hop[0, 0, 1])
    level = onsite[0, 0]
    sigma = sigma_in[:, 0]

    def forward(received, energies, sig):
        temp = complex_mul("ij,ejl->eil", coupling, (received[:, 0], received[:, 1]))
        left = complex_mul("eij,jl->eil", temp, adjoint)
        z_real = energies[:, None] - level[None, :]
        mat_real = identity * z_real[:, None, :] - hopping[0] - sig[:, 0] - left[0]
        mat_imag = identity * ETA - hopping[1] - sig[:, 1] - left[1]
        green = newton_inverse(mat_real, mat_imag, "eij,ejl->eil", identity)
        return jnp.stack(green, axis=1)

    def backward(green, received):
        pair = (green[:, 0], green[:, 1])
        temp = complex_mul("eij,ejl->eil", pair, (received[:, 0], received[:, 1]))
        extra = complex_mul("eij,ejl->eil", temp, pair)
        full = (pair[0] + extra[0], pair[1] + extra[1])
        temp = complex_mul("ij,ejl->eil", adjoint, full)
        coupled = complex_mul("eij,jl->eil", temp, coupling)
        return (jnp.stack(full, axis=1), jnp.stack(coupled, axis=1))

    empty = jnp.zeros((e_local, 2, width, width), jnp.float32)

    def forward_step(step, green_all):
        received = shifted(green_all, "slab", 1)
        return lax.cond(
            slab_index == step, lambda: forward(received, energy, sigma), lambda: green_all
        )

    green_all = lax.fori_loop(0, slab_count, forward_step, empty)

    def backward_step(step, carry):
        received = shifted(carry[1], "slab", -1)
        return lax.cond(
            slab_index == slab_count - 1 - step,
            lambda: backward(green_all, received),
            lambda: carry,
        )

    full_all, coupled_all = lax.fori_loop(0, slab_count, backward_step, (empty, empty))
    phonon = phonon_matrix(shifts, mode_weight, total)
    blocks = full_all[:, None]
    mixed = jnp.einsum(
        "ef,fsrjl->esrjl",
        phonon,
        lax.all_to_all(blocks, "energy", split_axis=3, concat_axis=0, tiled=True),
        precision=HIGH,
    )
    result = lax.psum(mixed, "mom") / mom_count
    return result


VMEM_BYTES = 24 * 1024 * 1024


BLOCKS = 2


def halves(value):
    high = value.astype(jnp.bfloat16)
    low = (value - high.astype(jnp.float32)).astype(jnp.bfloat16)
    return high, low


def form(pair):
    return halves(pair[0]), halves(pair[1]), halves(pair[0] + pair[1])


def real_dot(left, right):
    rows = left[0].shape[0]
    both = jnp.concatenate([left[0], left[1]], axis=0)
    main = jnp.dot(both, right[0], preferred_element_type=jnp.float32)
    rest = jnp.dot(left[0], right[1], preferred_element_type=jnp.float32)
    return main[:rows] + main[rows:] + rest


def mul(left, right):
    first = real_dot(left[0], right[0])
    second = real_dot(left[1], right[1])
    third = real_dot(left[2], right[2])
    return first - second, third - first - second


def mul_twice(blocks, right, last):
    inner = mul(form_rows(blocks), right)
    return [mul(form(block), last) for block in split_rows(inner)]


def split_rows(pair):
    size = pair[0].shape[0] // BLOCKS
    return [tuple(part[b * size : (b + 1) * size] for part in pair) for b in range(BLOCKS)]


def join_rows(blocks):
    return tuple(jnp.concatenate([block[i] for block in blocks], axis=0) for i in range(2))


def form_rows(forms):
    return tuple(
        tuple(jnp.concatenate([f[plane][term] for f in forms], axis=0) for term in range(2))
        for plane in range(3)
    )


def read(ref):
    return ref[0], ref[1]


def write(ref, blocks):
    size = blocks[0][0].shape[0]
    for b, block in enumerate(blocks):
        ref[0, b * size : (b + 1) * size] = block[0]
        ref[1, b * size : (b + 1) * size] = block[1]


def choose(cond, left, right):
    return jnp.where(cond, left[0], right[0]), jnp.where(cond, left[1], right[1])


def times(left, right):
    return left[0] * right[0] - left[1] * right[1], left[0] * right[1] + left[1] * right[0]


def inverse(mats):
    size, width = mats[0][0].shape

    def invert(real, imag):
        denom = real * real + imag * imag
        return real / denom, -imag / denom

    eyes, scaled = [], []
    across = (0.0, 0.0)
    for b, mat in enumerate(mats):
        eye = lax.broadcasted_iota(jnp.int32, (size, width), 0) + b * size == (
            lax.broadcasted_iota(jnp.int32, (size, width), 1)
        )
        on = [jnp.where(eye, part, 0.0) for part in mat]
        off = [jnp.where(eye, 0.0, part) for part in mat]
        across = tuple(
            total + jnp.sum(part, axis=0, keepdims=True) for total, part in zip(across, on)
        )
        down = invert(*(jnp.sum(part, axis=1, keepdims=True) for part in on))
        eyes.append(eye)
        scaled.append(times(down, off))
    forms = [form(block) for block in scaled]
    right = form_rows(forms)
    squares = split_rows(mul(right, right))
    cubes = [mul(form(block), right) for block in squares]
    factor = invert(*across)
    out = []
    for eye, one, two, three in zip(eyes, scaled, squares, cubes):
        real = jnp.where(eye, 1.0, 0.0) - one[0] + two[0] - three[0]
        out.append(times((real, two[1] - one[1] - three[1]), factor))
    return out


def pick_block(y, x, slab, own, x_side, y_side, far):
    same_y = y == slab // 2
    same_x = x == slab % 2
    near = choose(same_x, read(own), read(x_side))
    away = choose(same_x, read(y_side), read(far))
    return choose(same_y, near, away)


def stored_form(ref, slab, side):
    at = (slab - 1, side)
    return tuple(tuple(ref[(*at, 2 * plane + term)] for term in range(2)) for plane in range(3))


def stored_rows(ref, slab, side):
    size = ref.shape[-2] // BLOCKS
    at = (slab - 1, side)
    return [
        tuple(
            tuple(ref[(*at, 2 * plane + term, slice(b * size, (b + 1) * size))] for term in range(2))
            for plane in range(3)
        )
        for b in range(BLOCKS)
    ]


def coupling_kernel(place, c_own, c_x, c_y, far_mine, far_theirs, out_ref, c_far):
    y, x = place[0], place[1]
    first, rows = place[2] == 0, far_mine.shape[1]
    for part in range(2):
        mine, theirs = far_mine[part], far_theirs[part]
        c_far[part, :rows] = jnp.where(first, mine, theirs)
        c_far[part, rows:] = jnp.where(first, theirs, mine)
    for slab in (1, 2, 3):
        real, imag = pick_block(y, x, slab, c_own, c_x, c_y, c_far)
        for side, pair in enumerate(((real, imag), (real.T, -imag.T))):
            for plane, terms in enumerate(form(pair)):
                for term in range(2):
                    out_ref[slab - 1, side, 2 * plane + term] = terms[term]


def chain_kernel(place, b_own, b_x, b_y, b_far, c_forms, keep_ref, give_ref):
    y, x = place[0], place[1]
    greens, forms = [], []
    for slab in range(4):
        mats = split_rows(pick_block(y, x, slab, b_own, b_x, b_y, b_far))
        if slab:
            terms = mul_twice(
                stored_rows(c_forms, slab, 0), form_rows(forms[-1]), stored_form(c_forms, slab, 1)
            )
            mats = [(m[0] - t[0], m[1] - t[1]) for m, t in zip(mats, terms)]
        greens.append(inverse(mats))
        forms.append([form(block) for block in greens[-1]])

    def finish(slab, blocks):
        full = join_rows(blocks)
        keep_ref[slab] = jnp.where(x == 0, full[0], full[1])
        give_ref[slab] = jnp.where(x == 0, full[1], full[0])

    finish(3, greens[3])
    full_form = form_rows(forms[3])
    for slab in (2, 1, 0):
        coupled = mul_twice(
            stored_rows(c_forms, slab + 1, 1), full_form, stored_form(c_forms, slab + 1, 0)
        )
        coupled_form = form_rows([form(block) for block in coupled])
        extra = mul_twice(forms[slab], coupled_form, form_rows(forms[slab]))
        fulls = [(g[0] + e[0], g[1] + e[1]) for g, e in zip(greens[slab], extra)]
        finish(slab, fulls)
        if slab:
            full_form = form_rows([form(block) for block in fulls])


def mix_kernel(phonon, parts_ref, out_ref):
    slots, rows, _ = parts_ref.shape
    energies = out_ref.shape[0]
    planes, step = slots // 4, 8

    def source(slot):
        return 2 * (slot % planes) + slot // planes // 2

    for row in range(0, rows, step):
        here = slice(row, row + step)
        values = [None] * energies
        for slot in range(slots):
            value = parts_ref[slot, here, :]
            held = values[source(slot)]
            values[source(slot)] = value if held is None else held + value
        for energy in range(energies):
            total = phonon[energy, 0] * values[0]
            for other in range(1, energies):
                total = total + phonon[energy, other] * values[other]
            out_ref[energy, here, :] = total


def call(kernel, place, arrays, shape, count, products):
    width = arrays[0].shape[-1]
    vmem = pl.BlockSpec(memory_space=pltpu.VMEM)
    return pl.pallas_call(
        kernel,
        out_shape=[jax.ShapeDtypeStruct(shape, jnp.float32)] * count,
        in_specs=[pl.BlockSpec(memory_space=pltpu.SMEM)] + [vmem] * len(arrays),
        out_specs=[vmem] * count,
        compiler_params=pltpu.CompilerParams(vmem_limit_bytes=VMEM_BYTES),
        cost_estimate=pl.CostEstimate(
            flops=products * 9 * 2 * width**3,
            bytes_accessed=(len(arrays) + count) * 2 * width * width * 4,
            transcendentals=0,
        ),
    )(place, *arrays)


def owner_body(onsite, hop, couple, sigma_in, shifts, mode_weight):
    e_local = sigma_in.shape[0]
    width = onsite.shape[-1]
    energy_count = lax.axis_size("energy")
    mom_count = lax.axis_size("mom")
    total = e_local * energy_count
    axes = ("slab", "energy", "mom")
    slab = lax.axis_index("slab")
    z = lax.axis_index("energy")
    k = lax.axis_index("mom")
    y, x = slab // 2, slab % 2
    place = jnp.stack([y, x, z % 2]).astype(jnp.int32)
    active = k == x

    def device(yy, xx, zz, kk):
        return ((2 * yy + xx) * energy_count + zz) * mom_count + kk

    chips = [(yy, xx, zz) for yy in range(2) for xx in range(2) for zz in range(energy_count)]
    to_x = [(device(a, b, c, 1 - b), device(a, 1 - b, c, 1 - b)) for a, b, c in chips]
    to_y = [(device(a, b, c, b), device(1 - a, b, c, b)) for a, b, c in chips]
    to_far = [(device(a, b, c, 1 - b), device(1 - a, 1 - b, c, 1 - b)) for a, b, c in chips]

    def routes(*pairs):
        return [
            (device(*divmod(s, 2), zz, t % 2), device(*divmod(t, 2), zz, t % 2))
            for s, t in pairs
            for zz in range(energy_count)
        ]

    beside = [(device(a, b, c, b), device(a, b, c ^ 1, b)) for a, b, c in chips]
    siblings = [(device(a, b, c, d), device(a, b, c, 1 - d)) for a, b, c in chips for d in range(2)]
    gift = [(device(a, b, c, b), device(a, b, c, 1 - b)) for a, b, c in chips]

    def send(value, pairs):
        return lax.ppermute(value, axes, pairs)

    smem = pl.BlockSpec(memory_space=pltpu.SMEM)
    vmem = pl.BlockSpec(memory_space=pltpu.VMEM)
    eye = jnp.eye(width, dtype=bool)

    def block(local):
        index = (z * e_local + local).astype(jnp.float32)
        energy = -0.5 + (index + 0.5) / total
        sigma = lax.dynamic_index_in_dim(sigma_in[:, 0], local, 0, keepdims=False)
        real = jnp.where(eye, (energy - onsite[0, 0])[None, :], 0.0) - hop[0, 0, 0] - sigma[0]
        imag = jnp.where(eye, ETA, 0.0) - hop[0, 0, 1] - sigma[1]
        return jnp.stack([real, imag])

    b_other, b_own = block(1 - y), block(y)
    coupling = couple[0, 0]
    c_part = lax.dynamic_slice_in_dim(coupling, (z % 2) * (width // 2), width // 2, axis=1)
    far_mine = send(c_part, routes((1, 2), (2, 1), (3, 0)))
    c_x = send(coupling, routes((1, 0), (2, 3), (3, 2)))
    c_y = send(coupling, routes((1, 3), (2, 0), (3, 1)))
    far_mine, c_x, c_y = lax.optimization_barrier((far_mine, c_x, c_y))
    far_theirs = send(far_mine, beside)
    b_far = send(b_other, to_far)
    b_x = send(b_own, to_x)
    b_y = send(b_other, to_y)

    c_forms = pl.pallas_call(
        coupling_kernel,
        out_shape=jax.ShapeDtypeStruct((3, 2, 6, width, width), jnp.bfloat16),
        in_specs=[smem] + [vmem] * 5,
        out_specs=vmem,
        scratch_shapes=[pltpu.VMEM((2, width, width), jnp.float32)],
        compiler_params=pltpu.CompilerParams(vmem_limit_bytes=VMEM_BYTES),
    )(place, coupling, c_x, c_y, far_mine, far_theirs)
    shape = (4, width, width)
    keep, give = call(chain_kernel, place, (b_own, b_x, b_y, b_far, c_forms), shape, 2, 26)
    half = jnp.where(active, keep, send(give, gift))

    rows = width // energy_count
    slots = 4 * energy_count
    parts = lax.all_to_all(
        half.reshape(slots, rows, width), ("slab", "energy"), 0, 0, tiled=True
    )
    phonon = phonon_matrix(shifts, mode_weight, total) / mom_count
    mixed = pl.pallas_call(
        mix_kernel,
        out_shape=jax.ShapeDtypeStruct((total, rows, width), jnp.float32),
        in_specs=[smem, vmem],
        out_specs=vmem,
        compiler_params=pltpu.CompilerParams(vmem_limit_bytes=VMEM_BYTES),
    )(phonon, parts)
    other = send(mixed, siblings)
    mine = jnp.arange(2)[:, None, None] == k
    result = jnp.where(mine, mixed[:, None], other[:, None])
    return result[:, None]


def solution(mesh):
    in_specs = (
        P("mom", "slab", None),
        P("mom", "slab", None, None, None),
        P("mom", "slab", None, None, None),
        P("energy", "slab", None, None, None),
        P(),
        P(),
    )
    out_specs = P(None, "slab", None, "energy", None)
    count = mesh.shape["energy"]

    def run(onsite, hop, couple, sigma_in, shifts, mode_weight):
        owned = (
            mesh.shape["slab"] == 4
            and mesh.shape["mom"] == 2
            and couple.shape[:2] == (2, 4)
            and sigma_in.shape[0] == 2 * count
            and count & (count - 1) == 0
        )
        inner = owner_body if owned else chain_body
        sharded = jax.shard_map(
            inner, mesh=mesh, in_specs=in_specs, out_specs=out_specs, check_vma=False
        )
        return sharded(onsite, hop, couple, sigma_in, shifts, mode_weight)

    return run
```

```python
import functools

import jax
import jax.numpy as jnp
from jax import lax
from jax.experimental import pallas as pl
from jax.experimental.pallas import tpu as pltpu
from jax.sharding import PartitionSpec as P

ETA = 0.5
HIGH = lax.Precision.HIGHEST


def shifted(shard, axis, by):
    length = lax.axis_size(axis)
    pairs = [(i, i + by) for i in range(length) if 0 <= i + by < length]
    return lax.ppermute(shard, axis, pairs)


def complex_mul(form, left, right):

    def product(first, second):
        return jnp.einsum(form, first, second, precision=HIGH)

    return (
        product(left[0], right[0]) - product(left[1], right[1]),
        product(left[0], right[1]) + product(left[1], right[0]),
    )


def newton_inverse(mat_real, mat_imag, form, identity):
    diag_real = jnp.diagonal(mat_real, axis1=-2, axis2=-1)
    diag_imag = jnp.diagonal(mat_imag, axis1=-2, axis2=-1)
    denom = diag_real * diag_real + diag_imag * diag_imag
    x_real = diag_real / denom
    x_imag = -diag_imag / denom
    rows_real = x_real[..., :, None] * mat_real - x_imag[..., :, None] * mat_imag
    rows_imag = x_real[..., :, None] * mat_imag + x_imag[..., :, None] * mat_real
    both_real = rows_real * x_real[..., None, :] - rows_imag * x_imag[..., None, :]
    both_imag = rows_real * x_imag[..., None, :] + rows_imag * x_real[..., None, :]
    first = (
        2.0 * identity * x_real[..., None, :] - both_real,
        2.0 * identity * x_imag[..., None, :] - both_imag,
    )
    resid = complex_mul(form, (mat_real, mat_imag), first)
    second = complex_mul(form, first, resid)
    return (2.0 * first[0] - second[0], 2.0 * first[1] - second[1])


def phonon_matrix(shifts, mode_weight, count):
    rows = jnp.arange(count)[:, None, None]
    cols = jnp.arange(count)[None, :, None]
    offset = shifts[None, None, :]
    upper = (cols == rows + offset).astype(jnp.float32)
    lower = (cols == rows - offset).astype(jnp.float32)
    return jnp.sum(upper * mode_weight[0] + lower * mode_weight[1], axis=2)


def chain_body(onsite, hop, couple, sigma_in, shifts, mode_weight):
    e_local = sigma_in.shape[0]
    width = onsite.shape[-1]
    slab_count = lax.axis_size("slab")
    slab_index = lax.axis_index("slab")
    energy_count = lax.axis_size("energy")
    mom_count = lax.axis_size("mom")
    total = e_local * energy_count
    identity = jnp.eye(width, dtype=jnp.float32)
    global_index = lax.axis_index("energy") * e_local + jnp.arange(e_local)
    energy = -0.5 + (global_index.astype(jnp.float32) + 0.5) / total
    coupling = (couple[0, 0, 0], couple[0, 0, 1])
    adjoint = (coupling[0].T, -coupling[1].T)
    hopping = (hop[0, 0, 0], hop[0, 0, 1])
    level = onsite[0, 0]
    sigma = sigma_in[:, 0]

    def forward(received, energies, sig):
        temp = complex_mul("ij,ejl->eil", coupling, (received[:, 0], received[:, 1]))
        left = complex_mul("eij,jl->eil", temp, adjoint)
        z_real = energies[:, None] - level[None, :]
        mat_real = identity * z_real[:, None, :] - hopping[0] - sig[:, 0] - left[0]
        mat_imag = identity * ETA - hopping[1] - sig[:, 1] - left[1]
        green = newton_inverse(mat_real, mat_imag, "eij,ejl->eil", identity)
        return jnp.stack(green, axis=1)

    def backward(green, received):
        pair = (green[:, 0], green[:, 1])
        temp = complex_mul("eij,ejl->eil", pair, (received[:, 0], received[:, 1]))
        extra = complex_mul("eij,ejl->eil", temp, pair)
        full = (pair[0] + extra[0], pair[1] + extra[1])
        temp = complex_mul("ij,ejl->eil", adjoint, full)
        coupled = complex_mul("eij,jl->eil", temp, coupling)
        return (jnp.stack(full, axis=1), jnp.stack(coupled, axis=1))

    empty = jnp.zeros((e_local, 2, width, width), jnp.float32)

    def forward_step(step, green_all):
        received = shifted(green_all, "slab", 1)
        return lax.cond(
            slab_index == step, lambda: forward(received, energy, sigma), lambda: green_all
        )

    green_all = lax.fori_loop(0, slab_count, forward_step, empty)

    def backward_step(step, carry):
        received = shifted(carry[1], "slab", -1)
        return lax.cond(
            slab_index == slab_count - 1 - step,
            lambda: backward(green_all, received),
            lambda: carry,
        )

    full_all, coupled_all = lax.fori_loop(0, slab_count, backward_step, (empty, empty))
    phonon = phonon_matrix(shifts, mode_weight, total)
    blocks = full_all[:, None]
    mixed = jnp.einsum(
        "ef,fsrjl->esrjl",
        phonon,
        lax.all_to_all(blocks, "energy", split_axis=3, concat_axis=0, tiled=True),
        precision=HIGH,
    )
    result = lax.psum(mixed, "mom") / mom_count
    return result


VMEM_BYTES = 24 * 1024 * 1024


BLOCKS = 2


def halves(value):
    high = value.astype(jnp.bfloat16)
    low = (value - high.astype(jnp.float32)).astype(jnp.bfloat16)
    return high, low


def form(pair):
    return halves(pair[0]), halves(pair[1]), halves(pair[0] + pair[1])


def real_dot(left, right):
    rows = left[0].shape[0]
    both = jnp.concatenate([left[0], left[1]], axis=0)
    main = jnp.dot(both, right[0], preferred_element_type=jnp.float32)
    rest = jnp.dot(left[0], right[1], preferred_element_type=jnp.float32)
    return main[:rows] + main[rows:] + rest


def mul(left, right):
    first = real_dot(left[0], right[0])
    second = real_dot(left[1], right[1])
    third = real_dot(left[2], right[2])
    return first - second, third - first - second


def mul_twice(blocks, right, last):
    inner = [mul(block, right) for block in blocks]
    return [mul(form(block), last) for block in inner]


def split_rows(pair):
    size = pair[0].shape[0] // BLOCKS
    return [tuple(part[b * size : (b + 1) * size] for part in pair) for b in range(BLOCKS)]


def join_rows(blocks):
    return tuple(jnp.concatenate([block[i] for block in blocks], axis=0) for i in range(2))


def form_rows(forms):
    return tuple(
        tuple(jnp.concatenate([f[plane][term] for f in forms], axis=0) for term in range(2))
        for plane in range(3)
    )


def read(ref):
    return ref[0], ref[1]


def write(ref, blocks):
    size = blocks[0][0].shape[0]
    for b, block in enumerate(blocks):
        ref[0, b * size : (b + 1) * size] = block[0]
        ref[1, b * size : (b + 1) * size] = block[1]


def choose(cond, left, right):
    return jnp.where(cond, left[0], right[0]), jnp.where(cond, left[1], right[1])


def times(left, right):
    return left[0] * right[0] - left[1] * right[1], left[0] * right[1] + left[1] * right[0]


def inverse(mats):
    size, width = mats[0][0].shape

    def invert(real, imag):
        denom = real * real + imag * imag
        return real / denom, -imag / denom

    eyes, scaled = [], []
    across = (0.0, 0.0)
    for b, mat in enumerate(mats):
        eye = lax.broadcasted_iota(jnp.int32, (size, width), 0) + b * size == (
            lax.broadcasted_iota(jnp.int32, (size, width), 1)
        )
        on = [jnp.where(eye, part, 0.0) for part in mat]
        off = [jnp.where(eye, 0.0, part) for part in mat]
        across = tuple(
            total + jnp.sum(part, axis=0, keepdims=True) for total, part in zip(across, on)
        )
        down = invert(*(jnp.sum(part, axis=1, keepdims=True) for part in on))
        eyes.append(eye)
        scaled.append(times(down, off))
    forms = [form(block) for block in scaled]
    right = form_rows(forms)
    squares = [mul(block, right) for block in forms]
    cubes = [mul(form(block), right) for block in squares]
    factor = invert(*across)
    out = []
    for eye, one, two, three in zip(eyes, scaled, squares, cubes):
        real = jnp.where(eye, 1.0, 0.0) - one[0] + two[0] - three[0]
        out.append(times((real, two[1] - one[1] - three[1]), factor))
    return out


def pick_block(y, x, slab, own, x_side, y_side, far):
    same_y = y == slab // 2
    same_x = x == slab % 2
    near = choose(same_x, read(own), read(x_side))
    away = choose(same_x, read(y_side), read(far))
    return choose(same_y, near, away)


def stored_form(ref, slab, side):
    at = (slab - 1, side)
    return tuple(tuple(ref[(*at, 2 * plane + term)] for term in range(2)) for plane in range(3))


def stored_rows(ref, slab, side):
    size = ref.shape[-2] // BLOCKS
    at = (slab - 1, side)
    return [
        tuple(
            tuple(ref[(*at, 2 * plane + term, slice(b * size, (b + 1) * size))] for term in range(2))
            for plane in range(3)
        )
        for b in range(BLOCKS)
    ]


def coupling_kernel(place, c_own, c_x, c_y, far_mine, far_theirs, out_ref, c_far):
    y, x = place[0], place[1]
    first, rows = place[2] == 0, far_mine.shape[1]
    for part in range(2):
        mine, theirs = far_mine[part], far_theirs[part]
        c_far[part, :rows] = jnp.where(first, mine, theirs)
        c_far[part, rows:] = jnp.where(first, theirs, mine)
    for slab in (1, 2, 3):
        real, imag = pick_block(y, x, slab, c_own, c_x, c_y, c_far)
        for side, pair in enumerate(((real, imag), (real.T, -imag.T))):
            for plane, terms in enumerate(form(pair)):
                for term in range(2):
                    out_ref[slab - 1, side, 2 * plane + term] = terms[term]


def chain_kernel(place, b_own, b_x, b_y, b_far, c_forms, keep_ref, give_ref):
    y, x = place[0], place[1]
    greens, forms = [], []
    for slab in range(4):
        mats = split_rows(pick_block(y, x, slab, b_own, b_x, b_y, b_far))
        if slab:
            terms = mul_twice(
                stored_rows(c_forms, slab, 0), form_rows(forms[-1]), stored_form(c_forms, slab, 1)
            )
            mats = [(m[0] - t[0], m[1] - t[1]) for m, t in zip(mats, terms)]
        greens.append(inverse(mats))
        forms.append([form(block) for block in greens[-1]])

    def finish(slab, blocks):
        full = join_rows(blocks)
        keep_ref[slab] = jnp.where(x == 0, full[0], full[1])
        give_ref[slab] = jnp.where(x == 0, full[1], full[0])

    finish(3, greens[3])
    full_form = form_rows(forms[3])
    for slab in (2, 1, 0):
        coupled = mul_twice(
            stored_rows(c_forms, slab + 1, 1), full_form, stored_form(c_forms, slab + 1, 0)
        )
        coupled_form = form_rows([form(block) for block in coupled])
        extra = mul_twice(forms[slab], coupled_form, form_rows(forms[slab]))
        fulls = [(g[0] + e[0], g[1] + e[1]) for g, e in zip(greens[slab], extra)]
        finish(slab, fulls)
        if slab:
            full_form = form_rows([form(block) for block in fulls])


def mix_kernel(phonon, parts_ref, out_ref):
    slots, rows, _ = parts_ref.shape
    energies = out_ref.shape[0]
    planes, step = slots // 4, 8

    def source(slot):
        return 2 * (slot % planes) + slot // planes // 2

    for row in range(0, rows, step):
        here = slice(row, row + step)
        values = [None] * energies
        for slot in range(slots):
            value = parts_ref[slot, here, :]
            held = values[source(slot)]
            values[source(slot)] = value if held is None else held + value
        for energy in range(energies):
            total = phonon[energy, 0] * values[0]
            for other in range(1, energies):
                total = total + phonon[energy, other] * values[other]
            out_ref[energy, here, :] = total


def pick_kernel(active, keep_ref, got_ref, out_ref):
    for slab in range(out_ref.shape[0]):
        out_ref[slab] = jnp.where(active[0] == 1, keep_ref[slab], got_ref[slab])


def prepare_kernel(place, scale, onsite_ref, hop_ref, sigma_ref, own_ref, other_ref):
    width = hop_ref.shape[-1]
    eye = lax.broadcasted_iota(jnp.int32, (width, width), 0) == lax.broadcasted_iota(
        jnp.int32, (width, width), 1
    )
    for ref, local, energy in ((other_ref, 1 - place[0], scale[1]), (own_ref, place[0], scale[0])):
        level = energy - onsite_ref[...]
        ref[0] = jnp.where(eye, level, 0.0) - hop_ref[0] - sigma_ref[local, 0]
        ref[1] = jnp.where(eye, ETA, 0.0) - hop_ref[1] - sigma_ref[local, 1]


def call(kernel, place, arrays, shape, count, products):
    width = arrays[0].shape[-1]
    vmem = pl.BlockSpec(memory_space=pltpu.VMEM)
    return pl.pallas_call(
        kernel,
        out_shape=[jax.ShapeDtypeStruct(shape, jnp.float32)] * count,
        in_specs=[pl.BlockSpec(memory_space=pltpu.SMEM)] + [vmem] * len(arrays),
        out_specs=[vmem] * count,
        compiler_params=pltpu.CompilerParams(vmem_limit_bytes=VMEM_BYTES),
        cost_estimate=pl.CostEstimate(
            flops=products * 9 * 2 * width**3,
            bytes_accessed=(len(arrays) + count) * 2 * width * width * 4,
            transcendentals=0,
        ),
    )(place, *arrays)


def owner_body(onsite, hop, couple, sigma_in, shifts, mode_weight):
    e_local = sigma_in.shape[0]
    width = onsite.shape[-1]
    energy_count = lax.axis_size("energy")
    mom_count = lax.axis_size("mom")
    total = e_local * energy_count
    axes = ("slab", "energy", "mom")
    slab = lax.axis_index("slab")
    z = lax.axis_index("energy")
    k = lax.axis_index("mom")
    y, x = slab // 2, slab % 2
    place = jnp.stack([y, x, z % 2]).astype(jnp.int32)
    active = k == x

    def device(yy, xx, zz, kk):
        return ((2 * yy + xx) * energy_count + zz) * mom_count + kk

    chips = [(yy, xx, zz) for yy in range(2) for xx in range(2) for zz in range(energy_count)]
    to_x = [(device(a, b, c, 1 - b), device(a, 1 - b, c, 1 - b)) for a, b, c in chips]
    to_y = [(device(a, b, c, b), device(1 - a, b, c, b)) for a, b, c in chips]
    to_far = [(device(a, b, c, 1 - b), device(1 - a, 1 - b, c, 1 - b)) for a, b, c in chips]

    def routes(*pairs):
        return [
            (device(*divmod(s, 2), zz, t % 2), device(*divmod(t, 2), zz, t % 2))
            for s, t in pairs
            for zz in range(energy_count)
        ]

    beside = [(device(a, b, c, b), device(a, b, c ^ 1, b)) for a, b, c in chips]
    siblings = [(device(a, b, c, d), device(a, b, c, 1 - d)) for a, b, c in chips for d in range(2)]
    gift = [(device(a, b, c, b), device(a, b, c, 1 - b)) for a, b, c in chips]

    def send(value, pairs):
        return lax.ppermute(value, axes, pairs)

    locals_ = jnp.stack([y, 1 - y])
    energies = -0.5 + ((z * e_local + locals_).astype(jnp.float32) + 0.5) / total
    smem = pl.BlockSpec(memory_space=pltpu.SMEM)
    vmem = pl.BlockSpec(memory_space=pltpu.VMEM)
    block_shape = jax.ShapeDtypeStruct((2, width, width), jnp.float32)
    b_own, b_other = pl.pallas_call(
        prepare_kernel,
        out_shape=[block_shape] * 2,
        in_specs=[smem, smem, vmem, vmem, vmem],
        out_specs=[vmem] * 2,
        compiler_params=pltpu.CompilerParams(vmem_limit_bytes=VMEM_BYTES),
    )(place, energies, onsite[0], hop[0, 0], sigma_in[:, 0])

    coupling = couple[0, 0]
    c_part = lax.dynamic_slice_in_dim(coupling, (z % 2) * (width // 2), width // 2, axis=1)
    far_mine = send(c_part, routes((1, 2), (2, 1), (3, 0)))
    c_x = send(coupling, routes((1, 0), (2, 3), (3, 2)))
    c_y = send(coupling, routes((1, 3), (2, 0), (3, 1)))
    far_mine, c_x, c_y = lax.optimization_barrier((far_mine, c_x, c_y))
    far_theirs = send(far_mine, beside)
    b_far = send(b_other, to_far)
    b_x = send(b_own, to_x)
    b_y = send(b_other, to_y)

    c_forms = pl.pallas_call(
        coupling_kernel,
        out_shape=jax.ShapeDtypeStruct((3, 2, 6, width, width), jnp.bfloat16),
        in_specs=[smem] + [vmem] * 5,
        out_specs=vmem,
        scratch_shapes=[pltpu.VMEM((2, width, width), jnp.float32)],
        compiler_params=pltpu.CompilerParams(vmem_limit_bytes=VMEM_BYTES),
    )(place, coupling, c_x, c_y, far_mine, far_theirs)
    shape = (4, width, width)
    keep, give = call(chain_kernel, place, (b_own, b_x, b_y, b_far, c_forms), shape, 2, 26)
    half = pl.pallas_call(
        pick_kernel,
        out_shape=jax.ShapeDtypeStruct(shape, jnp.float32),
        in_specs=[smem, vmem, vmem],
        out_specs=vmem,
        compiler_params=pltpu.CompilerParams(vmem_limit_bytes=VMEM_BYTES),
    )(active[None].astype(jnp.int32), keep, send(give, gift))

    rows = width // energy_count
    slots = 4 * energy_count
    parts = lax.all_to_all(
        half.reshape(slots, rows, width), ("slab", "energy"), 0, 0, tiled=True
    )
    phonon = phonon_matrix(shifts, mode_weight, total) / mom_count
    mixed = pl.pallas_call(
        mix_kernel,
        out_shape=jax.ShapeDtypeStruct((total, rows, width), jnp.float32),
        in_specs=[smem, vmem],
        out_specs=vmem,
        compiler_params=pltpu.CompilerParams(vmem_limit_bytes=VMEM_BYTES),
    )(phonon, parts)
    other = send(mixed, siblings)
    mine = jnp.arange(2)[:, None, None] == k
    result = jnp.where(mine, mixed[:, None], other[:, None])
    return result[:, None]


def solution(mesh):
    in_specs = (
        P("mom", "slab", None),
        P("mom", "slab", None, None, None),
        P("mom", "slab", None, None, None),
        P("energy", "slab", None, None, None),
        P(),
        P(),
    )
    out_specs = P(None, "slab", None, "energy", None)
    count = mesh.shape["energy"]

    def run(onsite, hop, couple, sigma_in, shifts, mode_weight):
        owned = (
            mesh.shape["slab"] == 4
            and mesh.shape["mom"] == 2
            and couple.shape[:2] == (2, 4)
            and sigma_in.shape[0] == 2 * count
            and count & (count - 1) == 0
        )
        inner = owner_body if owned else chain_body
        sharded = jax.shard_map(
            inner, mesh=mesh, in_specs=in_specs, out_specs=out_specs, check_vma=False
        )
        return sharded(onsite, hop, couple, sigma_in, shifts, mode_weight)

    return run
```

```python
import functools

import jax
import jax.numpy as jnp
from jax import lax
from jax.experimental import pallas as pl
from jax.experimental.pallas import tpu as pltpu
from jax.sharding import PartitionSpec as P

ETA = 0.5
HIGH = lax.Precision.HIGHEST


def shifted(shard, axis, by):
    length = lax.axis_size(axis)
    pairs = [(i, i + by) for i in range(length) if 0 <= i + by < length]
    return lax.ppermute(shard, axis, pairs)


def complex_mul(form, left, right):

    def product(first, second):
        return jnp.einsum(form, first, second, precision=HIGH)

    return (
        product(left[0], right[0]) - product(left[1], right[1]),
        product(left[0], right[1]) + product(left[1], right[0]),
    )


def newton_inverse(mat_real, mat_imag, form, identity):
    diag_real = jnp.diagonal(mat_real, axis1=-2, axis2=-1)
    diag_imag = jnp.diagonal(mat_imag, axis1=-2, axis2=-1)
    denom = diag_real * diag_real + diag_imag * diag_imag
    x_real = diag_real / denom
    x_imag = -diag_imag / denom
    rows_real = x_real[..., :, None] * mat_real - x_imag[..., :, None] * mat_imag
    rows_imag = x_real[..., :, None] * mat_imag + x_imag[..., :, None] * mat_real
    both_real = rows_real * x_real[..., None, :] - rows_imag * x_imag[..., None, :]
    both_imag = rows_real * x_imag[..., None, :] + rows_imag * x_real[..., None, :]
    first = (
        2.0 * identity * x_real[..., None, :] - both_real,
        2.0 * identity * x_imag[..., None, :] - both_imag,
    )
    resid = complex_mul(form, (mat_real, mat_imag), first)
    second = complex_mul(form, first, resid)
    return (2.0 * first[0] - second[0], 2.0 * first[1] - second[1])


def phonon_matrix(shifts, mode_weight, count):
    rows = jnp.arange(count)[:, None, None]
    cols = jnp.arange(count)[None, :, None]
    offset = shifts[None, None, :]
    upper = (cols == rows + offset).astype(jnp.float32)
    lower = (cols == rows - offset).astype(jnp.float32)
    return jnp.sum(upper * mode_weight[0] + lower * mode_weight[1], axis=2)


def chain_body(onsite, hop, couple, sigma_in, shifts, mode_weight):
    e_local = sigma_in.shape[0]
    width = onsite.shape[-1]
    slab_count = lax.axis_size("slab")
    slab_index = lax.axis_index("slab")
    energy_count = lax.axis_size("energy")
    mom_count = lax.axis_size("mom")
    total = e_local * energy_count
    identity = jnp.eye(width, dtype=jnp.float32)
    global_index = lax.axis_index("energy") * e_local + jnp.arange(e_local)
    energy = -0.5 + (global_index.astype(jnp.float32) + 0.5) / total
    coupling = (couple[0, 0, 0], couple[0, 0, 1])
    adjoint = (coupling[0].T, -coupling[1].T)
    hopping = (hop[0, 0, 0], hop[0, 0, 1])
    level = onsite[0, 0]
    sigma = sigma_in[:, 0]

    def forward(received, energies, sig):
        temp = complex_mul("ij,ejl->eil", coupling, (received[:, 0], received[:, 1]))
        left = complex_mul("eij,jl->eil", temp, adjoint)
        z_real = energies[:, None] - level[None, :]
        mat_real = identity * z_real[:, None, :] - hopping[0] - sig[:, 0] - left[0]
        mat_imag = identity * ETA - hopping[1] - sig[:, 1] - left[1]
        green = newton_inverse(mat_real, mat_imag, "eij,ejl->eil", identity)
        return jnp.stack(green, axis=1)

    def backward(green, received):
        pair = (green[:, 0], green[:, 1])
        temp = complex_mul("eij,ejl->eil", pair, (received[:, 0], received[:, 1]))
        extra = complex_mul("eij,ejl->eil", temp, pair)
        full = (pair[0] + extra[0], pair[1] + extra[1])
        temp = complex_mul("ij,ejl->eil", adjoint, full)
        coupled = complex_mul("eij,jl->eil", temp, coupling)
        return (jnp.stack(full, axis=1), jnp.stack(coupled, axis=1))

    empty = jnp.zeros((e_local, 2, width, width), jnp.float32)

    def forward_step(step, green_all):
        received = shifted(green_all, "slab", 1)
        return lax.cond(
            slab_index == step, lambda: forward(received, energy, sigma), lambda: green_all
        )

    green_all = lax.fori_loop(0, slab_count, forward_step, empty)

    def backward_step(step, carry):
        received = shifted(carry[1], "slab", -1)
        return lax.cond(
            slab_index == slab_count - 1 - step,
            lambda: backward(green_all, received),
            lambda: carry,
        )

    full_all, coupled_all = lax.fori_loop(0, slab_count, backward_step, (empty, empty))
    phonon = phonon_matrix(shifts, mode_weight, total)
    blocks = full_all[:, None]
    mixed = jnp.einsum(
        "ef,fsrjl->esrjl",
        phonon,
        lax.all_to_all(blocks, "energy", split_axis=3, concat_axis=0, tiled=True),
        precision=HIGH,
    )
    result = lax.psum(mixed, "mom") / mom_count
    return result


VMEM_BYTES = 24 * 1024 * 1024


BLOCKS = 2


def halves(value):
    high = value.astype(jnp.bfloat16)
    low = (value - high.astype(jnp.float32)).astype(jnp.bfloat16)
    return high, low


def form(pair):
    return halves(pair[0]), halves(pair[1]), halves(pair[0] + pair[1])


def real_dot(left, right):
    rows = left[0].shape[0]
    both = jnp.concatenate([left[0], left[1]], axis=0)
    main = jnp.dot(both, right[0], preferred_element_type=jnp.float32)
    rest = jnp.dot(left[0], right[1], preferred_element_type=jnp.float32)
    return main[:rows] + main[rows:] + rest


def mul(left, right):
    first = real_dot(left[0], right[0])
    second = real_dot(left[1], right[1])
    third = real_dot(left[2], right[2])
    return first - second, third - first - second


def mul_twice(blocks, right, last):
    inner = [mul(block, right) for block in blocks]
    return [mul(form(block), last) for block in inner]


def split_rows(pair):
    size = pair[0].shape[0] // BLOCKS
    return [tuple(part[b * size : (b + 1) * size] for part in pair) for b in range(BLOCKS)]


def join_rows(blocks):
    return tuple(jnp.concatenate([block[i] for block in blocks], axis=0) for i in range(2))


def form_rows(forms):
    return tuple(
        tuple(jnp.concatenate([f[plane][term] for f in forms], axis=0) for term in range(2))
        for plane in range(3)
    )


def read(ref):
    return ref[0], ref[1]


def write(ref, blocks):
    size = blocks[0][0].shape[0]
    for b, block in enumerate(blocks):
        ref[0, b * size : (b + 1) * size] = block[0]
        ref[1, b * size : (b + 1) * size] = block[1]


def choose(cond, left, right):
    return jnp.where(cond, left[0], right[0]), jnp.where(cond, left[1], right[1])


def times(left, right):
    return left[0] * right[0] - left[1] * right[1], left[0] * right[1] + left[1] * right[0]


def inverse(mats):
    size, width = mats[0][0].shape

    def invert(real, imag):
        denom = real * real + imag * imag
        return real / denom, -imag / denom

    eyes, scaled = [], []
    across = (0.0, 0.0)
    for b, mat in enumerate(mats):
        eye = lax.broadcasted_iota(jnp.int32, (size, width), 0) + b * size == (
            lax.broadcasted_iota(jnp.int32, (size, width), 1)
        )
        on = [jnp.where(eye, part, 0.0) for part in mat]
        off = [jnp.where(eye, 0.0, part) for part in mat]
        across = tuple(
            total + jnp.sum(part, axis=0, keepdims=True) for total, part in zip(across, on)
        )
        down = invert(*(jnp.sum(part, axis=1, keepdims=True) for part in on))
        eyes.append(eye)
        scaled.append(times(down, off))
    forms = [form(block) for block in scaled]
    right = form_rows(forms)
    squares = [mul(block, right) for block in forms]
    cubes = [mul(form(block), right) for block in squares]
    factor = invert(*across)
    out = []
    for eye, one, two, three in zip(eyes, scaled, squares, cubes):
        real = jnp.where(eye, 1.0, 0.0) - one[0] + two[0] - three[0]
        out.append(times((real, two[1] - one[1] - three[1]), factor))
    return out


def pick_block(y, x, slab, own, x_side, y_side, far):
    same_y = y == slab // 2
    same_x = x == slab % 2
    near = choose(same_x, read(own), read(x_side))
    away = choose(same_x, read(y_side), read(far))
    return choose(same_y, near, away)


def stored_form(ref, slab, side):
    at = (slab - 1, side)
    return tuple(tuple(ref[(*at, 2 * plane + term)] for term in range(2)) for plane in range(3))


def stored_rows(ref, slab, side):
    size = ref.shape[-2] // BLOCKS
    at = (slab - 1, side)
    return [
        tuple(
            tuple(ref[(*at, 2 * plane + term, slice(b * size, (b + 1) * size))] for term in range(2))
            for plane in range(3)
        )
        for b in range(BLOCKS)
    ]


def place_of():
    slab = lax.axis_index("slab")
    return slab // 2, slab % 2


def coupling_kernel(c_own, c_x, c_y, far_mine, far_theirs, out_ref, c_far):
    y, x = place_of()
    first, rows = lax.axis_index("energy") % 2 == 0, far_mine.shape[1]
    for part in range(2):
        mine, theirs = far_mine[part], far_theirs[part]
        c_far[part, :rows] = jnp.where(first, mine, theirs)
        c_far[part, rows:] = jnp.where(first, theirs, mine)
    for slab in (1, 2, 3):
        real, imag = pick_block(y, x, slab, c_own, c_x, c_y, c_far)
        for side, pair in enumerate(((real, imag), (real.T, -imag.T))):
            for plane, terms in enumerate(form(pair)):
                for term in range(2):
                    out_ref[slab - 1, side, 2 * plane + term] = terms[term]


def chain_kernel(b_own, b_x, b_y, b_far, c_forms, keep_ref, give_ref):
    y, x = place_of()
    greens, forms = [], []
    for slab in range(4):
        mats = split_rows(pick_block(y, x, slab, b_own, b_x, b_y, b_far))
        if slab:
            terms = mul_twice(
                stored_rows(c_forms, slab, 0), form_rows(forms[-1]), stored_form(c_forms, slab, 1)
            )
            mats = [(m[0] - t[0], m[1] - t[1]) for m, t in zip(mats, terms)]
        greens.append(inverse(mats))
        forms.append([form(block) for block in greens[-1]])

    def finish(slab, blocks):
        full = join_rows(blocks)
        keep_ref[slab] = jnp.where(x == 0, full[0], full[1])
        give_ref[slab] = jnp.where(x == 0, full[1], full[0])

    finish(3, greens[3])
    full_form = form_rows(forms[3])
    for slab in (2, 1, 0):
        coupled = mul_twice(
            stored_rows(c_forms, slab + 1, 1), full_form, stored_form(c_forms, slab + 1, 0)
        )
        coupled_form = form_rows([form(block) for block in coupled])
        extra = mul_twice(forms[slab], coupled_form, form_rows(forms[slab]))
        fulls = [(g[0] + e[0], g[1] + e[1]) for g, e in zip(greens[slab], extra)]
        finish(slab, fulls)
        if slab:
            full_form = form_rows([form(block) for block in fulls])


def mix_kernel(phonon, parts_ref, out_ref):
    slots, rows, _ = parts_ref.shape
    energies = out_ref.shape[0]
    planes, step = slots // 4, 8

    def source(slot):
        return 2 * (slot % planes) + slot // planes // 2

    for row in range(0, rows, step):
        here = slice(row, row + step)
        values = [None] * energies
        for slot in range(slots):
            value = parts_ref[slot, here, :]
            held = values[source(slot)]
            values[source(slot)] = value if held is None else held + value
        for energy in range(energies):
            total = phonon[energy, 0] * values[0]
            for other in range(1, energies):
                total = total + phonon[energy, other] * values[other]
            out_ref[energy, here, :] = total


def pick_kernel(keep_ref, got_ref, out_ref):
    owner = lax.axis_index("mom") == place_of()[1]
    for slab in range(out_ref.shape[0]):
        out_ref[slab] = jnp.where(owner, keep_ref[slab], got_ref[slab])


def prepare_kernel(planes, onsite_ref, hop_ref, sigma_ref, own_ref, other_ref):
    width = hop_ref.shape[-1]
    y, _ = place_of()
    eye = lax.broadcasted_iota(jnp.int32, (width, width), 0) == lax.broadcasted_iota(
        jnp.int32, (width, width), 1
    )
    count = sigma_ref.shape[0]
    for ref, local in ((other_ref, 1 - y), (own_ref, y)):
        index = (lax.axis_index("energy") * count + local).astype(jnp.float32)
        level = (-0.5 + (index + 0.5) / (count * planes)) - onsite_ref[...]
        ref[0] = jnp.where(eye, level, 0.0) - hop_ref[0] - sigma_ref[local, 0]
        ref[1] = jnp.where(eye, ETA, 0.0) - hop_ref[1] - sigma_ref[local, 1]


def call(kernel, arrays, shape, count, products):
    width = arrays[0].shape[-1]
    vmem = pl.BlockSpec(memory_space=pltpu.VMEM)
    return pl.pallas_call(
        kernel,
        out_shape=[jax.ShapeDtypeStruct(shape, jnp.float32)] * count,
        in_specs=[vmem] * len(arrays),
        out_specs=[vmem] * count,
        compiler_params=pltpu.CompilerParams(vmem_limit_bytes=VMEM_BYTES),
        cost_estimate=pl.CostEstimate(
            flops=products * 9 * 2 * width**3,
            bytes_accessed=(len(arrays) + count) * 2 * width * width * 4,
            transcendentals=0,
        ),
    )(*arrays)


def owner_body(onsite, hop, couple, sigma_in, shifts, mode_weight):
    e_local = sigma_in.shape[0]
    width = onsite.shape[-1]
    energy_count = lax.axis_size("energy")
    mom_count = lax.axis_size("mom")
    total = e_local * energy_count
    axes = ("slab", "energy", "mom")
    slab = lax.axis_index("slab")
    z = lax.axis_index("energy")
    k = lax.axis_index("mom")
    y, x = slab // 2, slab % 2

    def device(yy, xx, zz, kk):
        return ((2 * yy + xx) * energy_count + zz) * mom_count + kk

    chips = [(yy, xx, zz) for yy in range(2) for xx in range(2) for zz in range(energy_count)]
    to_x = [(device(a, b, c, 1 - b), device(a, 1 - b, c, 1 - b)) for a, b, c in chips]
    to_y = [(device(a, b, c, b), device(1 - a, b, c, b)) for a, b, c in chips]
    to_far = [(device(a, b, c, 1 - b), device(1 - a, 1 - b, c, 1 - b)) for a, b, c in chips]

    def routes(*pairs):
        return [
            (device(*divmod(s, 2), zz, t % 2), device(*divmod(t, 2), zz, t % 2))
            for s, t in pairs
            for zz in range(energy_count)
        ]

    beside = [(device(a, b, c, b), device(a, b, c ^ 1, b)) for a, b, c in chips]
    siblings = [(device(a, b, c, d), device(a, b, c, 1 - d)) for a, b, c in chips for d in range(2)]
    gift = [(device(a, b, c, b), device(a, b, c, 1 - b)) for a, b, c in chips]

    def send(value, pairs):
        return lax.ppermute(value, axes, pairs)

    smem = pl.BlockSpec(memory_space=pltpu.SMEM)
    vmem = pl.BlockSpec(memory_space=pltpu.VMEM)
    block_shape = jax.ShapeDtypeStruct((2, width, width), jnp.float32)
    b_own, b_other = pl.pallas_call(
        functools.partial(prepare_kernel, energy_count),
        out_shape=[block_shape] * 2,
        in_specs=[vmem] * 3,
        out_specs=[vmem] * 2,
        compiler_params=pltpu.CompilerParams(vmem_limit_bytes=VMEM_BYTES),
    )(onsite[0], hop[0, 0], sigma_in[:, 0])

    coupling = couple[0, 0]
    c_part = lax.dynamic_slice_in_dim(coupling, (z % 2) * (width // 2), width // 2, axis=1)
    far_mine = send(c_part, routes((1, 2), (2, 1), (3, 0)))
    c_x = send(coupling, routes((1, 0), (2, 3), (3, 2)))
    c_y = send(coupling, routes((1, 3), (2, 0), (3, 1)))
    far_mine, c_x, c_y = lax.optimization_barrier((far_mine, c_x, c_y))
    far_theirs = send(far_mine, beside)
    b_far = send(b_other, to_far)
    b_x = send(b_own, to_x)
    b_y = send(b_other, to_y)

    c_forms = pl.pallas_call(
        coupling_kernel,
        out_shape=jax.ShapeDtypeStruct((3, 2, 6, width, width), jnp.bfloat16),
        in_specs=[vmem] * 5,
        out_specs=vmem,
        scratch_shapes=[pltpu.VMEM((2, width, width), jnp.float32)],
        compiler_params=pltpu.CompilerParams(vmem_limit_bytes=VMEM_BYTES),
    )(coupling, c_x, c_y, far_mine, far_theirs)
    shape = (4, width, width)
    keep, give = call(chain_kernel, (b_own, b_x, b_y, b_far, c_forms), shape, 2, 26)
    half = pl.pallas_call(
        pick_kernel,
        out_shape=jax.ShapeDtypeStruct(shape, jnp.float32),
        in_specs=[vmem, vmem],
        out_specs=vmem,
        compiler_params=pltpu.CompilerParams(vmem_limit_bytes=VMEM_BYTES),
    )(keep, send(give, gift))

    rows = width // energy_count
    slots = 4 * energy_count
    parts = lax.all_to_all(
        half.reshape(slots, rows, width), ("slab", "energy"), 0, 0, tiled=True
    )
    phonon = phonon_matrix(shifts, mode_weight, total) / mom_count
    mixed = pl.pallas_call(
        mix_kernel,
        out_shape=jax.ShapeDtypeStruct((total, rows, width), jnp.float32),
        in_specs=[smem, vmem],
        out_specs=vmem,
        compiler_params=pltpu.CompilerParams(vmem_limit_bytes=VMEM_BYTES),
    )(phonon, parts)
    other = send(mixed, siblings)
    mine = jnp.arange(2)[:, None, None] == k
    result = jnp.where(mine, mixed[:, None], other[:, None])
    return result[:, None]


def solution(mesh):
    in_specs = (
        P("mom", "slab", None),
        P("mom", "slab", None, None, None),
        P("mom", "slab", None, None, None),
        P("energy", "slab", None, None, None),
        P(),
        P(),
    )
    out_specs = P(None, "slab", None, "energy", None)
    count = mesh.shape["energy"]

    def run(onsite, hop, couple, sigma_in, shifts, mode_weight):
        owned = (
            mesh.shape["slab"] == 4
            and mesh.shape["mom"] == 2
            and couple.shape[:2] == (2, 4)
            and sigma_in.shape[0] == 2 * count
            and count & (count - 1) == 0
        )
        inner = owner_body if owned else chain_body
        sharded = jax.shard_map(
            inner, mesh=mesh, in_specs=in_specs, out_specs=out_specs, check_vma=False
        )
        return sharded(onsite, hop, couple, sigma_in, shifts, mode_weight)

    return run
```

```python
import functools

import jax
import jax.numpy as jnp
from jax import lax
from jax.experimental import pallas as pl
from jax.experimental.pallas import tpu as pltpu
from jax.sharding import PartitionSpec as P

ETA = 0.5
HIGH = lax.Precision.HIGHEST


def shifted(shard, axis, by):
    length = lax.axis_size(axis)
    pairs = [(i, i + by) for i in range(length) if 0 <= i + by < length]
    return lax.ppermute(shard, axis, pairs)


def complex_mul(form, left, right):

    def product(first, second):
        return jnp.einsum(form, first, second, precision=HIGH)

    return (
        product(left[0], right[0]) - product(left[1], right[1]),
        product(left[0], right[1]) + product(left[1], right[0]),
    )


def newton_inverse(mat_real, mat_imag, form, identity):
    diag_real = jnp.diagonal(mat_real, axis1=-2, axis2=-1)
    diag_imag = jnp.diagonal(mat_imag, axis1=-2, axis2=-1)
    denom = diag_real * diag_real + diag_imag * diag_imag
    x_real = diag_real / denom
    x_imag = -diag_imag / denom
    rows_real = x_real[..., :, None] * mat_real - x_imag[..., :, None] * mat_imag
    rows_imag = x_real[..., :, None] * mat_imag + x_imag[..., :, None] * mat_real
    both_real = rows_real * x_real[..., None, :] - rows_imag * x_imag[..., None, :]
    both_imag = rows_real * x_imag[..., None, :] + rows_imag * x_real[..., None, :]
    first = (
        2.0 * identity * x_real[..., None, :] - both_real,
        2.0 * identity * x_imag[..., None, :] - both_imag,
    )
    resid = complex_mul(form, (mat_real, mat_imag), first)
    second = complex_mul(form, first, resid)
    return (2.0 * first[0] - second[0], 2.0 * first[1] - second[1])


def phonon_matrix(shifts, mode_weight, count):
    rows = jnp.arange(count)[:, None, None]
    cols = jnp.arange(count)[None, :, None]
    offset = shifts[None, None, :]
    upper = (cols == rows + offset).astype(jnp.float32)
    lower = (cols == rows - offset).astype(jnp.float32)
    return jnp.sum(upper * mode_weight[0] + lower * mode_weight[1], axis=2)


def chain_body(onsite, hop, couple, sigma_in, shifts, mode_weight):
    e_local = sigma_in.shape[0]
    width = onsite.shape[-1]
    slab_count = lax.axis_size("slab")
    slab_index = lax.axis_index("slab")
    energy_count = lax.axis_size("energy")
    mom_count = lax.axis_size("mom")
    total = e_local * energy_count
    identity = jnp.eye(width, dtype=jnp.float32)
    global_index = lax.axis_index("energy") * e_local + jnp.arange(e_local)
    energy = -0.5 + (global_index.astype(jnp.float32) + 0.5) / total
    coupling = (couple[0, 0, 0], couple[0, 0, 1])
    adjoint = (coupling[0].T, -coupling[1].T)
    hopping = (hop[0, 0, 0], hop[0, 0, 1])
    level = onsite[0, 0]
    sigma = sigma_in[:, 0]

    def forward(received, energies, sig):
        temp = complex_mul("ij,ejl->eil", coupling, (received[:, 0], received[:, 1]))
        left = complex_mul("eij,jl->eil", temp, adjoint)
        z_real = energies[:, None] - level[None, :]
        mat_real = identity * z_real[:, None, :] - hopping[0] - sig[:, 0] - left[0]
        mat_imag = identity * ETA - hopping[1] - sig[:, 1] - left[1]
        green = newton_inverse(mat_real, mat_imag, "eij,ejl->eil", identity)
        return jnp.stack(green, axis=1)

    def backward(green, received):
        pair = (green[:, 0], green[:, 1])
        temp = complex_mul("eij,ejl->eil", pair, (received[:, 0], received[:, 1]))
        extra = complex_mul("eij,ejl->eil", temp, pair)
        full = (pair[0] + extra[0], pair[1] + extra[1])
        temp = complex_mul("ij,ejl->eil", adjoint, full)
        coupled = complex_mul("eij,jl->eil", temp, coupling)
        return (jnp.stack(full, axis=1), jnp.stack(coupled, axis=1))

    empty = jnp.zeros((e_local, 2, width, width), jnp.float32)

    def forward_step(step, green_all):
        received = shifted(green_all, "slab", 1)
        return lax.cond(
            slab_index == step, lambda: forward(received, energy, sigma), lambda: green_all
        )

    green_all = lax.fori_loop(0, slab_count, forward_step, empty)

    def backward_step(step, carry):
        received = shifted(carry[1], "slab", -1)
        return lax.cond(
            slab_index == slab_count - 1 - step,
            lambda: backward(green_all, received),
            lambda: carry,
        )

    full_all, coupled_all = lax.fori_loop(0, slab_count, backward_step, (empty, empty))
    phonon = phonon_matrix(shifts, mode_weight, total)
    blocks = full_all[:, None]
    mixed = jnp.einsum(
        "ef,fsrjl->esrjl",
        phonon,
        lax.all_to_all(blocks, "energy", split_axis=3, concat_axis=0, tiled=True),
        precision=HIGH,
    )
    result = lax.psum(mixed, "mom") / mom_count
    return result


VMEM_BYTES = 24 * 1024 * 1024


BLOCKS = 2


def halves(value):
    high = value.astype(jnp.bfloat16)
    low = (value - high.astype(jnp.float32)).astype(jnp.bfloat16)
    return high, low


def form(pair):
    return halves(pair[0]), halves(pair[1]), halves(pair[0] + pair[1])


def real_dot(left, right):
    rows = left[0].shape[0]
    both = jnp.concatenate([left[0], left[1]], axis=0)
    main = jnp.dot(both, right[0], preferred_element_type=jnp.float32)
    rest = jnp.dot(left[0], right[1], preferred_element_type=jnp.float32)
    return main[:rows] + main[rows:] + rest


def mul(left, right):
    first = real_dot(left[0], right[0])
    second = real_dot(left[1], right[1])
    third = real_dot(left[2], right[2])
    return first - second, third - first - second


def mul_twice(blocks, right, last):
    inner = [mul(block, right) for block in blocks]
    return [mul(form(block), last) for block in inner]


def split_rows(pair):
    size = pair[0].shape[0] // BLOCKS
    return [tuple(part[b * size : (b + 1) * size] for part in pair) for b in range(BLOCKS)]


def join_rows(blocks):
    return tuple(jnp.concatenate([block[i] for block in blocks], axis=0) for i in range(2))


def form_rows(forms):
    return tuple(
        tuple(jnp.concatenate([f[plane][term] for f in forms], axis=0) for term in range(2))
        for plane in range(3)
    )


def read(ref):
    return ref[0], ref[1]


def write(ref, blocks):
    size = blocks[0][0].shape[0]
    for b, block in enumerate(blocks):
        ref[0, b * size : (b + 1) * size] = block[0]
        ref[1, b * size : (b + 1) * size] = block[1]


def choose(cond, left, right):
    return jnp.where(cond, left[0], right[0]), jnp.where(cond, left[1], right[1])


def times(left, right):
    return left[0] * right[0] - left[1] * right[1], left[0] * right[1] + left[1] * right[0]


def inverse(mats):
    size, width = mats[0][0].shape

    def invert(real, imag):
        denom = real * real + imag * imag
        return real / denom, -imag / denom

    eyes, scaled = [], []
    across = (0.0, 0.0)
    for b, mat in enumerate(mats):
        eye = lax.broadcasted_iota(jnp.int32, (size, width), 0) + b * size == (
            lax.broadcasted_iota(jnp.int32, (size, width), 1)
        )
        on = [jnp.where(eye, part, 0.0) for part in mat]
        off = [jnp.where(eye, 0.0, part) for part in mat]
        across = tuple(
            total + jnp.sum(part, axis=0, keepdims=True) for total, part in zip(across, on)
        )
        down = invert(*(jnp.sum(part, axis=1, keepdims=True) for part in on))
        eyes.append(eye)
        scaled.append(times(down, off))
    forms = [form(block) for block in scaled]
    right = form_rows(forms)
    squares = [mul(block, right) for block in forms]
    cubes = [mul(form(block), right) for block in squares]
    factor = invert(*across)
    out = []
    for eye, one, two, three in zip(eyes, scaled, squares, cubes):
        real = jnp.where(eye, 1.0, 0.0) - one[0] + two[0] - three[0]
        out.append(times((real, two[1] - one[1] - three[1]), factor))
    return out


def pick_block(y, x, slab, own, x_side, y_side, far):
    same_y = y == slab // 2
    same_x = x == slab % 2
    near = choose(same_x, read(own), read(x_side))
    away = choose(same_x, read(y_side), read(far))
    return choose(same_y, near, away)


def stored_form(ref, slab, side):
    at = (slab - 1, side)
    return tuple(tuple(ref[(*at, 2 * plane + term)] for term in range(2)) for plane in range(3))


def stored_rows(ref, slab, side):
    size = ref.shape[-2] // BLOCKS
    at = (slab - 1, side)
    return [
        tuple(
            tuple(ref[(*at, 2 * plane + term, slice(b * size, (b + 1) * size))] for term in range(2))
            for plane in range(3)
        )
        for b in range(BLOCKS)
    ]


def place_of():
    slab = lax.axis_index("slab")
    return slab // 2, slab % 2


def coupling_kernel(c_part, c_rest, c_x, c_y, far_mine, far_theirs, out_ref, c_own, c_far):
    y, x = place_of()
    first, rows = lax.axis_index("energy") % 2 == 0, far_mine.shape[1]
    for ref, here, beside in ((c_own, c_part, c_rest), (c_far, far_mine, far_theirs)):
        for part in range(2):
            mine, theirs = here[part], beside[part]
            ref[part, :rows] = jnp.where(first, mine, theirs)
            ref[part, rows:] = jnp.where(first, theirs, mine)
    for slab in (1, 2, 3):
        real, imag = pick_block(y, x, slab, c_own, c_x, c_y, c_far)
        for side, pair in enumerate(((real, imag), (real.T, -imag.T))):
            for plane, terms in enumerate(form(pair)):
                for term in range(2):
                    out_ref[slab - 1, side, 2 * plane + term] = terms[term]


def chain_kernel(b_own, b_x, b_y, b_far, c_forms, keep_ref, give_ref):
    y, x = place_of()
    greens, forms = [], []
    for slab in range(4):
        mats = split_rows(pick_block(y, x, slab, b_own, b_x, b_y, b_far))
        if slab:
            terms = mul_twice(
                stored_rows(c_forms, slab, 0), form_rows(forms[-1]), stored_form(c_forms, slab, 1)
            )
            mats = [(m[0] - t[0], m[1] - t[1]) for m, t in zip(mats, terms)]
        greens.append(inverse(mats))
        forms.append([form(block) for block in greens[-1]])

    def finish(slab, blocks):
        full = join_rows(blocks)
        keep_ref[slab] = jnp.where(x == 0, full[0], full[1])
        give_ref[slab] = jnp.where(x == 0, full[1], full[0])

    finish(3, greens[3])
    full_form = form_rows(forms[3])
    for slab in (2, 1, 0):
        coupled = mul_twice(
            stored_rows(c_forms, slab + 1, 1), full_form, stored_form(c_forms, slab + 1, 0)
        )
        coupled_form = form_rows([form(block) for block in coupled])
        extra = mul_twice(forms[slab], coupled_form, form_rows(forms[slab]))
        fulls = [(g[0] + e[0], g[1] + e[1]) for g, e in zip(greens[slab], extra)]
        finish(slab, fulls)
        if slab:
            full_form = form_rows([form(block) for block in fulls])


def mix_kernel(weight, parts_ref, out_ref):
    slots, rows, width = parts_ref.shape
    energies = out_ref.shape[0]
    planes = slots // 4
    high, wide = weight.shape[2:]

    def source(slot):
        return 2 * (slot % planes) + slot // planes // 2

    for row in range(0, rows, high):
        for column in range(0, width, wide):
            here = (slice(row, row + high), slice(column, column + wide))
            values = [None] * energies
            for slot in range(slots):
                value = parts_ref[(slot, *here)]
                held = values[source(slot)]
                values[source(slot)] = value if held is None else held + value
            for energy in range(energies):
                total = weight[energy, 0] * values[0]
                for other in range(1, energies):
                    total = total + weight[energy, other] * values[other]
                out_ref[(energy, *here)] = total


def pick_kernel(keep_ref, got_ref, out_ref, sem):
    owner = lax.axis_index("mom") == place_of()[1]

    @pl.when(owner)
    def _():
        copy = pltpu.make_async_copy(keep_ref, out_ref, sem)
        copy.start()
        copy.wait()

    @pl.when(jnp.logical_not(owner))
    def _():
        copy = pltpu.make_async_copy(got_ref, out_ref, sem)
        copy.start()
        copy.wait()


def prepare_kernel(planes, onsite_ref, hop_ref, sigma_ref, own_ref, other_ref):
    width = hop_ref.shape[-1]
    y, _ = place_of()
    eye = lax.broadcasted_iota(jnp.int32, (width, width), 0) == lax.broadcasted_iota(
        jnp.int32, (width, width), 1
    )
    count = sigma_ref.shape[0]
    for ref, local in ((other_ref, 1 - y), (own_ref, y)):
        index = (lax.axis_index("energy") * count + local).astype(jnp.float32)
        level = (-0.5 + (index + 0.5) / (count * planes)) - onsite_ref[...]
        ref[0] = jnp.where(eye, level, 0.0) - hop_ref[0] - sigma_ref[local, 0]
        ref[1] = jnp.where(eye, ETA, 0.0) - hop_ref[1] - sigma_ref[local, 1]


def call(kernel, arrays, shape, count, products):
    width = arrays[0].shape[-1]
    vmem = pl.BlockSpec(memory_space=pltpu.VMEM)
    return pl.pallas_call(
        kernel,
        out_shape=[jax.ShapeDtypeStruct(shape, jnp.float32)] * count,
        in_specs=[vmem] * len(arrays),
        out_specs=[vmem] * count,
        compiler_params=pltpu.CompilerParams(vmem_limit_bytes=VMEM_BYTES),
        cost_estimate=pl.CostEstimate(
            flops=products * 9 * 2 * width**3,
            bytes_accessed=(len(arrays) + count) * 2 * width * width * 4,
            transcendentals=0,
        ),
    )(*arrays)


def owner_body(onsite, hop, couple, sigma_in, shifts, mode_weight):
    e_local = sigma_in.shape[0]
    width = onsite.shape[-1]
    energy_count = lax.axis_size("energy")
    mom_count = lax.axis_size("mom")
    total = e_local * energy_count
    axes = ("slab", "energy", "mom")
    slab = lax.axis_index("slab")
    z = lax.axis_index("energy")
    k = lax.axis_index("mom")
    y, x = slab // 2, slab % 2

    def device(yy, xx, zz, kk):
        return ((2 * yy + xx) * energy_count + zz) * mom_count + kk

    chips = [(yy, xx, zz) for yy in range(2) for xx in range(2) for zz in range(energy_count)]
    to_x = [(device(a, b, c, 1 - b), device(a, 1 - b, c, 1 - b)) for a, b, c in chips]
    to_y = [(device(a, b, c, b), device(1 - a, b, c, b)) for a, b, c in chips]
    to_far = [(device(a, b, c, 1 - b), device(1 - a, 1 - b, c, 1 - b)) for a, b, c in chips]

    def routes(*pairs):
        return [
            (device(*divmod(s, 2), zz, t % 2), device(*divmod(t, 2), zz, t % 2))
            for s, t in pairs
            for zz in range(energy_count)
        ]

    beside = [(device(a, b, c, b), device(a, b, c ^ 1, b)) for a, b, c in chips]
    siblings = [(device(a, b, c, d), device(a, b, c, 1 - d)) for a, b, c in chips for d in range(2)]
    gift = [(device(a, b, c, b), device(a, b, c, 1 - b)) for a, b, c in chips]

    def send(value, pairs):
        return lax.ppermute(value, axes, pairs)

    vmem = pl.BlockSpec(memory_space=pltpu.VMEM)
    block_shape = jax.ShapeDtypeStruct((2, width, width), jnp.float32)
    b_own, b_other = pl.pallas_call(
        functools.partial(prepare_kernel, energy_count),
        out_shape=[block_shape] * 2,
        in_specs=[vmem] * 3,
        out_specs=[vmem] * 2,
        compiler_params=pltpu.CompilerParams(vmem_limit_bytes=VMEM_BYTES),
    )(onsite[0], hop[0, 0], sigma_in[:, 0])

    coupling = couple[0, 0]
    size = width // 2
    c_part = lax.dynamic_slice_in_dim(coupling, (z % 2) * size, size, axis=1)
    c_rest = lax.dynamic_slice_in_dim(coupling, (1 - z % 2) * size, size, axis=1)
    far_mine = send(c_part, routes((1, 2), (2, 1), (3, 0)))
    c_x = send(coupling, routes((1, 0), (2, 3), (3, 2)))
    c_y = send(coupling, routes((1, 3), (2, 0), (3, 1)))
    far_mine, c_x, c_y = lax.optimization_barrier((far_mine, c_x, c_y))
    far_theirs = send(far_mine, beside)
    b_far = send(b_other, to_far)
    b_x = send(b_own, to_x)
    b_y = send(b_other, to_y)

    c_forms = pl.pallas_call(
        coupling_kernel,
        out_shape=jax.ShapeDtypeStruct((3, 2, 6, width, width), jnp.bfloat16),
        in_specs=[vmem] * 6,
        out_specs=vmem,
        scratch_shapes=[pltpu.VMEM((2, width, width), jnp.float32)] * 2,
        compiler_params=pltpu.CompilerParams(vmem_limit_bytes=VMEM_BYTES),
    )(c_part, c_rest, c_x, c_y, far_mine, far_theirs)
    shape = (4, width, width)
    keep, give = call(chain_kernel, (b_own, b_x, b_y, b_far, c_forms), shape, 2, 26)
    anywhere = pl.BlockSpec(memory_space=pl.ANY)
    half = pl.pallas_call(
        pick_kernel,
        out_shape=jax.ShapeDtypeStruct(shape, jnp.float32),
        in_specs=[anywhere] * 2,
        out_specs=anywhere,
        scratch_shapes=[pltpu.SemaphoreType.DMA],
        compiler_params=pltpu.CompilerParams(vmem_limit_bytes=VMEM_BYTES),
    )(keep, send(give, gift))

    rows = width // energy_count
    slots = 4 * energy_count
    parts = lax.all_to_all(
        half.reshape(slots, rows, width), ("slab", "energy"), 0, 0, tiled=True
    )
    phonon = phonon_matrix(shifts, mode_weight, total) / mom_count
    weight = jnp.broadcast_to(phonon[:, :, None, None], (total, total, 8, 128))
    mixed = pl.pallas_call(
        mix_kernel,
        out_shape=jax.ShapeDtypeStruct((total, rows, width), jnp.float32),
        in_specs=[vmem, vmem],
        out_specs=vmem,
        compiler_params=pltpu.CompilerParams(vmem_limit_bytes=VMEM_BYTES),
    )(weight, parts)
    other = send(mixed, siblings)
    mine = jnp.arange(2)[:, None, None] == k
    result = jnp.where(mine, mixed[:, None], other[:, None])
    return result[:, None]


def solution(mesh):
    in_specs = (
        P("mom", "slab", None),
        P("mom", "slab", None, None, None),
        P("mom", "slab", None, None, None),
        P("energy", "slab", None, None, None),
        P(),
        P(),
    )
    out_specs = P(None, "slab", None, "energy", None)
    count = mesh.shape["energy"]

    def run(onsite, hop, couple, sigma_in, shifts, mode_weight):
        owned = (
            mesh.shape["slab"] == 4
            and mesh.shape["mom"] == 2
            and couple.shape[:2] == (2, 4)
            and sigma_in.shape[0] == 2 * count
            and count & (count - 1) == 0
        )
        inner = owner_body if owned else chain_body
        sharded = jax.shard_map(
            inner, mesh=mesh, in_specs=in_specs, out_specs=out_specs, check_vma=False
        )
        return sharded(onsite, hop, couple, sigma_in, shifts, mode_weight)

    return run
```

```python
import functools

import jax
import jax.numpy as jnp
from jax import lax
from jax.experimental import pallas as pl
from jax.experimental.pallas import tpu as pltpu
from jax.sharding import PartitionSpec as P

ETA = 0.5
HIGH = lax.Precision.HIGHEST


def shifted(shard, axis, by):
    length = lax.axis_size(axis)
    pairs = [(i, i + by) for i in range(length) if 0 <= i + by < length]
    return lax.ppermute(shard, axis, pairs)


def complex_mul(form, left, right):

    def product(first, second):
        return jnp.einsum(form, first, second, precision=HIGH)

    return (
        product(left[0], right[0]) - product(left[1], right[1]),
        product(left[0], right[1]) + product(left[1], right[0]),
    )


def newton_inverse(mat_real, mat_imag, form, identity):
    diag_real = jnp.diagonal(mat_real, axis1=-2, axis2=-1)
    diag_imag = jnp.diagonal(mat_imag, axis1=-2, axis2=-1)
    denom = diag_real * diag_real + diag_imag * diag_imag
    x_real = diag_real / denom
    x_imag = -diag_imag / denom
    rows_real = x_real[..., :, None] * mat_real - x_imag[..., :, None] * mat_imag
    rows_imag = x_real[..., :, None] * mat_imag + x_imag[..., :, None] * mat_real
    both_real = rows_real * x_real[..., None, :] - rows_imag * x_imag[..., None, :]
    both_imag = rows_real * x_imag[..., None, :] + rows_imag * x_real[..., None, :]
    first = (
        2.0 * identity * x_real[..., None, :] - both_real,
        2.0 * identity * x_imag[..., None, :] - both_imag,
    )
    resid = complex_mul(form, (mat_real, mat_imag), first)
    second = complex_mul(form, first, resid)
    return (2.0 * first[0] - second[0], 2.0 * first[1] - second[1])


def phonon_matrix(shifts, mode_weight, count):
    rows = jnp.arange(count)[:, None, None]
    cols = jnp.arange(count)[None, :, None]
    offset = shifts[None, None, :]
    upper = (cols == rows + offset).astype(jnp.float32)
    lower = (cols == rows - offset).astype(jnp.float32)
    return jnp.sum(upper * mode_weight[0] + lower * mode_weight[1], axis=2)


def chain_body(onsite, hop, couple, sigma_in, shifts, mode_weight):
    e_local = sigma_in.shape[0]
    width = onsite.shape[-1]
    slab_count = lax.axis_size("slab")
    slab_index = lax.axis_index("slab")
    energy_count = lax.axis_size("energy")
    mom_count = lax.axis_size("mom")
    total = e_local * energy_count
    identity = jnp.eye(width, dtype=jnp.float32)
    global_index = lax.axis_index("energy") * e_local + jnp.arange(e_local)
    energy = -0.5 + (global_index.astype(jnp.float32) + 0.5) / total
    coupling = (couple[0, 0, 0], couple[0, 0, 1])
    adjoint = (coupling[0].T, -coupling[1].T)
    hopping = (hop[0, 0, 0], hop[0, 0, 1])
    level = onsite[0, 0]
    sigma = sigma_in[:, 0]

    def forward(received, energies, sig):
        temp = complex_mul("ij,ejl->eil", coupling, (received[:, 0], received[:, 1]))
        left = complex_mul("eij,jl->eil", temp, adjoint)
        z_real = energies[:, None] - level[None, :]
        mat_real = identity * z_real[:, None, :] - hopping[0] - sig[:, 0] - left[0]
        mat_imag = identity * ETA - hopping[1] - sig[:, 1] - left[1]
        green = newton_inverse(mat_real, mat_imag, "eij,ejl->eil", identity)
        return jnp.stack(green, axis=1)

    def backward(green, received):
        pair = (green[:, 0], green[:, 1])
        temp = complex_mul("eij,ejl->eil", pair, (received[:, 0], received[:, 1]))
        extra = complex_mul("eij,ejl->eil", temp, pair)
        full = (pair[0] + extra[0], pair[1] + extra[1])
        temp = complex_mul("ij,ejl->eil", adjoint, full)
        coupled = complex_mul("eij,jl->eil", temp, coupling)
        return (jnp.stack(full, axis=1), jnp.stack(coupled, axis=1))

    empty = jnp.zeros((e_local, 2, width, width), jnp.float32)

    def forward_step(step, green_all):
        received = shifted(green_all, "slab", 1)
        return lax.cond(
            slab_index == step, lambda: forward(received, energy, sigma), lambda: green_all
        )

    green_all = lax.fori_loop(0, slab_count, forward_step, empty)

    def backward_step(step, carry):
        received = shifted(carry[1], "slab", -1)
        return lax.cond(
            slab_index == slab_count - 1 - step,
            lambda: backward(green_all, received),
            lambda: carry,
        )

    full_all, coupled_all = lax.fori_loop(0, slab_count, backward_step, (empty, empty))
    phonon = phonon_matrix(shifts, mode_weight, total)
    blocks = full_all[:, None]
    mixed = jnp.einsum(
        "ef,fsrjl->esrjl",
        phonon,
        lax.all_to_all(blocks, "energy", split_axis=3, concat_axis=0, tiled=True),
        precision=HIGH,
    )
    result = lax.psum(mixed, "mom") / mom_count
    return result


VMEM_BYTES = 24 * 1024 * 1024


BLOCKS = 2


def halves(value):
    high = value.astype(jnp.bfloat16)
    low = (value - high.astype(jnp.float32)).astype(jnp.bfloat16)
    return high, low


def form(pair):
    return halves(pair[0]), halves(pair[1]), halves(pair[0] + pair[1])


def real_dot(left, right):
    rows = left[0].shape[0]
    both = jnp.concatenate([left[0], left[1]], axis=0)
    main = jnp.dot(both, right[0], preferred_element_type=jnp.float32)
    rest = jnp.dot(left[0], right[1], preferred_element_type=jnp.float32)
    return main[:rows] + main[rows:] + rest


def mul(left, right):
    first = real_dot(left[0], right[0])
    second = real_dot(left[1], right[1])
    third = real_dot(left[2], right[2])
    return first - second, third - first - second


def mul_twice(blocks, right, last):
    inner = [mul(block, right) for block in blocks]
    return [mul(form(block), last) for block in inner]


def split_rows(pair):
    size = pair[0].shape[0] // BLOCKS
    return [tuple(part[b * size : (b + 1) * size] for part in pair) for b in range(BLOCKS)]


def join_rows(blocks):
    return tuple(jnp.concatenate([block[i] for block in blocks], axis=0) for i in range(2))


def form_rows(forms):
    return tuple(
        tuple(jnp.concatenate([f[plane][term] for f in forms], axis=0) for term in range(2))
        for plane in range(3)
    )


def read(ref):
    return ref[0], ref[1]


def write(ref, blocks):
    size = blocks[0][0].shape[0]
    for b, block in enumerate(blocks):
        ref[0, b * size : (b + 1) * size] = block[0]
        ref[1, b * size : (b + 1) * size] = block[1]


def choose(cond, left, right):
    return jnp.where(cond, left[0], right[0]), jnp.where(cond, left[1], right[1])


def times(left, right):
    return left[0] * right[0] - left[1] * right[1], left[0] * right[1] + left[1] * right[0]


def inverse(mats):
    size, width = mats[0][0].shape

    def invert(real, imag):
        denom = real * real + imag * imag
        return real / denom, -imag / denom

    eyes, scaled = [], []
    across = (0.0, 0.0)
    for b, mat in enumerate(mats):
        eye = lax.broadcasted_iota(jnp.int32, (size, width), 0) + b * size == (
            lax.broadcasted_iota(jnp.int32, (size, width), 1)
        )
        on = [jnp.where(eye, part, 0.0) for part in mat]
        off = [jnp.where(eye, 0.0, part) for part in mat]
        across = tuple(
            total + jnp.sum(part, axis=0, keepdims=True) for total, part in zip(across, on)
        )
        down = invert(*(jnp.sum(part, axis=1, keepdims=True) for part in on))
        eyes.append(eye)
        scaled.append(times(down, off))
    forms = [form(block) for block in scaled]
    right = form_rows(forms)
    squares = [mul(block, right) for block in forms]
    cubes = [mul(form(block), right) for block in squares]
    factor = invert(*across)
    out = []
    for eye, one, two, three in zip(eyes, scaled, squares, cubes):
        real = jnp.where(eye, 1.0, 0.0) - one[0] + two[0] - three[0]
        out.append(times((real, two[1] - one[1] - three[1]), factor))
    return out


def pick_block(y, x, slab, own, x_side, y_side, far):
    same_y = y == slab // 2
    same_x = x == slab % 2
    near = choose(same_x, read(own), read(x_side))
    away = choose(same_x, read(y_side), read(far))
    return choose(same_y, near, away)


def stored_form(ref, slab, side):
    at = (slab - 1, side)
    return tuple(tuple(ref[(*at, 2 * plane + term)] for term in range(2)) for plane in range(3))


def stored_rows(ref, slab, side):
    size = ref.shape[-2] // BLOCKS
    at = (slab - 1, side)
    return [
        tuple(
            tuple(ref[(*at, 2 * plane + term, slice(b * size, (b + 1) * size))] for term in range(2))
            for plane in range(3)
        )
        for b in range(BLOCKS)
    ]


def place_of():
    slab = lax.axis_index("slab")
    return slab // 2, slab % 2


def coupling_kernel(c_part, c_rest, c_x, c_y, far_mine, far_theirs, out_ref, c_own, c_far):
    y, x = place_of()
    first, rows = lax.axis_index("energy") % 2 == 0, far_mine.shape[1]
    for ref, here, beside in ((c_own, c_part, c_rest), (c_far, far_mine, far_theirs)):
        for part in range(2):
            mine, theirs = here[part], beside[part]
            ref[part, :rows] = jnp.where(first, mine, theirs)
            ref[part, rows:] = jnp.where(first, theirs, mine)
    for slab in (1, 2, 3):
        real, imag = pick_block(y, x, slab, c_own, c_x, c_y, c_far)
        for side, pair in enumerate(((real, imag), (real.T, -imag.T))):
            for plane, terms in enumerate(form(pair)):
                for term in range(2):
                    out_ref[slab - 1, side, 2 * plane + term] = terms[term]


def chain_kernel(b_own, b_x, b_y, b_far, c_forms, keep_ref, give_ref):
    y, x = place_of()
    greens, forms = [], []
    for slab in range(4):
        mats = split_rows(pick_block(y, x, slab, b_own, b_x, b_y, b_far))
        if slab:
            terms = mul_twice(
                stored_rows(c_forms, slab, 0), form_rows(forms[-1]), stored_form(c_forms, slab, 1)
            )
            mats = [(m[0] - t[0], m[1] - t[1]) for m, t in zip(mats, terms)]
        greens.append(inverse(mats))
        forms.append([form(block) for block in greens[-1]])

    def finish(slab, blocks):
        full = join_rows(blocks)
        keep_ref[slab] = jnp.where(x == 0, full[0], full[1])
        give_ref[slab] = jnp.where(x == 0, full[1], full[0])

    finish(3, greens[3])
    full_form = form_rows(forms[3])
    for slab in (2, 1, 0):
        coupled = mul_twice(
            stored_rows(c_forms, slab + 1, 1), full_form, stored_form(c_forms, slab + 1, 0)
        )
        coupled_form = form_rows([form(block) for block in coupled])
        extra = mul_twice(forms[slab], coupled_form, form_rows(forms[slab]))
        fulls = [(g[0] + e[0], g[1] + e[1]) for g, e in zip(greens[slab], extra)]
        finish(slab, fulls)
        if slab:
            full_form = form_rows([form(block) for block in fulls])


def mix_kernel(weight, parts_ref, out_ref):
    slots, rows, width = parts_ref.shape
    energies = out_ref.shape[0]
    planes = slots // 4
    high, wide = weight.shape[2:]

    def source(slot):
        return 2 * (slot % planes) + slot // planes // 2

    for row in range(0, rows, high):
        for column in range(0, width, wide):
            here = (slice(row, row + high), slice(column, column + wide))
            values = [None] * energies
            for slot in range(slots):
                value = parts_ref[(slot, *here)]
                held = values[source(slot)]
                values[source(slot)] = value if held is None else held + value
            for energy in range(energies):
                total = weight[energy, 0] * values[0]
                for other in range(1, energies):
                    total = total + weight[energy, other] * values[other]
                out_ref[(energy, *here)] = total


def pick_kernel(keep_ref, got_ref, out_ref, sem):
    owner = lax.axis_index("mom") == place_of()[1]

    @pl.when(owner)
    def _():
        copy = pltpu.make_async_copy(keep_ref, out_ref, sem)
        copy.start()
        copy.wait()

    @pl.when(jnp.logical_not(owner))
    def _():
        copy = pltpu.make_async_copy(got_ref, out_ref, sem)
        copy.start()
        copy.wait()


def join_kernel(mine_ref, other_ref, out_ref, sems):
    core = lax.axis_index("mom")
    mine = pltpu.make_async_copy(mine_ref, out_ref.at[:, core], sems.at[0])
    other = pltpu.make_async_copy(other_ref, out_ref.at[:, 1 - core], sems.at[1])
    mine.start()
    other.start()
    mine.wait()
    other.wait()


def prepare_kernel(planes, onsite_ref, hop_ref, sigma_ref, own_ref, other_ref):
    width = hop_ref.shape[-1]
    y, _ = place_of()
    eye = lax.broadcasted_iota(jnp.int32, (width, width), 0) == lax.broadcasted_iota(
        jnp.int32, (width, width), 1
    )
    count = sigma_ref.shape[0]
    for ref, local in ((other_ref, 1 - y), (own_ref, y)):
        index = (lax.axis_index("energy") * count + local).astype(jnp.float32)
        level = (-0.5 + (index + 0.5) / (count * planes)) - onsite_ref[...]
        ref[0] = jnp.where(eye, level, 0.0) - hop_ref[0] - sigma_ref[local, 0]
        ref[1] = jnp.where(eye, ETA, 0.0) - hop_ref[1] - sigma_ref[local, 1]


def call(kernel, arrays, shape, count, products):
    width = arrays[0].shape[-1]
    vmem = pl.BlockSpec(memory_space=pltpu.VMEM)
    return pl.pallas_call(
        kernel,
        out_shape=[jax.ShapeDtypeStruct(shape, jnp.float32)] * count,
        in_specs=[vmem] * len(arrays),
        out_specs=[vmem] * count,
        compiler_params=pltpu.CompilerParams(vmem_limit_bytes=VMEM_BYTES),
        cost_estimate=pl.CostEstimate(
            flops=products * 9 * 2 * width**3,
            bytes_accessed=(len(arrays) + count) * 2 * width * width * 4,
            transcendentals=0,
        ),
    )(*arrays)


def owner_body(onsite, hop, couple, sigma_in, shifts, mode_weight):
    e_local = sigma_in.shape[0]
    width = onsite.shape[-1]
    energy_count = lax.axis_size("energy")
    mom_count = lax.axis_size("mom")
    total = e_local * energy_count
    axes = ("slab", "energy", "mom")
    slab = lax.axis_index("slab")
    z = lax.axis_index("energy")
    y, x = slab // 2, slab % 2

    def device(yy, xx, zz, kk):
        return ((2 * yy + xx) * energy_count + zz) * mom_count + kk

    chips = [(yy, xx, zz) for yy in range(2) for xx in range(2) for zz in range(energy_count)]
    to_x = [(device(a, b, c, 1 - b), device(a, 1 - b, c, 1 - b)) for a, b, c in chips]
    to_y = [(device(a, b, c, b), device(1 - a, b, c, b)) for a, b, c in chips]
    to_far = [(device(a, b, c, 1 - b), device(1 - a, 1 - b, c, 1 - b)) for a, b, c in chips]

    def routes(*pairs):
        return [
            (device(*divmod(s, 2), zz, t % 2), device(*divmod(t, 2), zz, t % 2))
            for s, t in pairs
            for zz in range(energy_count)
        ]

    beside = [(device(a, b, c, b), device(a, b, c ^ 1, b)) for a, b, c in chips]
    siblings = [(device(a, b, c, d), device(a, b, c, 1 - d)) for a, b, c in chips for d in range(2)]
    gift = [(device(a, b, c, b), device(a, b, c, 1 - b)) for a, b, c in chips]

    def send(value, pairs):
        return lax.ppermute(value, axes, pairs)

    vmem = pl.BlockSpec(memory_space=pltpu.VMEM)
    block_shape = jax.ShapeDtypeStruct((2, width, width), jnp.float32)
    b_own, b_other = pl.pallas_call(
        functools.partial(prepare_kernel, energy_count),
        out_shape=[block_shape] * 2,
        in_specs=[vmem] * 3,
        out_specs=[vmem] * 2,
        compiler_params=pltpu.CompilerParams(vmem_limit_bytes=VMEM_BYTES),
    )(onsite[0], hop[0, 0], sigma_in[:, 0])

    coupling = couple[0, 0]
    size = width // 2
    c_part = lax.dynamic_slice_in_dim(coupling, (z % 2) * size, size, axis=1)
    c_rest = lax.dynamic_slice_in_dim(coupling, (1 - z % 2) * size, size, axis=1)
    far_mine = send(c_part, routes((1, 2), (2, 1), (3, 0)))
    c_x = send(coupling, routes((1, 0), (2, 3), (3, 2)))
    c_y = send(coupling, routes((1, 3), (2, 0), (3, 1)))
    far_mine, c_x, c_y = lax.optimization_barrier((far_mine, c_x, c_y))
    far_theirs = send(far_mine, beside)
    b_far = send(b_other, to_far)
    b_x = send(b_own, to_x)
    b_y = send(b_other, to_y)

    c_forms = pl.pallas_call(
        coupling_kernel,
        out_shape=jax.ShapeDtypeStruct((3, 2, 6, width, width), jnp.bfloat16),
        in_specs=[vmem] * 6,
        out_specs=vmem,
        scratch_shapes=[pltpu.VMEM((2, width, width), jnp.float32)] * 2,
        compiler_params=pltpu.CompilerParams(vmem_limit_bytes=VMEM_BYTES),
    )(c_part, c_rest, c_x, c_y, far_mine, far_theirs)
    shape = (4, width, width)
    keep, give = call(chain_kernel, (b_own, b_x, b_y, b_far, c_forms), shape, 2, 26)
    anywhere = pl.BlockSpec(memory_space=pl.ANY)
    half = pl.pallas_call(
        pick_kernel,
        out_shape=jax.ShapeDtypeStruct(shape, jnp.float32),
        in_specs=[anywhere] * 2,
        out_specs=anywhere,
        scratch_shapes=[pltpu.SemaphoreType.DMA],
        compiler_params=pltpu.CompilerParams(vmem_limit_bytes=VMEM_BYTES),
    )(keep, send(give, gift))

    rows = width // energy_count
    slots = 4 * energy_count
    parts = lax.all_to_all(
        half.reshape(slots, rows, width), ("slab", "energy"), 0, 0, tiled=True
    )
    phonon = phonon_matrix(shifts, mode_weight, total) / mom_count
    weight = jnp.broadcast_to(phonon[:, :, None, None], (total, total, 8, 128))
    mixed = pl.pallas_call(
        mix_kernel,
        out_shape=jax.ShapeDtypeStruct((total, rows, width), jnp.float32),
        in_specs=[vmem, vmem],
        out_specs=vmem,
        compiler_params=pltpu.CompilerParams(vmem_limit_bytes=VMEM_BYTES),
    )(weight, parts)
    other = send(mixed, siblings)
    result = pl.pallas_call(
        join_kernel,
        out_shape=jax.ShapeDtypeStruct((total, 2, rows, width), jnp.float32),
        in_specs=[anywhere] * 2,
        out_specs=anywhere,
        scratch_shapes=[pltpu.SemaphoreType.DMA((2,))],
        compiler_params=pltpu.CompilerParams(vmem_limit_bytes=VMEM_BYTES),
    )(mixed, other)
    return result[:, None]


def solution(mesh):
    in_specs = (
        P("mom", "slab", None),
        P("mom", "slab", None, None, None),
        P("mom", "slab", None, None, None),
        P("energy", "slab", None, None, None),
        P(),
        P(),
    )
    out_specs = P(None, "slab", None, "energy", None)
    count = mesh.shape["energy"]

    def run(onsite, hop, couple, sigma_in, shifts, mode_weight):
        owned = (
            mesh.shape["slab"] == 4
            and mesh.shape["mom"] == 2
            and couple.shape[:2] == (2, 4)
            and sigma_in.shape[0] == 2 * count
            and count & (count - 1) == 0
        )
        inner = owner_body if owned else chain_body
        sharded = jax.shard_map(
            inner, mesh=mesh, in_specs=in_specs, out_specs=out_specs, check_vma=False
        )
        return sharded(onsite, hop, couple, sigma_in, shifts, mode_weight)

    return run
```

```python
import functools

import jax
import jax.numpy as jnp
from jax import lax
from jax.experimental import pallas as pl
from jax.experimental.pallas import tpu as pltpu
from jax.sharding import PartitionSpec as P

ETA = 0.5
HIGH = lax.Precision.HIGHEST


def shifted(shard, axis, by):
    length = lax.axis_size(axis)
    pairs = [(i, i + by) for i in range(length) if 0 <= i + by < length]
    return lax.ppermute(shard, axis, pairs)


def complex_mul(form, left, right):

    def product(first, second):
        return jnp.einsum(form, first, second, precision=HIGH)

    return (
        product(left[0], right[0]) - product(left[1], right[1]),
        product(left[0], right[1]) + product(left[1], right[0]),
    )


def newton_inverse(mat_real, mat_imag, form, identity):
    diag_real = jnp.diagonal(mat_real, axis1=-2, axis2=-1)
    diag_imag = jnp.diagonal(mat_imag, axis1=-2, axis2=-1)
    denom = diag_real * diag_real + diag_imag * diag_imag
    x_real = diag_real / denom
    x_imag = -diag_imag / denom
    rows_real = x_real[..., :, None] * mat_real - x_imag[..., :, None] * mat_imag
    rows_imag = x_real[..., :, None] * mat_imag + x_imag[..., :, None] * mat_real
    both_real = rows_real * x_real[..., None, :] - rows_imag * x_imag[..., None, :]
    both_imag = rows_real * x_imag[..., None, :] + rows_imag * x_real[..., None, :]
    first = (
        2.0 * identity * x_real[..., None, :] - both_real,
        2.0 * identity * x_imag[..., None, :] - both_imag,
    )
    resid = complex_mul(form, (mat_real, mat_imag), first)
    second = complex_mul(form, first, resid)
    return (2.0 * first[0] - second[0], 2.0 * first[1] - second[1])


def phonon_matrix(shifts, mode_weight, count):
    rows = jnp.arange(count)[:, None, None]
    cols = jnp.arange(count)[None, :, None]
    offset = shifts[None, None, :]
    upper = (cols == rows + offset).astype(jnp.float32)
    lower = (cols == rows - offset).astype(jnp.float32)
    return jnp.sum(upper * mode_weight[0] + lower * mode_weight[1], axis=2)


def chain_body(onsite, hop, couple, sigma_in, shifts, mode_weight):
    e_local = sigma_in.shape[0]
    width = onsite.shape[-1]
    slab_count = lax.axis_size("slab")
    slab_index = lax.axis_index("slab")
    energy_count = lax.axis_size("energy")
    mom_count = lax.axis_size("mom")
    total = e_local * energy_count
    identity = jnp.eye(width, dtype=jnp.float32)
    global_index = lax.axis_index("energy") * e_local + jnp.arange(e_local)
    energy = -0.5 + (global_index.astype(jnp.float32) + 0.5) / total
    coupling = (couple[0, 0, 0], couple[0, 0, 1])
    adjoint = (coupling[0].T, -coupling[1].T)
    hopping = (hop[0, 0, 0], hop[0, 0, 1])
    level = onsite[0, 0]
    sigma = sigma_in[:, 0]

    def forward(received, energies, sig):
        temp = complex_mul("ij,ejl->eil", coupling, (received[:, 0], received[:, 1]))
        left = complex_mul("eij,jl->eil", temp, adjoint)
        z_real = energies[:, None] - level[None, :]
        mat_real = identity * z_real[:, None, :] - hopping[0] - sig[:, 0] - left[0]
        mat_imag = identity * ETA - hopping[1] - sig[:, 1] - left[1]
        green = newton_inverse(mat_real, mat_imag, "eij,ejl->eil", identity)
        return jnp.stack(green, axis=1)

    def backward(green, received):
        pair = (green[:, 0], green[:, 1])
        temp = complex_mul("eij,ejl->eil", pair, (received[:, 0], received[:, 1]))
        extra = complex_mul("eij,ejl->eil", temp, pair)
        full = (pair[0] + extra[0], pair[1] + extra[1])
        temp = complex_mul("ij,ejl->eil", adjoint, full)
        coupled = complex_mul("eij,jl->eil", temp, coupling)
        return (jnp.stack(full, axis=1), jnp.stack(coupled, axis=1))

    empty = jnp.zeros((e_local, 2, width, width), jnp.float32)

    def forward_step(step, green_all):
        received = shifted(green_all, "slab", 1)
        return lax.cond(
            slab_index == step, lambda: forward(received, energy, sigma), lambda: green_all
        )

    green_all = lax.fori_loop(0, slab_count, forward_step, empty)

    def backward_step(step, carry):
        received = shifted(carry[1], "slab", -1)
        return lax.cond(
            slab_index == slab_count - 1 - step,
            lambda: backward(green_all, received),
            lambda: carry,
        )

    full_all, coupled_all = lax.fori_loop(0, slab_count, backward_step, (empty, empty))
    phonon = phonon_matrix(shifts, mode_weight, total)
    blocks = full_all[:, None]
    mixed = jnp.einsum(
        "ef,fsrjl->esrjl",
        phonon,
        lax.all_to_all(blocks, "energy", split_axis=3, concat_axis=0, tiled=True),
        precision=HIGH,
    )
    result = lax.psum(mixed, "mom") / mom_count
    return result


VMEM_BYTES = 24 * 1024 * 1024


BLOCKS = 2


def halves(value):
    high = value.astype(jnp.bfloat16)
    low = (value - high.astype(jnp.float32)).astype(jnp.bfloat16)
    return high, low


def form(pair):
    return halves(pair[0]), halves(pair[1]), halves(pair[0] + pair[1])


def real_dot(left, right):
    rows = left[0].shape[0]
    both = jnp.concatenate([left[0], left[1]], axis=0)
    main = jnp.dot(both, right[0], preferred_element_type=jnp.float32)
    rest = jnp.dot(left[0], right[1], preferred_element_type=jnp.float32)
    return main[:rows] + main[rows:] + rest


def mul(left, right):
    first = real_dot(left[0], right[0])
    second = real_dot(left[1], right[1])
    third = real_dot(left[2], right[2])
    return first - second, third - first - second


def mul_twice(blocks, right, last):
    inner = [mul(block, right) for block in blocks]
    return [mul(form(block), last) for block in inner]


def split_rows(pair):
    size = pair[0].shape[0] // BLOCKS
    return [tuple(part[b * size : (b + 1) * size] for part in pair) for b in range(BLOCKS)]


def join_rows(blocks):
    return tuple(jnp.concatenate([block[i] for block in blocks], axis=0) for i in range(2))


def form_rows(forms):
    return tuple(
        tuple(jnp.concatenate([f[plane][term] for f in forms], axis=0) for term in range(2))
        for plane in range(3)
    )


def read(ref):
    return ref[0], ref[1]


def write(ref, blocks):
    size = blocks[0][0].shape[0]
    for b, block in enumerate(blocks):
        ref[0, b * size : (b + 1) * size] = block[0]
        ref[1, b * size : (b + 1) * size] = block[1]


def choose(cond, left, right):
    return jnp.where(cond, left[0], right[0]), jnp.where(cond, left[1], right[1])


def times(left, right):
    return left[0] * right[0] - left[1] * right[1], left[0] * right[1] + left[1] * right[0]


def inverse(mats):
    size, width = mats[0][0].shape

    def invert(real, imag):
        denom = real * real + imag * imag
        return real / denom, -imag / denom

    eyes, scaled = [], []
    across = (0.0, 0.0)
    for b, mat in enumerate(mats):
        eye = lax.broadcasted_iota(jnp.int32, (size, width), 0) + b * size == (
            lax.broadcasted_iota(jnp.int32, (size, width), 1)
        )
        on = [jnp.where(eye, part, 0.0) for part in mat]
        off = [jnp.where(eye, 0.0, part) for part in mat]
        across = tuple(
            total + jnp.sum(part, axis=0, keepdims=True) for total, part in zip(across, on)
        )
        down = invert(*(jnp.sum(part, axis=1, keepdims=True) for part in on))
        eyes.append(eye)
        scaled.append(times(down, off))
    forms = [form(block) for block in scaled]
    right = form_rows(forms)
    squares = [mul(block, right) for block in forms]
    cubes = [mul(form(block), right) for block in squares]
    factor = invert(*across)
    out = []
    for eye, one, two, three in zip(eyes, scaled, squares, cubes):
        real = jnp.where(eye, 1.0, 0.0) - one[0] + two[0] - three[0]
        out.append(times((real, two[1] - one[1] - three[1]), factor))
    return out


def pick_block(y, x, slab, own, x_side, y_side, far):
    same_y = y == slab // 2
    same_x = x == slab % 2
    near = choose(same_x, read(own), read(x_side))
    away = choose(same_x, read(y_side), read(far))
    return choose(same_y, near, away)


def stored_form(ref, slab, side):
    at = (slab - 1, side)
    return tuple(tuple(ref[(*at, 2 * plane + term)] for term in range(2)) for plane in range(3))


def stored_rows(ref, slab, side):
    size = ref.shape[-2] // BLOCKS
    at = (slab - 1, side)
    return [
        tuple(
            tuple(ref[(*at, 2 * plane + term, slice(b * size, (b + 1) * size))] for term in range(2))
            for plane in range(3)
        )
        for b in range(BLOCKS)
    ]


def place_of():
    slab = lax.axis_index("slab")
    return slab // 2, slab % 2


def coupling_kernel(c_part, c_rest, c_x, c_y, far_mine, far_theirs, out_ref, c_own, c_far):
    y, x = place_of()
    first, rows = lax.axis_index("energy") % 2 == 0, far_mine.shape[1]
    for ref, here, beside in ((c_own, c_part, c_rest), (c_far, far_mine, far_theirs)):
        for part in range(2):
            mine, theirs = here[part], beside[part]
            ref[part, :rows] = jnp.where(first, mine, theirs)
            ref[part, rows:] = jnp.where(first, theirs, mine)
    for slab in (1, 2, 3):
        real, imag = pick_block(y, x, slab, c_own, c_x, c_y, c_far)
        for side, pair in enumerate(((real, imag), (real.T, -imag.T))):
            for plane, terms in enumerate(form(pair)):
                for term in range(2):
                    out_ref[slab - 1, side, 2 * plane + term] = terms[term]


def chain_kernel(b_own, b_y, b_x, b_far, c_forms, keep_ref, give_ref):
    y, x = place_of()
    greens, forms = [], []
    for slab in range(4):
        mats = split_rows(pick_block(y, x, slab, b_own, b_x, b_y, b_far))
        if slab:
            terms = mul_twice(
                stored_rows(c_forms, slab, 0), form_rows(forms[-1]), stored_form(c_forms, slab, 1)
            )
            mats = [(m[0] - t[0], m[1] - t[1]) for m, t in zip(mats, terms)]
        greens.append(inverse(mats))
        forms.append([form(block) for block in greens[-1]])

    def finish(slab, blocks):
        full = join_rows(blocks)
        keep_ref[slab] = jnp.where(x == 0, full[0], full[1])
        give_ref[slab] = jnp.where(x == 0, full[1], full[0])

    finish(3, greens[3])
    full_form = form_rows(forms[3])
    for slab in (2, 1, 0):
        coupled = mul_twice(
            stored_rows(c_forms, slab + 1, 1), full_form, stored_form(c_forms, slab + 1, 0)
        )
        coupled_form = form_rows([form(block) for block in coupled])
        extra = mul_twice(forms[slab], coupled_form, form_rows(forms[slab]))
        fulls = [(g[0] + e[0], g[1] + e[1]) for g, e in zip(greens[slab], extra)]
        finish(slab, fulls)
        if slab:
            full_form = form_rows([form(block) for block in fulls])


def mix_kernel(weight, parts_ref, out_ref):
    slots, rows, width = parts_ref.shape
    energies = out_ref.shape[0]
    planes = slots // 4
    high, wide = weight.shape[2:]

    def source(slot):
        return 2 * (slot % planes) + slot // planes // 2

    for row in range(0, rows, high):
        for column in range(0, width, wide):
            here = (slice(row, row + high), slice(column, column + wide))
            values = [None] * energies
            for slot in range(slots):
                value = parts_ref[(slot, *here)]
                held = values[source(slot)]
                values[source(slot)] = value if held is None else held + value
            for energy in range(energies):
                total = weight[energy, 0] * values[0]
                for other in range(1, energies):
                    total = total + weight[energy, other] * values[other]
                out_ref[(energy, *here)] = total


def pick_kernel(keep_ref, got_ref, out_ref, sem):
    owner = lax.axis_index("mom") == place_of()[1]

    @pl.when(owner)
    def _():
        copy = pltpu.make_async_copy(keep_ref, out_ref, sem)
        copy.start()
        copy.wait()

    @pl.when(jnp.logical_not(owner))
    def _():
        copy = pltpu.make_async_copy(got_ref, out_ref, sem)
        copy.start()
        copy.wait()


def join_kernel(mine_ref, other_ref, out_ref, sems):
    core = lax.axis_index("mom")
    mine = pltpu.make_async_copy(mine_ref, out_ref.at[:, core], sems.at[0])
    other = pltpu.make_async_copy(other_ref, out_ref.at[:, 1 - core], sems.at[1])
    mine.start()
    other.start()
    mine.wait()
    other.wait()


def prepare_kernel(planes, onsite_ref, hop_ref, sigma_ref, own_ref, other_ref):
    width = hop_ref.shape[-1]
    y, _ = place_of()
    eye = lax.broadcasted_iota(jnp.int32, (width, width), 0) == lax.broadcasted_iota(
        jnp.int32, (width, width), 1
    )
    count = sigma_ref.shape[0]
    for ref, local in ((other_ref, 1 - y), (own_ref, y)):
        index = (lax.axis_index("energy") * count + local).astype(jnp.float32)
        level = (-0.5 + (index + 0.5) / (count * planes)) - onsite_ref[...]
        ref[0] = jnp.where(eye, level, 0.0) - hop_ref[0] - sigma_ref[local, 0]
        ref[1] = jnp.where(eye, ETA, 0.0) - hop_ref[1] - sigma_ref[local, 1]


def call(kernel, arrays, shape, count, products):
    width = arrays[0].shape[-1]
    vmem = pl.BlockSpec(memory_space=pltpu.VMEM)
    return pl.pallas_call(
        kernel,
        out_shape=[jax.ShapeDtypeStruct(shape, jnp.float32)] * count,
        in_specs=[vmem] * len(arrays),
        out_specs=[vmem] * count,
        compiler_params=pltpu.CompilerParams(vmem_limit_bytes=VMEM_BYTES),
        cost_estimate=pl.CostEstimate(
            flops=products * 9 * 2 * width**3,
            bytes_accessed=(len(arrays) + count) * 2 * width * width * 4,
            transcendentals=0,
        ),
    )(*arrays)


def owner_body(onsite, hop, couple, sigma_in, shifts, mode_weight):
    e_local = sigma_in.shape[0]
    width = onsite.shape[-1]
    energy_count = lax.axis_size("energy")
    mom_count = lax.axis_size("mom")
    total = e_local * energy_count
    axes = ("slab", "energy", "mom")
    slab = lax.axis_index("slab")
    z = lax.axis_index("energy")
    y, x = slab // 2, slab % 2

    def device(yy, xx, zz, kk):
        return ((2 * yy + xx) * energy_count + zz) * mom_count + kk

    chips = [(yy, xx, zz) for yy in range(2) for xx in range(2) for zz in range(energy_count)]
    to_x = [(device(a, b, c, 1 - b), device(a, 1 - b, c, 1 - b)) for a, b, c in chips]
    to_y = [(device(a, b, c, b), device(1 - a, b, c, b)) for a, b, c in chips]
    to_far = [(device(a, b, c, 1 - b), device(1 - a, 1 - b, c, 1 - b)) for a, b, c in chips]

    def routes(*pairs):
        return [
            (device(*divmod(s, 2), zz, t % 2), device(*divmod(t, 2), zz, t % 2))
            for s, t in pairs
            for zz in range(energy_count)
        ]

    beside = [(device(a, b, c, b), device(a, b, c ^ 1, b)) for a, b, c in chips]
    siblings = [(device(a, b, c, d), device(a, b, c, 1 - d)) for a, b, c in chips for d in range(2)]
    gift = [(device(a, b, c, b), device(a, b, c, 1 - b)) for a, b, c in chips]

    def send(value, pairs):
        return lax.ppermute(value, axes, pairs)

    vmem = pl.BlockSpec(memory_space=pltpu.VMEM)
    block_shape = jax.ShapeDtypeStruct((2, width, width), jnp.float32)
    b_own, b_other = pl.pallas_call(
        functools.partial(prepare_kernel, energy_count),
        out_shape=[block_shape] * 2,
        in_specs=[vmem] * 3,
        out_specs=[vmem] * 2,
        compiler_params=pltpu.CompilerParams(vmem_limit_bytes=VMEM_BYTES),
    )(onsite[0], hop[0, 0], sigma_in[:, 0])

    coupling = couple[0, 0]
    size = width // 2
    c_part = lax.dynamic_slice_in_dim(coupling, (z % 2) * size, size, axis=1)
    c_rest = lax.dynamic_slice_in_dim(coupling, (1 - z % 2) * size, size, axis=1)
    far_mine = send(c_part, routes((1, 2), (2, 1), (3, 0)))
    c_x = send(coupling, routes((1, 0), (2, 3), (3, 2)))
    c_y = send(coupling, routes((1, 3), (2, 0), (3, 1)))
    far_mine, c_x, c_y = lax.optimization_barrier((far_mine, c_x, c_y))
    far_theirs = send(far_mine, beside)
    b_far = send(b_other, to_far)
    b_y = send(b_other, to_y)
    b_x = send(b_own, to_x)

    c_forms = pl.pallas_call(
        coupling_kernel,
        out_shape=jax.ShapeDtypeStruct((3, 2, 6, width, width), jnp.bfloat16),
        in_specs=[vmem] * 6,
        out_specs=vmem,
        scratch_shapes=[pltpu.VMEM((2, width, width), jnp.float32)] * 2,
        compiler_params=pltpu.CompilerParams(vmem_limit_bytes=VMEM_BYTES),
    )(c_part, c_rest, c_x, c_y, far_mine, far_theirs)
    shape = (4, width, width)
    keep, give = call(chain_kernel, (b_own, b_y, b_x, b_far, c_forms), shape, 2, 26)
    anywhere = pl.BlockSpec(memory_space=pl.ANY)
    half = pl.pallas_call(
        pick_kernel,
        out_shape=jax.ShapeDtypeStruct(shape, jnp.float32),
        in_specs=[anywhere] * 2,
        out_specs=anywhere,
        scratch_shapes=[pltpu.SemaphoreType.DMA],
        compiler_params=pltpu.CompilerParams(vmem_limit_bytes=VMEM_BYTES),
    )(keep, send(give, gift))

    rows = width // energy_count
    slots = 4 * energy_count
    parts = lax.all_to_all(
        half.reshape(slots, rows, width), ("slab", "energy"), 0, 0, tiled=True
    )
    phonon = phonon_matrix(shifts, mode_weight, total) / mom_count
    weight = jnp.broadcast_to(phonon[:, :, None, None], (total, total, 8, 128))
    mixed = pl.pallas_call(
        mix_kernel,
        out_shape=jax.ShapeDtypeStruct((total, rows, width), jnp.float32),
        in_specs=[vmem, vmem],
        out_specs=vmem,
        compiler_params=pltpu.CompilerParams(vmem_limit_bytes=VMEM_BYTES),
    )(weight, parts)
    other = send(mixed, siblings)
    result = pl.pallas_call(
        join_kernel,
        out_shape=jax.ShapeDtypeStruct((total, 2, rows, width), jnp.float32),
        in_specs=[anywhere] * 2,
        out_specs=anywhere,
        scratch_shapes=[pltpu.SemaphoreType.DMA((2,))],
        compiler_params=pltpu.CompilerParams(vmem_limit_bytes=VMEM_BYTES),
    )(mixed, other)
    return result[:, None]


def solution(mesh):
    in_specs = (
        P("mom", "slab", None),
        P("mom", "slab", None, None, None),
        P("mom", "slab", None, None, None),
        P("energy", "slab", None, None, None),
        P(),
        P(),
    )
    out_specs = P(None, "slab", None, "energy", None)
    count = mesh.shape["energy"]

    def run(onsite, hop, couple, sigma_in, shifts, mode_weight):
        owned = (
            mesh.shape["slab"] == 4
            and mesh.shape["mom"] == 2
            and couple.shape[:2] == (2, 4)
            and sigma_in.shape[0] == 2 * count
            and count & (count - 1) == 0
        )
        inner = owner_body if owned else chain_body
        sharded = jax.shard_map(
            inner, mesh=mesh, in_specs=in_specs, out_specs=out_specs, check_vma=False
        )
        return sharded(onsite, hop, couple, sigma_in, shifts, mode_weight)

    return run
```
